128 devices in a mesh: dp: 16 (over y, x), pipe: 2 (over z_lo), tensor: 4 (over z_hi, core).
Axes of the slice: x: 4, y: 4, z: 4 (z_hi: 2, z_lo: 2; z = z_hi * 2 + z_lo), core: 2. Of those that a mesh axis runs over, the one named last changes fastest.
Arguments:
- block_input: bfloat16 [4, 4608, 768], P(None, ('dp', 'tensor')), may hold values from -6 to 6
- out_cotangent: bfloat16 [4, 4608, 768], P(None, ('dp', 'tensor')), may hold values from -6 to 6
- drop_flags: int32 [4, 48], P(None, 'dp'), may hold values from 0 to 2
- key_valid: int32 [4, 48, 96], P(None, 'dp'), may hold values 0 or 1
- qkv_weight: bfloat16 [2, 768, 3, 768], P('pipe', None, None, 'tensor'), may hold values from -0.21875 to 0.21875
- out_weight: bfloat16 [2, 768, 768], P('pipe', 'tensor'), may hold values from -1.25 to 1.25
- up_weight: bfloat16 [2, 768, 3072], P('pipe', None, 'tensor'), may hold values from -0.21875 to 0.21875
- down_weight: bfloat16 [2, 3072, 768], P('pipe', 'tensor'), may hold values from -0.15625 to 0.15625
- hidden_bias: float32 [2, 3072], P('pipe', 'tensor'), may hold values from -3 to 3
- norm_gains: float32 [2, 2, 768], P('pipe'), may hold values from 0.5 to 1.5
- norm_shifts: float32 [2, 2, 768], P('pipe'), may hold values from -2 to 2
- out_biases: float32 [2, 2, 768], P('pipe'), may hold values from -2 to 2
Outputs:
- activations: bfloat16 [2, 4, 4608, 768], P('pipe', None, ('dp', 'tensor'))
- input_grads: bfloat16 [2, 4, 4608, 768], P('pipe', None, ('dp', 'tensor'))
- grad_qkv_weight: float32 [2, 768, 3, 768], P('pipe', 'dp', None, 'tensor')
- grad_out_weight: float32 [2, 768, 768], P('pipe', 'tensor', 'dp')
- grad_up_weight: float32 [2, 768, 3072], P('pipe', 'dp', 'tensor')
- grad_down_weight: float32 [2, 3072, 768], P('pipe', 'tensor', 'dp')
- grad_hidden_bias: float32 [2, 3072], P('pipe')
- grad_norm_gains: float32 [2, 2, 768], P('pipe')
- grad_norm_shifts: float32 [2, 2, 768], P('pipe')
- grad_out_biases: float32 [2, 2, 768], P('pipe')
The draws below stay inside these ranges and needn't reach their ends.
Inputs may be any that keep to these rules, and one draw needn't show every extreme that they name: `drop_flags`: flag 0 keeps both modalities of a page, 1 drops its visual blocks, 2 its text blocks.
All inputs are finite; a program needn't handle non-finite values. No bound on the sum of `key_valid` on one device may be relied on, other than what follows from the above.
Results may differ from the reference program's by a relative error of at most 0.025.
Values may be sent and summed in bfloat16 or wider, within the bound.
No kernel may reach another device: no remote copies, remote signals or barrier semaphores. Data moves between devices by JAX's collectives and lax.ppermute only.
A program may use at most 128 MiB of HBM per device.

```python
import jax
import jax.numpy as jnp
from jax import lax

D = 768
HEADS = 12
HEAD = 64
FF = 3072
BLOCKS = 96
TEXT = 72
MICRO = 4
PAGES_MB = 3
PAGES_ROW = 48
TOK_MB = 4608


def plant(values, key, least, top_value):
    index_at = [jax.random.randint(jax.random.fold_in(key, axis), (), 0, length) for axis, length in enumerate(values.shape)]
    longest = values.shape.index(max(values.shape))
    neighbour = index_at[:longest] + [(index_at[longest] + 1) % values.shape[longest]] + index_at[longest + 1:]
    return values.at[tuple(index_at)].set(least).at[tuple(neighbour)].set(top_value)


def levels(rng, extent, pieces, low, high):
    factor_of, own = 1.0, jax.random.fold_in(rng, 6)
    for position, blocks in pieces:
        steps = jnp.exp(jax.random.uniform(jax.random.fold_in(own, position), (blocks,), jnp.float32, low / len(pieces), high / len(pieces)))
        factor_of = factor_of * jnp.repeat(steps, extent[position] // blocks).reshape([-1 if axis == position else 1 for axis in range(len(extent))])
    return factor_of


def noise(rng, shape, scale, limit, pieces=(), kind=jnp.bfloat16):
    result = scale * jax.random.normal(rng, shape, jnp.float32)
    if pieces:
        result = result * levels(rng, shape, pieces, -0.22, 0.18)
    return jnp.clip(result, -limit, limit).astype(kind)


def setup_inputs(seed: int = 0) -> dict:
    arg_keys = jax.random.split(jax.random.key(seed), 13)
    return {
        "block_input": noise(arg_keys[0], (MICRO, TOK_MB, D), 1.0, 6.0, ((1, 64),)),
        "out_cotangent": noise(arg_keys[1], (MICRO, TOK_MB, D), 1.0, 6.0, ((1, 64),)),
        "drop_flags": plant(jax.random.randint(arg_keys[2], (MICRO, PAGES_ROW), 0, 3), jax.random.fold_in(arg_keys[2], 1), 0, 2).astype(jnp.int32),
        "key_valid": plant((jax.random.randint(arg_keys[3], (MICRO, PAGES_ROW, BLOCKS), 0, 4) < 3).astype(jnp.int32), jax.random.fold_in(arg_keys[3], 1), 0, 1),
        "qkv_weight": noise(arg_keys[4], (2, D, 3, D), D ** -0.5, 0.21875, ((0, 2), (3, 4))),
        "out_weight": noise(arg_keys[5], (2, D, D), (D // 32) ** -0.5, 1.25, ((0, 2), (1, 4))),
        "up_weight": noise(arg_keys[6], (2, D, FF), D ** -0.5, 0.21875, ((0, 2), (2, 4))),
        "down_weight": noise(arg_keys[7], (2, FF, D), (FF // 2) ** -0.5, 0.15625, ((0, 2), (1, 4))),
        "hidden_bias": noise(arg_keys[8], (2, FF), 0.5, 3.0, ((0, 2), (1, 4)), jnp.float32),
        "norm_gains": jnp.clip(1.0 + 0.1 * jax.random.normal(arg_keys[9], (2, 2, D), jnp.float32), 0.5, 1.5),
        "norm_shifts": noise(arg_keys[10], (2, 2, D), 0.3, 2.0, ((0, 2),), jnp.float32),
        "out_biases": noise(arg_keys[11], (2, 2, D), 0.3, 2.0, ((0, 2),), jnp.float32),
    }


@jax.custom_vjp
def low(v):
    return lax.optimization_barrier(v.astype(jnp.bfloat16)).astype(jnp.float32)

@jax.custom_vjp
def low_back(v):
    return v

def low_keep(v):
    return (low(v), None)

def low_pass(kept, grad):
    return (grad,)

def back_keep(v):
    return (v, None)

def back_low(kept, grad):
    return (low(grad),)
low.defvjp(low_keep, low_pass)
low_back.defvjp(back_keep, back_low)
highest = lax.Precision.HIGHEST

def layer_norm(values, gain, shift):
    centre = values - lax.optimization_barrier(jnp.mean(values, axis=-1, keepdims=True))
    spread = lax.optimization_barrier(jnp.mean(centre * centre, axis=-1, keepdims=True))
    return centre * lax.rsqrt(spread + 1e-05) * gain + shift

def allowed_pairs(flags, valid, crossing):
    place = jnp.arange(BLOCKS, dtype=jnp.int32)
    visual = place >= TEXT
    dropped = (flags[:, None] == 1) & visual[None] | (flags[:, None] == 2) & ~visual[None]
    key_ok = (valid == 1) & ~dropped
    same = place[:, None] == place[None, :]
    other = visual[:, None] != visual[None, :]
    pair_ok = jnp.logical_or(other, not crossing)
    return same[None] | pair_ok[None] & key_ok[:, None, :]

def layer(inputs, params, allowed):
    qkv_weight, out_weight, up_weight, hidden_bias, down_weight, gains, shifts, biases = params
    pages = inputs.shape[0]
    scale = HEAD ** (-0.5)
    normed = low(layer_norm(inputs, gains[0], shifts[0]))
    projected = low_back(low(jnp.einsum('pid,dch->pich', normed, qkv_weight, precision=highest)))
    split = projected.reshape(pages, BLOCKS, 3, HEADS, HEAD)
    scores = low_back(jnp.einsum('pihe,pjhe->phij', split[:, :, 0], split[:, :, 1], precision=highest) * scale)
    scores = jnp.where(allowed[:, None], scores, -1e+30)
    peak = lax.optimization_barrier(jnp.max(scores, axis=-1, keepdims=True))
    expo = jnp.exp(scores - peak)
    probs = expo / lax.optimization_barrier(jnp.sum(expo, axis=-1, keepdims=True))
    mixed = jnp.einsum('phij,pjhe->pihe', low(probs), split[:, :, 2], precision=highest)
    mixed = low_back(low(mixed)).reshape(pages, BLOCKS, D)
    middle = inputs + low_back(jnp.einsum('pih,hd->pid', mixed, out_weight, precision=highest)) + biases[0]
    second = low(layer_norm(middle, gains[1], shifts[1]))
    pre_act = low_back(jnp.einsum('pid,df->pif', second, up_weight, precision=highest) + hidden_bias)
    activated = low(jax.nn.gelu(pre_act, approximate=False))
    return middle + low_back(jnp.einsum('pif,fd->pid', activated, down_weight, precision=highest)) + biases[1]

def reference(block_input, out_cotangent, drop_flags, key_valid, qkv_weight, out_weight, up_weight, down_weight, hidden_bias, norm_gains, norm_shifts, out_biases):
    total_pages = drop_flags.shape[0] * drop_flags.shape[1]
    group = PAGES_MB * MICRO
    count = total_pages // group

    def pages_of(values):
        return values.astype(jnp.float32).reshape(count, group, BLOCKS, D)
    items = (pages_of(block_input), pages_of(out_cotangent), drop_flags.reshape(count, group), key_valid.reshape(count, group, BLOCKS))
    stacked = (qkv_weight, out_weight, up_weight, hidden_bias, down_weight, norm_gains, norm_shifts, out_biases)
    params = tuple((tuple((array[level].astype(jnp.float32) for array in stacked)) for level in range(2)))
    zeros = jax.tree.map(jnp.zeros_like, params)

    def step(totals, item):
        inputs, cotangent, flags, valid = item
        cross_mask = allowed_pairs(flags, valid, True)
        self_mask = allowed_pairs(flags, valid, False)
        first, back_one = jax.vjp(lambda values, weights: layer(values, weights, cross_mask), inputs, params[0])
        first_low = first.astype(jnp.bfloat16)
        second, back_two = jax.vjp(lambda values, weights: layer(values, weights, self_mask), first_low.astype(jnp.float32), params[1])
        grad_first, grad_two = back_two(cotangent)
        grad_first_low = grad_first.astype(jnp.bfloat16)
        grad_inputs, grad_one = back_one(grad_first_low.astype(jnp.float32))
        totals = jax.tree.map(lambda left, right: left + right, totals, (grad_one, grad_two))
        return (totals, (first_low, second.astype(jnp.bfloat16), grad_inputs.astype(jnp.bfloat16), grad_first_low))
    totals, outputs = lax.scan(step, zeros, items)
    first_low, second_low, grad_inputs, grad_first_low = outputs
    shape = (MICRO, TOK_MB, D)
    activations = jnp.stack([first_low.reshape(shape), second_low.reshape(shape)])
    input_grads = jnp.stack([grad_inputs.reshape(shape), grad_first_low.reshape(shape)])
    grads = [jnp.stack([totals[0][index], totals[1][index]]) for index in range(8)]
    return (activations, input_grads, grads[0], grads[1], grads[2], grads[4], grads[3], grads[5], grads[6], grads[7])
```

```python
from functools import partial

import jax
import jax.numpy as jnp
from jax import lax
from jax.experimental import pallas as pl
from jax.experimental.pallas import tpu as pltpu
from jax.sharding import Mesh
from jax.sharding import PartitionSpec as P

BF = jnp.bfloat16
F32 = jnp.float32
D = 768
BLOCKS = 96
TEXT = 72
ROWS = 288
PAGES = 3
SCALE = 0.125
VMEM_LIMIT = 48 * 1024 * 1024

MESH_AXES = ("y", "x", "pipe", "zhi", "core")
DP = ("y", "x")
TENSOR = ("zhi", "core")


def swap_cores(value):
    return lax.ppermute(value, "core", [(0, 1), (1, 0)])


def swap_z(value, k):
    pairs = []
    for p in range(2):
        for h in range(2):
            other = (2 * h + p) ^ k
            pairs.append((p * 2 + h, (other & 1) * 2 + (other >> 1)))
    return lax.ppermute(value, ("pipe", "zhi"), pairs)


def ring_shift(value, axis_of_core, shift):
    pairs = []
    for y in range(4):
        for x in range(4):
            for c in range(2):
                if axis_of_core[c] == "x":
                    to = (y, (x + shift) % 4)
                else:
                    to = ((y + shift) % 4, x)
                pairs.append(((y * 4 + x) * 2 + c, (to[0] * 4 + to[1]) * 2 + c))
    return lax.ppermute(value, ("y", "x", "core"), pairs)


FIRST = ("x", "y")
SECOND = ("y", "x")
ONLY_X = ("x", "x")
ONLY_Y = ("y", "y")


def mm(a, b):
    return lax.dot_general(a, b, (((1,), (0,)), ((), ())), preferred_element_type=F32)


def mt(a, b):
    return lax.dot_general(a, b, (((1,), (1,)), ((), ())), preferred_element_type=F32)


def tm(a, b):
    return lax.dot_general(a, b, (((0,), (0,)), ((), ())), preferred_element_type=F32)


def normed(values):
    centre = values - jnp.mean(values, axis=-1, keepdims=True)
    spread = jnp.mean(centre * centre, axis=-1, keepdims=True)
    inverse = lax.rsqrt(spread + 1e-05)
    return centre * inverse, inverse


def norm_back(grad, unit, inverse, gain):
    scaled = grad * gain
    mean_one = jnp.mean(scaled, axis=-1, keepdims=True)
    mean_two = jnp.mean(scaled * unit, axis=-1, keepdims=True)
    return inverse * (scaled - mean_one - unit * mean_two)


def column_sum(values):
    return jnp.sum(values, axis=0, keepdims=True)


def half_masks():
    lane = lax.broadcasted_iota(jnp.int32, (1, 128), 1)
    low = (lane < 64).astype(F32)
    return low.astype(BF), (1.0 - low).astype(BF)


def fetch_attn(layer, place, own_qkv, own_out, parts, held, sem):
    pipe, i1, i2 = place[0], place[1], place[2]

    def gathered(hh, k):
        for d2 in range(4):
            for d1 in range(4):
                group = (i2 + d2) & 3
                row = group * 384 + hh * 192 + ((i1 + d1) & 3) * 48
                pltpu.make_async_copy(
                    parts[d2].at[d1, k - 1, pl.ds(0, 48)],
                    held.at[pl.ds(pl.multiple_of(row, 16), 48)],
                    sem,
                ).start()

    @pl.when(pipe == layer)
    def _():
        for group in range(3):
            pltpu.make_async_copy(
                own_qkv.at[pl.ds(group * 192, 192)], held.at[pl.ds(group * 384, 192)], sem
            ).start()
        pltpu.make_async_copy(own_out, held.at[pl.ds(1152, 192)], sem).start()
        gathered(1, 2)

    @pl.when(pipe != layer)
    def _():
        gathered(0, 1)
        gathered(1, 3)


def fetch_ffn(layer, place, own_up, own_down, parts, held, sem):
    pipe, i1, i2 = place[0], place[1], place[2]

    def gathered(hh, k):
        for d2 in range(4):
            for d1 in range(4):
                row = (((i2 + d2) & 3) * 4 + ((i1 + d1) & 3)) * 96
                pltpu.make_async_copy(
                    parts[d2].at[d1, k - 1, pl.ds(48, 96)],
                    held.at[hh, pl.ds(pl.multiple_of(row, 16), 96)],
                    sem,
                ).start()

    @pl.when(pipe == layer)
    def _():
        pltpu.make_async_copy(own_up, held.at[0, pl.ds(0, 768)], sem).start()
        pltpu.make_async_copy(own_down, held.at[0, pl.ds(768, 768)], sem).start()
        gathered(1, 2)

    @pl.when(pipe != layer)
    def _():
        gathered(0, 1)
        gathered(1, 3)


def wait_whole(held, sem):
    pltpu.make_async_copy(held, held, sem).wait()


def send_blocks(place, held, outs, sem):
    core, i1 = place[3], place[1]
    step1 = jnp.where(core == 0, 48, 192)
    step2 = jnp.where(core == 0, 192, 48)
    for d1 in range(4):
        for j2 in range(4):
            row = ((i1 + d1) & 3) * step1 + j2 * step2
            pltpu.make_async_copy(
                held.at[pl.ds(pl.multiple_of(row, 16), 48)], outs[d1].at[j2], sem
            ).start()
    pltpu.make_async_copy(held, held, sem).wait()


def attn_forward_body(x, small, mask_ref, held, a_ref, p_ref, o_ref, part_ref, wait):
    unit, _ = normed(x)
    a_ref[...] = (unit * small[0:1] + small[1:2]).astype(BF)
    wait()
    for n in range(9):
        cols = pl.ds(n * 128, 128)
        p_ref[:, cols] = mt(a_ref[...], held[cols, :]).astype(BF)
    low, high = half_masks()
    for page in range(PAGES):
        rows = pl.ds(page * BLOCKS, BLOCKS)
        allowed = mask_ref[page] > 0.5
        for pair in range(3):
            q = p_ref[rows, pl.ds(pair * 128, 128)]
            k = p_ref[rows, pl.ds(384 + pair * 128, 128)]
            v = p_ref[rows, pl.ds(768 + pair * 128, 128)]
            total = None
            for half in (low, high):
                scores = jnp.where(allowed, mt(q, k * half) * SCALE, -1e30)
                peak = jnp.max(scores, axis=-1, keepdims=True)
                expo = jnp.exp(scores - peak)
                probs = expo / jnp.sum(expo, axis=-1, keepdims=True)
                term = mm(probs.astype(BF), v * half)
                total = term if total is None else total + term
            o_ref[rows, pl.ds(pair * 128, 128)] = total.astype(BF)
    part_ref[...] = mm(o_ref[...], held[pl.ds(1152, 384), :]).astype(BF)


def attn_first_kernel(
    place, x_ref, small, mask_ref, own_qkv, own_out, b0, b1, b2, b3,
    a_ref, p_ref, o_ref, part_ref, held, sem,
):
    fetch_attn(0, place, own_qkv, own_out, (b0, b1, b2, b3), held, sem)
    attn_forward_body(
        x_ref[...].astype(F32), small, mask_ref, held, a_ref, p_ref, o_ref, part_ref,
        lambda: wait_whole(held, sem),
    )


def attn_second_kernel(
    place, mid_ref, mine, other, before, small, mask_ref, own_qkv, own_out, b0, b1, b2, b3,
    y_ref, a_ref, p_ref, o_ref, part_ref, held, sem,
):
    fetch_attn(1, place, own_qkv, own_out, (b0, b1, b2, b3), held, sem)
    total = mine[...].astype(F32) + other[...].astype(F32)
    y_ref[...] = (mid_ref[...] + total + before[5:6]).astype(BF)
    attn_forward_body(
        y_ref[...].astype(F32), small, mask_ref, held, a_ref, p_ref, o_ref, part_ref,
        lambda: wait_whole(held, sem),
    )


def ffn_forward_body(x_ref, mine, other, small, hidden, held, mid_ref, c_ref, e_ref, slope_ref, part_ref, wait):
    mid = x_ref[...].astype(F32) + (mine[...].astype(F32) + other[...].astype(F32)) + small[4:5]
    mid_ref[...] = mid
    unit, _ = normed(mid)
    c_ref[...] = (unit * small[2:3] + small[3:4]).astype(BF)
    wait()
    for n in range(6):
        hh, cols = n // 3, pl.ds(n % 3 * 256, 256)
        wide = pl.ds(n * 256, 256)
        pre = mm(c_ref[...], held[hh, pl.ds(0, 768), cols]) + hidden[:, wide]
        cdf = 0.5 * (1.0 + lax.erf(pre * 0.7071067811865476))
        e_ref[:, wide] = (pre * cdf).astype(BF)
        slope_ref[:, wide] = cdf + pre * (jnp.exp(-0.5 * pre * pre) * 0.3989422804014327)
    part_ref[...] = (
        mm(e_ref[:, pl.ds(0, 768)], held[0, pl.ds(768, 768), :])
        + mm(e_ref[:, pl.ds(768, 768)], held[1, pl.ds(768, 768), :])
    ).astype(BF)


def ffn_backward_body(grad, e_unused, slope_ref, held, du_ref, part_ref, hidden_ref):
    for n in range(6):
        hh, wide = n // 3, pl.ds(n * 256, 256)
        grad_e = mt(grad, held[hh, pl.ds(768 + n % 3 * 256, 256), :])
        grad_u = (grad_e * slope_ref[:, wide]).astype(BF)
        du_ref[:, wide] = grad_u
        hidden_ref[:, wide] = column_sum(grad_u.astype(F32))
    part_ref[...] = (
        mt(du_ref[:, pl.ds(0, 768)], held[0, pl.ds(0, 768), :])
        + mt(du_ref[:, pl.ds(768, 768)], held[1, pl.ds(0, 768), :])
    ).astype(BF)


def ffn_first_kernel(
    place, x_ref, mine, other, small, hidden, own_up, own_down, b0, b1, b2, b3,
    mid_ref, c_ref, e_ref, slope_ref, part_ref, held, sem,
):
    fetch_ffn(0, place, own_up, own_down, (b0, b1, b2, b3), held, sem)
    ffn_forward_body(
        x_ref, mine, other, small, hidden, held, mid_ref, c_ref, e_ref, slope_ref, part_ref,
        lambda: wait_whole(held, sem),
    )


def ffn_second_kernel(
    place, x_ref, mine, other, small, hidden, grad_ref, own_up, own_down, b0, b1, b2, b3,
    mid_ref, c_ref, e_ref, part_ref, du_ref, back_ref, hidden_ref, held, slope, sem,
):
    fetch_ffn(1, place, own_up, own_down, (b0, b1, b2, b3), held, sem)
    ffn_forward_body(
        x_ref, mine, other, small, hidden, held, mid_ref, c_ref, e_ref, slope, part_ref,
        lambda: wait_whole(held, sem),
    )
    ffn_backward_body(grad_ref[...], None, slope, held, du_ref, back_ref, hidden_ref)


def ffn_back_kernel(
    place, mine, other, up_grad, x_ref, small, slope_ref, own_up, own_down, b0, b1, b2, b3,
    dx_ref, du_ref, back_ref, hidden_ref, sums_ref, held, sem,
):
    fetch_ffn(0, place, own_up, own_down, (b0, b1, b2, b3), held, sem)
    layer_input_back(mine, other, up_grad, x_ref, small, dx_ref, sums_ref)
    wait_whole(held, sem)
    ffn_backward_body(dx_ref[...], None, slope_ref, held, du_ref, back_ref, hidden_ref)


def layer_input_back(mine, other, up_grad, x_ref, small, dx_ref, sums_ref):
    grad = mine[...].astype(F32) + other[...].astype(F32)
    unit, inverse = normed(x_ref[...].astype(F32))
    sums_ref[0:1] = column_sum(grad * unit)
    sums_ref[1:2] = column_sum(grad)
    dx_ref[...] = (up_grad[...] + norm_back(grad, unit, inverse, small[0:1])).astype(BF)


def last_kernel(mine, other, up_grad, x_ref, small, dx_ref, sums_ref):
    layer_input_back(mine, other, up_grad, x_ref, small, dx_ref, sums_ref)


def attn_back_kernel(
    layer, place, mine, other, dy_ref, mid_ref, small, mask_ref, p_ref, own_qkv, own_out, b0, b1, b2, b3,
    dmid_ref, dr_ref, dp_ref, part_ref, sums_ref, held, grad_o, sem,
):
    fetch_attn(layer, place, own_qkv, own_out, (b0, b1, b2, b3), held, sem)
    grad = mine[...].astype(F32) + other[...].astype(F32)
    dy = dy_ref[...].astype(F32)
    unit, inverse = normed(mid_ref[...])
    sums_ref[0:1] = column_sum(grad * unit)
    sums_ref[1:2] = column_sum(grad)
    dmid = dy + norm_back(grad, unit, inverse, small[2:3])
    dmid_ref[...] = dmid
    sums_ref[2:3] = column_sum(dmid)
    sums_ref[3:4] = column_sum(dy)
    dr_ref[...] = dmid.astype(BF)
    wait_whole(held, sem)
    grad_o[...] = mt(dr_ref[...], held[pl.ds(1152, 384), :]).astype(BF)
    low, high = half_masks()
    for page in range(PAGES):
        rows = pl.ds(page * BLOCKS, BLOCKS)
        allowed = mask_ref[page] > 0.5
        for pair in range(3):
            q = p_ref[rows, pl.ds(pair * 128, 128)]
            k = p_ref[rows, pl.ds(384 + pair * 128, 128)]
            v = p_ref[rows, pl.ds(768 + pair * 128, 128)]
            do = grad_o[rows, pl.ds(pair * 128, 128)]
            dq = dk = dv = None
            for half in (low, high):
                kh = k * half
                scores = jnp.where(allowed, mt(kh, q) * SCALE, -1e30)
                peak = jnp.max(scores, axis=0, keepdims=True)
                expo = jnp.exp(scores - peak)
                probs = expo / jnp.sum(expo, axis=0, keepdims=True)
                dprobs = mt(v * half, do)
                inner = jnp.sum(probs * dprobs, axis=0, keepdims=True)
                dz = (probs * (dprobs - inner)).astype(BF)
                one = tm(dz, kh)
                two = mm(dz, q * half)
                three = mm(probs.astype(BF), do * half)
                dq = one if dq is None else dq + one
                dk = two if dk is None else dk + two
                dv = three if dv is None else dv + three
            dp_ref[rows, pl.ds(pair * 128, 128)] = (dq * SCALE).astype(BF)
            dp_ref[rows, pl.ds(384 + pair * 128, 128)] = (dk * SCALE).astype(BF)
            dp_ref[rows, pl.ds(768 + pair * 128, 128)] = dv.astype(BF)
    part_ref[...] = mm(dp_ref[...], held[pl.ds(0, 1152), :]).astype(BF)


def attn_grads_kernel(place, a_ref, dp_ref, dr_ref, o_ref, g0, g1, g2, g3, held, sem):
    for n in range(3):
        cols = pl.ds(n * 384, 384)
        held[:, cols] = tm(a_ref[...], dp_ref[:, cols]).astype(BF)
    held[:, pl.ds(1152, 384)] = tm(dr_ref[...], o_ref[...]).astype(BF)
    send_blocks(place, held, (g0, g1, g2, g3), sem)


def ffn_grads_kernel(place, c_ref, du_ref, df_ref, e_ref, g0, g1, g2, g3, held, sem):
    for n in range(4):
        cols = pl.ds(n * 384, 384)
        held[:, cols] = tm(c_ref[...], du_ref[:, cols]).astype(BF)
    for n in range(4):
        held[:, pl.ds(1536 + n * 384, 384)] = tm(df_ref[...], e_ref[:, pl.ds(n * 384, 384)]).astype(BF)
    send_blocks(place, held, (g0, g1, g2, g3), sem)


VM = pl.BlockSpec(memory_space=pltpu.VMEM)
SM = pl.BlockSpec(memory_space=pltpu.SMEM)
ANY = pl.BlockSpec(memory_space=pl.ANY)


def shape(dims, dtype):
    return jax.ShapeDtypeStruct(dims, dtype)


def call(body, ins, outs, scratch, args, flops):
    sizes = sum(a.size * a.dtype.itemsize for a in args)
    return pl.pallas_call(
        body,
        in_specs=ins,
        out_specs=tuple(spec for spec, _ in outs),
        out_shape=tuple(form for _, form in outs),
        scratch_shapes=scratch,
        compiler_params=pltpu.CompilerParams(vmem_limit_bytes=VMEM_LIMIT),
        cost_estimate=pl.CostEstimate(flops=flops, bytes_accessed=sizes, transcendentals=0),
    )(*args)


ATTN_HELD = pltpu.VMEM((1536, 768), BF)
FFN_HELD = pltpu.VMEM((2, 1536, 768), BF)
SEM = pltpu.SemaphoreType.DMA(())
ROW_BF = (VM, shape((ROWS, D), BF))
ROW_F32 = (VM, shape((ROWS, D), F32))
WIDE_BF = (VM, shape((ROWS, 1536), BF))
ATTN_OUTS = [ROW_BF, (VM, shape((ROWS, 1152), BF)), (VM, shape((ROWS, 384), BF)), ROW_BF]


def pairs_allowed(flags, valid):
    place = lax.broadcasted_iota(jnp.int32, (BLOCKS,), 0)
    visual = place >= TEXT
    dropped = (flags[:, None] == 1) & visual[None] | (flags[:, None] == 2) & ~visual[None]
    key_ok = (valid == 1) & ~dropped
    same = place[:, None] == place[None, :]
    other = visual[:, None] != visual[None, :]
    cross = same[None] | other[None] & key_ok[:, None, :]
    plain = same[None] | key_ok[:, None, :]
    masks = []
    for allowed in (cross, plain):
        allowed = allowed.astype(F32)
        masks.append((allowed, jnp.swapaxes(allowed, 1, 2)))
    return masks


def reduce_rings(blocks, i2):
    got = [blocks[0]] + [ring_shift(blocks[s], FIRST, s) for s in (1, 2, 3)]
    total = sum(g.astype(F32) for g in got).astype(BF)
    mine = [lax.dynamic_index_in_dim(total, (i2 + s) & 3, 0, keepdims=False) for s in range(4)]
    got = [mine[0]] + [ring_shift(mine[s], SECOND, s) for s in (1, 2, 3)]
    return sum(g.astype(F32) for g in got)


def sum_ring(value, axes, place):
    got = jnp.stack([value] + [ring_shift(value, axes, s) for s in (1, 2, 3)])
    return sum(lax.dynamic_index_in_dim(got, (place - j) & 3, 0, keepdims=False) for j in range(4))


def on_device(
    block_input, out_cotangent, drop_flags, key_valid, qkv_weight, out_weight, up_weight, down_weight,
    hidden_bias, norm_gains, norm_shifts, out_biases,
):
    y, x = lax.axis_index("y"), lax.axis_index("x")
    pipe, zhi, core = lax.axis_index("pipe"), lax.axis_index("zhi"), lax.axis_index("core")
    zz = 2 * zhi + pipe
    i1 = jnp.where(core == 0, x, y)
    i2 = jnp.where(core == 0, y, x)
    place = jnp.stack([pipe, i1, i2, core]).astype(jnp.int32)

    own_qkv = jnp.transpose(qkv_weight[0], (1, 2, 0)).reshape(576, D)
    own_out, own_up, own_down = out_weight[0], up_weight[0], down_weight[0]
    number = i2 * 4 + i1
    attn_stack = jnp.concatenate([own_qkv, own_out])
    attn_slice = lax.dynamic_slice_in_dim(attn_stack, number * 48, 48)
    ffn_slice = jnp.where(
        number < 8,
        lax.dynamic_slice_in_dim(own_up, (number & 7) * 96, 96),
        lax.dynamic_slice_in_dim(own_down, (number & 7) * 96, 96),
    )
    piece = jnp.concatenate([attn_slice, ffn_slice])
    level = jnp.stack([swap_z(piece, k) for k in (1, 2, 3)])
    level = jnp.stack([level] + [ring_shift(level, FIRST, 4 - d) for d in (1, 2, 3)])
    parts = [level] + [ring_shift(level, SECOND, 4 - d) for d in (1, 2, 3)]

    small_own = jnp.stack(
        [norm_gains[0, 0], norm_shifts[0, 0], norm_gains[0, 1], norm_shifts[0, 1], out_biases[0, 0], out_biases[0, 1]]
    )
    packed = jnp.concatenate([small_own, hidden_bias])
    from_z = [packed] + [swap_z(packed, k) for k in (1, 2, 3)]
    own_layer = [from_z[0], from_z[2]]
    far_layer = [from_z[1], from_z[3]]
    small, hidden = [], []
    for layer in range(2):
        same, far = [jnp.where(pipe == layer, own_layer[i], far_layer[i]) for i in range(2)]
        small.append(same[:6])
        hidden.append(jnp.concatenate([same[6:7], far[6:7]], axis=1))

    both = jnp.stack([block_input, out_cotangent], axis=1)
    kept = lax.dynamic_index_in_dim(both, zz, 0, keepdims=False)
    came = swap_z(lax.dynamic_index_in_dim(both, zz ^ 3, 0, keepdims=False), 3)
    halves = jnp.where(zhi == 0, jnp.stack([kept, came]), jnp.stack([came, kept]))
    across = swap_cores(halves)
    rows = jnp.where(core == 0, jnp.stack([halves, across], 1), jnp.stack([across, halves], 1))
    x0 = rows[:, :, 0].reshape(ROWS, D)
    cotangent = rows[:, :, 1].reshape(ROWS, D)
    flags = lax.dynamic_index_in_dim(drop_flags, zz, 0, keepdims=False)
    valid = lax.dynamic_index_in_dim(key_valid, zz, 0, keepdims=False)
    masks = pairs_allowed(flags, valid)

    attn_args = [own_qkv, own_out, *parts]
    ffn_args = [own_up, own_down, *parts]
    any6 = [ANY] * 6
    unit = 2 * ROWS * D * 384

    a0, p0, o0, part = call(
        attn_first_kernel, [SM, VM, VM, VM] + any6, ATTN_OUTS, [ATTN_HELD, SEM],
        [place, x0, small[0], masks[0][0], *attn_args], 4 * unit,
    )
    mid0, c0, e0, slope0, part = call(
        ffn_first_kernel, [SM] + [VM] * 5 + any6,
        [ROW_F32, ROW_BF, WIDE_BF, (VM, shape((ROWS, 1536), F32)), ROW_BF], [FFN_HELD, SEM],
        [place, x0, part, swap_cores(part), small[0], hidden[0], *ffn_args], 8 * unit,
    )
    y0, a1, p1, o1, part = call(
        attn_second_kernel, [SM] + [VM] * 6 + any6, [ROW_BF] + ATTN_OUTS, [ATTN_HELD, SEM],
        [place, mid0, part, swap_cores(part), small[0], small[1], masks[1][0], *attn_args], 4 * unit,
    )
    hidden_sum = (VM, shape((1, 1536), F32))
    mid1, c1, e1, part, du1, back, dhidden1 = call(
        ffn_second_kernel, [SM] + [VM] * 6 + any6,
        [ROW_F32, ROW_BF, WIDE_BF, ROW_BF, WIDE_BF, ROW_BF, hidden_sum],
        [FFN_HELD, pltpu.VMEM((ROWS, 1536), F32), SEM],
        [place, y0, part, swap_cores(part), small[1], hidden[1], cotangent, *ffn_args], 16 * unit,
    )
    y1 = (mid1 + (part.astype(F32) + swap_cores(part).astype(F32)) + small[1][5]).astype(BF)

    attn_blocks = [(ANY, shape((4, 48, 1536), BF))] * 4
    ffn_blocks = [(ANY, shape((4, 48, 3072), BF))] * 4

    def ffn_grads(c, du, df, e):
        return call(
            ffn_grads_kernel, [SM] + [VM] * 4, ffn_blocks, [pltpu.VMEM((D, 3072), BF), SEM],
            [place, c, du, df, e], 8 * unit,
        )

    def attn_grads(a, dp, dr, o):
        return call(
            attn_grads_kernel, [SM] + [VM] * 4, attn_blocks, [pltpu.VMEM((D, 1536), BF), SEM],
            [place, a, dp, dr, o], 4 * unit,
        )

    def attn_back(layer, back, dy, mid, projected):
        return call(
            partial(attn_back_kernel, layer), [SM] + [VM] * 7 + any6,
            [ROW_F32, ROW_BF, (VM, shape((ROWS, 1152), BF)), ROW_BF, (VM, shape((4, D), F32))],
            [ATTN_HELD, pltpu.VMEM((ROWS, 384), BF), SEM],
            [place, back, swap_cores(back), dy, mid, small[layer], masks[layer][1], projected, *attn_args],
            5 * unit,
        )

    ffn1 = ffn_grads(c1, du1, cotangent, e1)
    ffn1 = reduce_rings(ffn1, i2)
    dmid1, dr1, dp1, back, sums1 = attn_back(1, back, cotangent, mid1, p1)
    attn1 = attn_grads(a1, dp1, dr1, o1)
    attn1 = reduce_rings(attn1, i2)
    two_sums = (VM, shape((2, D), F32))
    dx1, du0, back, dhidden0, first1 = call(
        ffn_back_kernel, [SM] + [VM] * 6 + any6, [ROW_BF, WIDE_BF, ROW_BF, hidden_sum, two_sums],
        [FFN_HELD, SEM],
        [place, back, swap_cores(back), dmid1, y0, small[1], slope0, *ffn_args], 8 * unit,
    )
    ffn0 = ffn_grads(c0, du0, dx1, e0)
    ffn0 = reduce_rings(ffn0, i2)
    dmid0, dr0, dp0, back, sums0 = attn_back(0, back, dx1, mid0, p0)
    attn0 = attn_grads(a0, dp0, dr0, o0)
    attn0 = reduce_rings(attn0, i2)
    dx0, first0 = call(
        last_kernel, [VM] * 5, [ROW_BF, two_sums], [],
        [back, swap_cores(back), dmid0, x0, small[0]], unit // 16,
    )

    by_layer = [
        (attn.reshape(48, 4, 2, 192), ffn.reshape(48, 2, 2, 768))
        for attn, ffn in ((attn0, ffn0), (attn1, ffn1))
    ]

    def for_partner(k):
        mine = pipe ^ (k & 1)
        attn = jnp.where(mine == 0, by_layer[0][0], by_layer[1][0])[:, :, k >> 1]
        ffn = jnp.where(mine == 0, by_layer[0][1], by_layer[1][1])[:, :, k >> 1]
        return jnp.concatenate([attn.reshape(48, D), ffn.reshape(48, 2 * D)], axis=1)

    final = for_partner(0)
    for k in (1, 2, 3):
        final = final + swap_z(for_partner(k).astype(BF), k).astype(F32)
    grad_qkv = final[:, :576].reshape(48, 3, 192)
    grad_out = final[:, 576:768].T
    grad_up = final[:, 768:1536]
    grad_down = final[:, 1536:].T

    def in_place(dhidden):
        two = dhidden.reshape(2, D)
        return jnp.where(zhi == 0, two, two[::-1])

    vec = jnp.concatenate(
        [first0, sums0, in_place(dhidden0), first1, sums1, in_place(dhidden1)]
    )
    vec = sum_ring(vec, ONLY_X, x)
    vec = sum_ring(vec, ONLY_Y, y)
    vec = vec.reshape(2, 8, D)
    got = [lax.dynamic_index_in_dim(vec, pipe, 0, keepdims=False)]
    for k in (1, 2, 3):
        got.append(swap_z(lax.dynamic_index_in_dim(vec, pipe ^ (k & 1), 0, keepdims=False), k))
    got = jnp.stack(got)
    vec = sum(lax.dynamic_index_in_dim(got, zz ^ j, 0, keepdims=False) for j in range(4))
    across = swap_cores(vec)
    low = jnp.where(core == 0, vec, across)
    high = jnp.where(core == 0, across, vec)
    grad_hidden = jnp.stack([low[6], high[6], low[7], high[7]]).reshape(1, 4 * D)
    grad_gains = low[jnp.array([0, 2])]
    grad_shifts = low[jnp.array([1, 3])]
    grad_biases = low[4:6]

    def spread(first, second):
        tall = jnp.stack([first, second]).reshape(2, 2, 2, 72, D)

        def for_chip(k):
            rows = lax.dynamic_index_in_dim(tall, pipe ^ (k & 1), 0, keepdims=False)
            rows = lax.dynamic_index_in_dim(rows, zhi ^ (k >> 1), 0, keepdims=False)
            return lax.dynamic_index_in_dim(rows, core, 0, keepdims=False)

        got = jnp.stack([for_chip(0)] + [swap_z(for_chip(k), k) for k in (1, 2, 3)])
        return jnp.stack([lax.dynamic_index_in_dim(got, zz ^ m, 0, keepdims=False) for m in range(4)])

    activations = spread(y0, y1)
    input_grads = spread(dx0, dx1)
    return (
        activations[None],
        input_grads[None],
        grad_qkv[None],
        grad_out[None],
        grad_up[None],
        grad_down[None],
        grad_hidden,
        grad_gains[None],
        grad_shifts[None],
        grad_biases[None],
    )


def solution(mesh):
    fine = Mesh(mesh.devices.reshape(4, 4, 2, 2, 2), MESH_AXES)
    rows = DP + TENSOR
    in_specs = (
        P(None, rows, None),
        P(None, rows, None),
        P(None, DP),
        P(None, DP, None),
        P("pipe", None, None, TENSOR),
        P("pipe", TENSOR, None),
        P("pipe", None, TENSOR),
        P("pipe", TENSOR, None),
        P("pipe", TENSOR),
        P("pipe", None, None),
        P("pipe", None, None),
        P("pipe", None, None),
    )
    out_specs = (
        P("pipe", None, rows, None),
        P("pipe", None, rows, None),
        P("pipe", DP, None, TENSOR),
        P("pipe", TENSOR, DP),
        P("pipe", DP, TENSOR),
        P("pipe", TENSOR, DP),
        P("pipe", None),
        P("pipe", None, None),
        P("pipe", None, None),
        P("pipe", None, None),
    )
    return jax.shard_map(on_device, mesh=fine, in_specs=in_specs, out_specs=out_specs, check_vma=False)
```

```python
from functools import partial

import jax
import jax.numpy as jnp
from jax import lax
from jax.experimental import pallas as pl
from jax.experimental.pallas import tpu as pltpu
from jax.sharding import Mesh
from jax.sharding import PartitionSpec as P

BF = jnp.bfloat16
F32 = jnp.float32
D = 768
BLOCKS = 96
TEXT = 72
ROWS = 288
PAGES = 3
SCALE = 0.125
VMEM_LIMIT = 20 * 1024 * 1024

MESH_AXES = ("y", "x", "pipe", "zhi", "core")
DP = ("y", "x")
TENSOR = ("zhi", "core")


def swap_cores(value):
    return lax.ppermute(value, "core", [(0, 1), (1, 0)])


def swap_z(value, k):
    pairs = []
    for p in range(2):
        for h in range(2):
            other = (2 * h + p) ^ k
            pairs.append((p * 2 + h, (other & 1) * 2 + (other >> 1)))
    return lax.ppermute(value, ("pipe", "zhi"), pairs)


def ring_shift(value, axis_of_core, shift):
    pairs = []
    for y in range(4):
        for x in range(4):
            for c in range(2):
                if axis_of_core[c] == "x":
                    to = (y, (x + shift) % 4)
                else:
                    to = ((y + shift) % 4, x)
                pairs.append(((y * 4 + x) * 2 + c, (to[0] * 4 + to[1]) * 2 + c))
    return lax.ppermute(value, ("y", "x", "core"), pairs)


FIRST = ("x", "y")
SECOND = ("y", "x")
ONLY_X = ("x", "x")
ONLY_Y = ("y", "y")


def mm(a, b):
    return lax.dot_general(a, b, (((1,), (0,)), ((), ())), preferred_element_type=F32)


def mt(a, b):
    return lax.dot_general(a, b, (((1,), (1,)), ((), ())), preferred_element_type=F32)


def tm(a, b):
    return lax.dot_general(a, b, (((0,), (0,)), ((), ())), preferred_element_type=F32)


def normed(values):
    centre = values - jnp.mean(values, axis=-1, keepdims=True)
    spread = jnp.mean(centre * centre, axis=-1, keepdims=True)
    inverse = lax.rsqrt(spread + 1e-05)
    return centre * inverse, inverse


def norm_back(grad, unit, inverse, gain):
    scaled = grad * gain
    mean_one = jnp.mean(scaled, axis=-1, keepdims=True)
    mean_two = jnp.mean(scaled * unit, axis=-1, keepdims=True)
    return inverse * (scaled - mean_one - unit * mean_two)


def column_sum(values):
    return jnp.sum(values, axis=0, keepdims=True)


def half_masks():
    lane = lax.broadcasted_iota(jnp.int32, (1, 128), 1)
    low = (lane < 64).astype(F32)
    return low.astype(BF), (1.0 - low).astype(BF)


def fetch_attn(layer, place, own, far1, far2a, far2b, far3, held, sem):
    pipe, zhi = place[0], place[4]

    def whole(source, half):
        for group in range(4):
            row = group * 384 + half * 192
            pltpu.make_async_copy(
                source.at[pl.ds(group * 192, 192)], held.at[pl.ds(pl.multiple_of(row, 16), 192)], sem
            ).start()

    def in_halves(half):
        for group in range(4):
            source = far2a if group < 2 else far2b
            row = group * 384 + half * 192
            pltpu.make_async_copy(
                source.at[pl.ds(group % 2 * 192, 192)],
                held.at[pl.ds(pl.multiple_of(row, 16), 192)],
                sem,
            ).start()

    @pl.when(pipe == layer)
    def _():
        whole(own, zhi)
        in_halves(1 - zhi)

    @pl.when(pipe != layer)
    def _():
        whole(far1, zhi)
        whole(far3, 1 - zhi)


def ffn_block(parts, slot, d2, d1):
    if slot < 2:
        if d2 == 2:
            return parts[3 + slot].at[d1]
        return parts[(0, 1, None, 2)[d2]].at[slot, d1]
    if d2 == 2:
        return parts[8 + d1 // 2].at[d1 % 2]
    return parts[(5, 6, None, 7)[d2]].at[d1]


def fetch_ffn(layer, place, own_up, own_down, parts, held, sem):
    pipe, i1, i2, zhi = place[0], place[1], place[2], place[4]

    def gathered(half, slot):
        for d2 in range(4):
            for d1 in range(4):
                row = (((i2 + d2) & 3) * 4 + ((i1 + d1) & 3)) * 96
                pltpu.make_async_copy(
                    ffn_block(parts, slot, d2, d1),
                    held.at[half, pl.ds(pl.multiple_of(row, 16), 96)],
                    sem,
                ).start()

    def mine():
        pltpu.make_async_copy(own_up, held.at[zhi, pl.ds(0, 768)], sem).start()
        pltpu.make_async_copy(own_down, held.at[zhi, pl.ds(768, 768)], sem).start()

    @pl.when(pipe == layer)
    def _():
        mine()
        gathered(1 - zhi, 2 * layer)

    @pl.when(pipe != layer)
    def _():
        gathered(zhi, layer)
        gathered(1 - zhi, layer + 1)


def wait_whole(held, sem):
    pltpu.make_async_copy(held, held, sem).wait()


def ring_slot(d1, j2):
    if d1 == 0:
        return 3
    if d1 == 2:
        return 0 if j2 < 2 else 1
    if d1 == 1:
        return 2 if j2 < 2 else 0
    return 1 if j2 < 2 else 2


def send_blocks(place, held, outs, sem, extra=None):
    core, i1 = place[3], place[1]
    step1 = jnp.where(core == 0, 48, 192)
    step2 = jnp.where(core == 0, 192, 48)
    width = held.shape[1]
    for d1 in range(4):
        for j2 in range(4):
            row = pl.multiple_of(((i1 + d1) & 3) * step1 + j2 * step2, 16)
            to = outs[ring_slot(d1, j2)]
            if extra is None:
                pltpu.make_async_copy(held.at[pl.ds(row, 48)], to.at[j2], sem).start()
            else:
                pltpu.make_async_copy(
                    held.at[pl.ds(row, 48)], to.at[j2, :, pl.ds(0, width)], sem
                ).start()
                pltpu.make_async_copy(
                    extra.at[pl.ds(row, 48)], to.at[j2, :, pl.ds(width, extra.shape[1])], sem
                ).start()
    pltpu.make_async_copy(held, held, sem).wait()
    if extra is not None:
        pltpu.make_async_copy(extra, extra, sem).wait()


def attn_forward_body(x, small, mask_ref, held, a_ref, p_ref, o_ref, part_ref, wait):
    unit, _ = normed(x)
    a_ref[...] = (unit * small[0:1] + small[1:2]).astype(BF)
    wait()
    for n in range(9):
        cols = pl.ds(n * 128, 128)
        p_ref[:, cols] = mt(a_ref[...], held[cols, :]).astype(BF)
    low, high = half_masks()
    for page in range(PAGES):
        rows = pl.ds(page * BLOCKS, BLOCKS)
        allowed = mask_ref[page] > 0.5
        for pair in range(3):
            q = p_ref[rows, pl.ds(pair * 128, 128)]
            k = p_ref[rows, pl.ds(384 + pair * 128, 128)]
            v = p_ref[rows, pl.ds(768 + pair * 128, 128)]
            total = None
            for half in (low, high):
                scores = jnp.where(allowed, mt(q, k * half) * SCALE, -1e30)
                peak = jnp.max(scores, axis=-1, keepdims=True)
                expo = jnp.exp(scores - peak)
                probs = expo / jnp.sum(expo, axis=-1, keepdims=True)
                term = mm(probs.astype(BF), v * half)
                total = term if total is None else total + term
            o_ref[rows, pl.ds(pair * 128, 128)] = total.astype(BF)
    part_ref[...] = mm(o_ref[...], held[pl.ds(1152, 384), :]).astype(BF)


def attn_first_kernel(
    place, x_ref, small, mask_ref, w0, w1, w2, w3, w4,
    a_ref, p_ref, o_ref, part_ref, held, sem,
):
    fetch_attn(0, place, w0, w1, w2, w3, w4, held, sem)
    attn_forward_body(
        x_ref[...].astype(F32), small, mask_ref, held, a_ref, p_ref, o_ref, part_ref,
        lambda: wait_whole(held, sem),
    )


def attn_second_kernel(
    place, mid_ref, mine, other, before, small, mask_ref, w0, w1, w2, w3, w4,
    y_ref, a_ref, p_ref, o_ref, part_ref, held, sem,
):
    fetch_attn(1, place, w0, w1, w2, w3, w4, held, sem)
    total = mine[...].astype(F32) + other[...].astype(F32)
    y_ref[...] = (mid_ref[...] + total + before[5:6]).astype(BF)
    attn_forward_body(
        y_ref[...].astype(F32), small, mask_ref, held, a_ref, p_ref, o_ref, part_ref,
        lambda: wait_whole(held, sem),
    )


def ffn_forward_body(x_ref, mine, other, small, hidden, held, mid_ref, c_ref, e_ref, slope_ref, part_ref, wait):
    mid = x_ref[...].astype(F32) + (mine[...].astype(F32) + other[...].astype(F32)) + small[4:5]
    mid_ref[...] = mid
    unit, _ = normed(mid)
    c_ref[...] = (unit * small[2:3] + small[3:4]).astype(BF)
    wait()
    for n in range(6):
        hh, cols = n // 3, pl.ds(n % 3 * 256, 256)
        wide = pl.ds(n * 256, 256)
        pre = mm(c_ref[...], held[hh, pl.ds(0, 768), cols]) + hidden[:, wide]
        cdf = 0.5 * (1.0 + lax.erf(pre * 0.7071067811865476))
        e_ref[:, wide] = (pre * cdf).astype(BF)
        slope_ref[:, wide] = cdf + pre * (jnp.exp(-0.5 * pre * pre) * 0.3989422804014327)
    part_ref[...] = (
        mm(e_ref[:, pl.ds(0, 768)], held[0, pl.ds(768, 768), :])
        + mm(e_ref[:, pl.ds(768, 768)], held[1, pl.ds(768, 768), :])
    ).astype(BF)


def ffn_backward_body(grad, e_unused, slope_ref, held, du_ref, part_ref, hidden_ref):
    for n in range(6):
        hh, wide = n // 3, pl.ds(n * 256, 256)
        grad_e = mt(grad, held[hh, pl.ds(768 + n % 3 * 256, 256), :])
        grad_u = (grad_e * slope_ref[:, wide]).astype(BF)
        du_ref[:, wide] = grad_u
        hidden_ref[:, wide] = column_sum(grad_u.astype(F32))
    part_ref[...] = (
        mt(du_ref[:, pl.ds(0, 768)], held[0, pl.ds(0, 768), :])
        + mt(du_ref[:, pl.ds(768, 768)], held[1, pl.ds(0, 768), :])
    ).astype(BF)


def ffn_first_kernel(
    place, x_ref, mine, other, small, hidden, own_up, own_down, t0, t1, t2, t3, t4,
    mid_ref, c_ref, e_ref, slope_ref, part_ref, held, sem,
):
    fetch_ffn(0, place, own_up, own_down, (t0, t1, t2, t3, t4), held, sem)
    ffn_forward_body(
        x_ref, mine, other, small, hidden, held, mid_ref, c_ref, e_ref, slope_ref, part_ref,
        lambda: wait_whole(held, sem),
    )


def ffn_second_kernel(
    place, x_ref, mine, other, small, hidden, grad_ref, own_up, own_down, t0, t1, t2, t3, t4, t5, t6, t7, t8, t9,
    mid_ref, c_ref, e_ref, part_ref, du_ref, back_ref, hidden_ref, held, slope, sem,
):
    fetch_ffn(1, place, own_up, own_down, (t0, t1, t2, t3, t4, t5, t6, t7, t8, t9), held, sem)
    ffn_forward_body(
        x_ref, mine, other, small, hidden, held, mid_ref, c_ref, e_ref, slope, part_ref,
        lambda: wait_whole(held, sem),
    )
    ffn_backward_body(grad_ref[...], None, slope, held, du_ref, back_ref, hidden_ref)


def ffn_back_kernel(
    place, mine, other, up_grad, x_ref, small, slope_ref, own_up, own_down, t0, t1, t2, t3, t4,
    dx_ref, du_ref, back_ref, hidden_ref, sums_ref, held, sem,
):
    fetch_ffn(0, place, own_up, own_down, (t0, t1, t2, t3, t4), held, sem)
    layer_input_back(mine, other, up_grad, x_ref, small, dx_ref, sums_ref)
    wait_whole(held, sem)
    ffn_backward_body(dx_ref[...], None, slope_ref, held, du_ref, back_ref, hidden_ref)


def layer_input_back(mine, other, up_grad, x_ref, small, dx_ref, sums_ref):
    grad = mine[...].astype(F32) + other[...].astype(F32)
    unit, inverse = normed(x_ref[...].astype(F32))
    sums_ref[0:1] = column_sum(grad * unit)
    sums_ref[1:2] = column_sum(grad)
    dx_ref[...] = (up_grad[...] + norm_back(grad, unit, inverse, small[0:1])).astype(BF)


def last_kernel(mine, other, up_grad, x_ref, small, dx_ref, sums_ref):
    layer_input_back(mine, other, up_grad, x_ref, small, dx_ref, sums_ref)


def attn_back_kernel(
    layer, place, mine, other, dy_ref, mid_ref, small, mask_ref, p_ref, w0, w1, w2, w3, w4,
    dmid_ref, dr_ref, dp_ref, part_ref, sums_ref, held, grad_o, sem,
):
    fetch_attn(layer, place, w0, w1, w2, w3, w4, held, sem)
    grad = mine[...].astype(F32) + other[...].astype(F32)
    dy = dy_ref[...].astype(F32)
    unit, inverse = normed(mid_ref[...])
    sums_ref[0:1] = column_sum(grad * unit)
    sums_ref[1:2] = column_sum(grad)
    dmid = dy + norm_back(grad, unit, inverse, small[2:3])
    dmid_ref[...] = dmid
    sums_ref[2:3] = column_sum(dmid)
    sums_ref[3:4] = column_sum(dy)
    dr_ref[...] = dmid.astype(BF)
    wait_whole(held, sem)
    grad_o[...] = mt(dr_ref[...], held[pl.ds(1152, 384), :]).astype(BF)
    low, high = half_masks()
    for page in range(PAGES):
        rows = pl.ds(page * BLOCKS, BLOCKS)
        allowed = mask_ref[page] > 0.5
        for pair in range(3):
            q = p_ref[rows, pl.ds(pair * 128, 128)]
            k = p_ref[rows, pl.ds(384 + pair * 128, 128)]
            v = p_ref[rows, pl.ds(768 + pair * 128, 128)]
            do = grad_o[rows, pl.ds(pair * 128, 128)]
            dq = dk = dv = None
            for half in (low, high):
                kh = k * half
                scores = jnp.where(allowed, mt(kh, q) * SCALE, -1e30)
                peak = jnp.max(scores, axis=0, keepdims=True)
                expo = jnp.exp(scores - peak)
                probs = expo / jnp.sum(expo, axis=0, keepdims=True)
                dprobs = mt(v * half, do)
                inner = jnp.sum(probs * dprobs, axis=0, keepdims=True)
                dz = (probs * (dprobs - inner)).astype(BF)
                one = tm(dz, kh)
                two = mm(dz, q * half)
                three = mm(probs.astype(BF), do * half)
                dq = one if dq is None else dq + one
                dk = two if dk is None else dk + two
                dv = three if dv is None else dv + three
            dp_ref[rows, pl.ds(pair * 128, 128)] = (dq * SCALE).astype(BF)
            dp_ref[rows, pl.ds(384 + pair * 128, 128)] = (dk * SCALE).astype(BF)
            dp_ref[rows, pl.ds(768 + pair * 128, 128)] = dv.astype(BF)
    part_ref[...] = mm(dp_ref[...], held[pl.ds(0, 1152), :]).astype(BF)


def attn_grads(a_ref, dp_ref, dr_ref, o_ref, held):
    for n in range(3):
        cols = pl.ds(n * 384, 384)
        held[:, cols] = tm(a_ref[...], dp_ref[:, cols]).astype(BF)
    held[:, pl.ds(1152, 384)] = tm(dr_ref[...], o_ref[...]).astype(BF)


def attn_grads_rings_kernel(place, a_ref, dp_ref, dr_ref, o_ref, g0, g1, g2, g3, held, sem):
    attn_grads(a_ref, dp_ref, dr_ref, o_ref, held)
    send_blocks(place, held, (g0, g1, g2, g3), sem)


def attn_grads_z_kernel(place, a_ref, dp_ref, dr_ref, o_ref, near, far, later, home, held, sem):
    attn_grads(a_ref, dp_ref, dr_ref, o_ref, held)
    zz = place[5]
    top, low = pl.ds(0, 384), pl.ds(384, 384)
    for k, half, to in (
        (2, top, near.at[top]),
        (1, top, near.at[low]),
        (3, low, far.at[top]),
        (2, low, far.at[low]),
        (3, top, later.at[top]),
        (1, low, later.at[low]),
        (0, top, home.at[top]),
        (0, low, home.at[low]),
    ):
        cols = pl.ds(pl.multiple_of((zz ^ k) * 384, 128), 384)
        pltpu.make_async_copy(held.at[half, cols], to, sem).start()
    pltpu.make_async_copy(held, held, sem).wait()


def ffn_grads(c_ref, du_ref, df_ref, e_ref, held):
    for n in range(4):
        cols = pl.ds(n * 384, 384)
        held[:, cols] = tm(c_ref[...], du_ref[:, cols]).astype(BF)
    for n in range(4):
        held[:, pl.ds(1536 + n * 384, 384)] = tm(df_ref[...], e_ref[:, pl.ds(n * 384, 384)]).astype(BF)


def ffn_grads_kernel(place, c_ref, du_ref, df_ref, e_ref, g0, g1, g2, g3, held, sem):
    ffn_grads(c_ref, du_ref, df_ref, e_ref, held)
    send_blocks(place, held, (g0, g1, g2, g3), sem)


def ffn_grads_more_kernel(place, c_ref, du_ref, df_ref, e_ref, extra, g0, g1, g2, g3, held, sem):
    ffn_grads(c_ref, du_ref, df_ref, e_ref, held)
    send_blocks(place, held, (g0, g1, g2, g3), sem, extra)


def pass_on_kernel(later, plus, minus, on_plus, on_minus):
    half = later.shape[0] // 2
    on_plus[...] = (later[0:half].astype(F32) + plus[0:half].astype(F32)).astype(BF)
    on_minus[...] = (later[half:].astype(F32) + minus[half:].astype(F32)).astype(BF)


def fold_kernel(place, home, plus, minus, last_plus, last_minus, m0, m1, m2, m3, total):
    total[0:2] = (
        home[0:2].astype(F32) + minus[0:2].astype(F32) + last_plus[...].astype(F32)
    ).astype(BF)
    total[2:4] = (
        home[2:4].astype(F32) + plus[2:4].astype(F32) + last_minus[...].astype(F32)
    ).astype(BF)
    for s, out in enumerate((m0, m1, m2, m3)):
        out[...] = total[(place[2] + s) & 3]


def pack_kernel(place, *refs):
    def total(four):
        return sum(r[...].astype(F32) for r in four)

    ffn1, ffn0, attn0 = total(refs[0:4]), total(refs[4:8]), total(refs[8:12])
    outs, staged = refs[12:16], refs[16]
    zz = place[5]
    for half in range(2):
        cols = slice(half * 768, half * 768 + 768)
        later = slice(1536 + half * 768, 1536 + half * 768 + 768)
        for group in range(4):
            at = slice(group * 384 + half * 192, group * 384 + half * 192 + 192)
            staged[2 * half, :, pl.ds(group * 192, 192)] = attn0[:, at].astype(BF)
            mine = ffn0[:, 3072 + half * 192 : 3072 + half * 192 + 192]
            staged[2 * half + 1, :, pl.ds(group * 192, 192)] = jnp.where(zz == group, mine, 0.0).astype(BF)
        for layer, ffn in ((0, ffn0), (1, ffn1)):
            staged[2 * half + layer, :, pl.ds(768, 768)] = ffn[:, cols].astype(BF)
            staged[2 * half + layer, :, pl.ds(1536, 768)] = ffn[:, later].astype(BF)
    for k in range(4):
        outs[k][...] = staged[zz ^ k]


def finish_kernel(a, b, c, d, qkv_ref, out_ref, up_ref, down_ref):
    total = sum(r[...].astype(F32) for r in (a, b, c, d))
    for group in range(3):
        qkv_ref[group] = total[:, group * 192 : group * 192 + 192]
    out_ref[...] = total[:, 576:768]
    up_ref[...] = total[:, 768:1536]
    down_ref[...] = total[:, 1536:2304]


VM = pl.BlockSpec(memory_space=pltpu.VMEM)
SM = pl.BlockSpec(memory_space=pltpu.SMEM)
ANY = pl.BlockSpec(memory_space=pl.ANY)


def shape(dims, dtype):
    return jax.ShapeDtypeStruct(dims, dtype)


def call(body, ins, outs, scratch, args, flops):
    sizes = sum(a.size * a.dtype.itemsize for a in args)
    return pl.pallas_call(
        body,
        in_specs=ins,
        out_specs=tuple(spec for spec, _ in outs),
        out_shape=tuple(form for _, form in outs),
        scratch_shapes=scratch,
        compiler_params=pltpu.CompilerParams(vmem_limit_bytes=VMEM_LIMIT),
        cost_estimate=pl.CostEstimate(flops=flops, bytes_accessed=sizes, transcendentals=0),
    )(*args)


ATTN_HELD = pltpu.VMEM((1536, 768), BF)
FFN_HELD = pltpu.VMEM((2, 1536, 768), BF)
SEM = pltpu.SemaphoreType.DMA(())
ROW_BF = (VM, shape((ROWS, D), BF))
ROW_F32 = (VM, shape((ROWS, D), F32))
WIDE_BF = (VM, shape((ROWS, 1536), BF))
ATTN_OUTS = [ROW_BF, (VM, shape((ROWS, 1152), BF)), (VM, shape((ROWS, 384), BF)), ROW_BF]


def pairs_allowed(flags, valid):
    place = lax.broadcasted_iota(jnp.int32, (BLOCKS,), 0)
    visual = place >= TEXT
    dropped = (flags[:, None] == 1) & visual[None] | (flags[:, None] == 2) & ~visual[None]
    key_ok = (valid == 1) & ~dropped
    same = place[:, None] == place[None, :]
    other = visual[:, None] != visual[None, :]
    cross = same[None] | other[None] & key_ok[:, None, :]
    plain = same[None] | key_ok[:, None, :]
    masks = []
    for allowed in (cross, plain):
        allowed = allowed.astype(F32)
        masks.append((allowed, jnp.swapaxes(allowed, 1, 2)))
    return masks


def fold_rings(blocks, place):
    plus, minus, later, home = blocks
    width = plus.shape[2]
    got_plus, got_minus = ring_shift(plus, FIRST, 1), ring_shift(minus, FIRST, 3)
    half = (VM, shape((2, 48, width), BF))
    on_plus, on_minus = call(pass_on_kernel, [VM] * 3, [half] * 2, [], [later, got_plus, got_minus], 0)
    last_plus, last_minus = ring_shift(on_plus, FIRST, 1), ring_shift(on_minus, FIRST, 3)
    mine = call(
        fold_kernel, [SM] + [VM] * 5, [(VM, shape((48, width), BF))] * 4, [pltpu.VMEM((4, 48, width), BF)],
        [place, home, got_plus, got_minus, last_plus, last_minus], 0,
    )
    return [mine[0]] + [ring_shift(mine[s], SECOND, s) for s in (1, 2, 3)]


def fold_z(blocks):
    near, far, later, home = blocks
    got_near, got_far = swap_z(near, 1), swap_z(far, 3)
    half = (VM, shape((384, 384), BF))
    on_far, on_near = call(pass_on_kernel, [VM] * 3, [half] * 2, [], [later, got_near, got_far], 0)
    last_far, last_near = swap_z(on_far, 3), swap_z(on_near, 1)
    near_terms = jnp.concatenate([got_near[384:], got_far[:384]])
    last_terms = jnp.concatenate([last_far, last_near])
    return (home.astype(F32) + near_terms.astype(F32) + last_terms.astype(F32)).astype(BF)


def sum_ring(value, axes, place):
    got = jnp.stack([value] + [ring_shift(value, axes, s) for s in (1, 2, 3)])
    return sum(lax.dynamic_index_in_dim(got, (place - j) & 3, 0, keepdims=False) for j in range(4))


def on_device(
    block_input, out_cotangent, drop_flags, key_valid, qkv_weight, out_weight, up_weight, down_weight,
    hidden_bias, norm_gains, norm_shifts, out_biases,
):
    y, x = lax.axis_index("y"), lax.axis_index("x")
    pipe, zhi, core = lax.axis_index("pipe"), lax.axis_index("zhi"), lax.axis_index("core")
    zz = 2 * zhi + pipe
    i1 = jnp.where(core == 0, x, y)
    i2 = jnp.where(core == 0, y, x)
    place = jnp.stack([pipe, i1, i2, core, zhi, zz]).astype(jnp.int32)

    packed = jnp.concatenate([
        norm_gains[0, 0:1], norm_shifts[0, 0:1], norm_gains[0, 1:2], norm_shifts[0, 1:2], out_biases[0],
        hidden_bias, jnp.zeros((1, D), F32),
    ])
    terms, rest = [], packed
    for _ in range(3):
        term = lax.reduce_precision(rest, 8, 7)
        terms.append(term.astype(BF))
        rest = rest - term
    packed_low = jnp.concatenate(terms + [jnp.zeros((8, D), BF)])

    own_attn = jnp.concatenate([jnp.transpose(qkv_weight[0], (1, 2, 0)).reshape(576, D), out_weight[0]])
    own_up, own_down = up_weight[0], down_weight[0]
    number = i2 * 4 + i1
    ffn_slice = jnp.where(
        number < 8,
        lax.dynamic_slice_in_dim(own_up, (number & 7) * 96, 96),
        lax.dynamic_slice_in_dim(own_down, (number & 7) * 96, 96),
    )
    piece = jnp.concatenate([ffn_slice, packed_low])
    from_z = [piece] + [swap_z(piece, k) for k in (1, 2, 3)]
    order = jnp.where(
        pipe == 0,
        jnp.stack([from_z[k][:96] for k in (2, 1, 3)]),
        jnp.stack([from_z[k][:96] for k in (1, 3, 2)]),
    )
    level = [order] + [ring_shift(order, FIRST, 4 - d) for d in (1, 2, 3)]
    first_level = jnp.stack([jnp.stack([part[slot] for part in level]) for slot in (0, 1)])
    last_level = jnp.stack([part[2] for part in level])
    after, before = ring_shift(first_level, SECOND, 3), ring_shift(first_level, SECOND, 1)
    across = [ring_shift(before[0], SECOND, 1), ring_shift(after[1], SECOND, 3)]
    parts = [first_level, after, before, *across]
    last_level, _, _ = lax.optimization_barrier((last_level, after, before))
    after, before = ring_shift(last_level, SECOND, 3), ring_shift(last_level, SECOND, 1)
    across = [ring_shift(before[0:2], SECOND, 1), ring_shift(after[2:4], SECOND, 3)]
    more_parts = parts + [last_level, after, before, *across]

    own_attn, _ = lax.optimization_barrier((own_attn, order))
    near, far = swap_z(own_attn, 1), swap_z(own_attn, 3)
    diagonal = [swap_z(near[:384], 3), swap_z(far[384:], 1)]

    def whole(k):
        return sum(from_z[k][96 + 8 * n : 104 + 8 * n].astype(F32) for n in range(3))

    full = [whole(k) for k in range(4)]
    small, hidden = [], []
    for layer in range(2):
        same = jnp.where(pipe == layer, full[0], full[1])
        other = jnp.where(pipe == layer, full[2], full[3])
        small.append(same[:6])
        hidden.append(
            jnp.where(
                zhi == 0,
                jnp.concatenate([same[6:7], other[6:7]], axis=1),
                jnp.concatenate([other[6:7], same[6:7]], axis=1),
            )
        )

    both = jnp.stack([block_input, out_cotangent], axis=1)
    kept = lax.dynamic_index_in_dim(both, zz, 0, keepdims=False)
    came = swap_z(lax.dynamic_index_in_dim(both, zz ^ 3, 0, keepdims=False), 3)
    halves = jnp.where(zhi == 0, jnp.stack([kept, came]), jnp.stack([came, kept]))
    across = swap_cores(halves)
    rows = jnp.where(core == 0, jnp.stack([halves, across], 1), jnp.stack([across, halves], 1))
    x0 = rows[:, :, 0].reshape(ROWS, D)
    cotangent = rows[:, :, 1].reshape(ROWS, D)
    flags = lax.dynamic_index_in_dim(drop_flags, zz, 0, keepdims=False)
    valid = lax.dynamic_index_in_dim(key_valid, zz, 0, keepdims=False)
    masks = pairs_allowed(flags, valid)

    attn_args = [own_attn, near, *diagonal, far]
    ffn_args = [own_up, own_down, *parts]
    more_args = [own_up, own_down, *more_parts]
    any5, any7, any12 = [ANY] * 5, [ANY] * 7, [ANY] * 12
    unit = 2 * ROWS * D * 384

    a0, p0, o0, part = call(
        attn_first_kernel, [SM, VM, VM, VM] + any5, ATTN_OUTS, [ATTN_HELD, SEM],
        [place, x0, small[0], masks[0][0], *attn_args], 4 * unit,
    )
    mid0, c0, e0, slope0, part = call(
        ffn_first_kernel, [SM] + [VM] * 5 + any7,
        [ROW_F32, ROW_BF, WIDE_BF, (VM, shape((ROWS, 1536), F32)), ROW_BF], [FFN_HELD, SEM],
        [place, x0, part, swap_cores(part), small[0], hidden[0], *ffn_args], 8 * unit,
    )
    y0, a1, p1, o1, part = call(
        attn_second_kernel, [SM] + [VM] * 6 + any5, [ROW_BF] + ATTN_OUTS, [ATTN_HELD, SEM],
        [place, mid0, part, swap_cores(part), small[0], small[1], masks[1][0], *attn_args], 4 * unit,
    )
    hidden_sum = (VM, shape((1, 1536), F32))
    mid1, c1, e1, part, du1, back, dhidden1 = call(
        ffn_second_kernel, [SM] + [VM] * 6 + any12,
        [ROW_F32, ROW_BF, WIDE_BF, ROW_BF, WIDE_BF, ROW_BF, hidden_sum],
        [FFN_HELD, pltpu.VMEM((ROWS, 1536), F32), SEM],
        [place, y0, part, swap_cores(part), small[1], hidden[1], cotangent, *more_args], 16 * unit,
    )
    y1 = (mid1 + (part.astype(F32) + swap_cores(part).astype(F32)) + small[1][5]).astype(BF)

    def blocks(width):
        return [(ANY, shape((4, 48, width), BF))] * 4

    def attn_back(layer, back, dy, mid, projected):
        return call(
            partial(attn_back_kernel, layer), [SM] + [VM] * 7 + any5,
            [ROW_F32, ROW_BF, (VM, shape((ROWS, 1152), BF)), ROW_BF, (VM, shape((4, D), F32))],
            [ATTN_HELD, pltpu.VMEM((ROWS, 384), BF), SEM],
            [place, back, swap_cores(back), dy, mid, small[layer], masks[layer][1], projected, *attn_args],
            5 * unit,
        )

    ffn1 = call(
        ffn_grads_kernel, [SM] + [VM] * 4, blocks(3072), [pltpu.VMEM((D, 3072), BF), SEM],
        [place, c1, du1, cotangent, e1], 8 * unit,
    )
    ffn1 = fold_rings(ffn1, place)
    dmid1, dr1, dp1, back, sums1 = attn_back(1, back, cotangent, mid1, p1)
    attn1 = call(
        attn_grads_z_kernel, [SM] + [VM] * 4, [(ANY, shape((D, 384), BF))] * 4,
        [pltpu.VMEM((D, 1536), BF), SEM], [place, a1, dp1, dr1, o1], 4 * unit,
    )
    attn1 = fold_z(attn1)
    two_sums = (VM, shape((2, D), F32))
    dx1, du0, back, dhidden0, first1 = call(
        ffn_back_kernel, [SM] + [VM] * 6 + any7, [ROW_BF, WIDE_BF, ROW_BF, hidden_sum, two_sums],
        [FFN_HELD, SEM],
        [place, back, swap_cores(back), dmid1, y0, small[1], slope0, *ffn_args], 8 * unit,
    )
    ffn0 = call(
        ffn_grads_more_kernel, [SM] + [VM] * 4 + [ANY], blocks(3456), [pltpu.VMEM((D, 3072), BF), SEM],
        [place, c0, du0, dx1, e0, attn1], 8 * unit,
    )
    ffn0 = fold_rings(ffn0, place)
    dmid0, dr0, dp0, back, sums0 = attn_back(0, back, dx1, mid0, p0)
    attn0 = call(
        attn_grads_rings_kernel, [SM] + [VM] * 4, blocks(1536), [pltpu.VMEM((D, 1536), BF), SEM],
        [place, a0, dp0, dr0, o0], 4 * unit,
    )
    attn0 = fold_rings(attn0, place)
    dx0, first0 = call(
        last_kernel, [VM] * 5, [ROW_BF, two_sums], [],
        [back, swap_cores(back), dmid0, x0, small[0]], unit // 16,
    )

    packs = call(
        pack_kernel, [SM] + [VM] * 12, [(VM, shape((48, 2304), BF))] * 4, [pltpu.VMEM((4, 48, 2304), BF)],
        [place, *ffn1, *ffn0, *attn0], 0,
    )
    grad_qkv, grad_out, grad_up, grad_down = call(
        finish_kernel, [VM] * 4,
        [(VM, shape((3, 48, 192), F32)), (VM, shape((48, 192), F32))] + [(VM, shape((48, D), F32))] * 2, [],
        [packs[0]] + [swap_z(packs[k], k) for k in (1, 2, 3)], 0,
    )
    grad_qkv = jnp.transpose(grad_qkv, (1, 0, 2))
    grad_out, grad_down = grad_out.T, grad_down.T

    vec = jnp.concatenate(
        [first0, sums0, dhidden0.reshape(2, D), first1, sums1, dhidden1.reshape(2, D)]
    )
    vec = sum_ring(vec, ONLY_X, x)
    vec = sum_ring(vec, ONLY_Y, y)
    vec = vec.reshape(2, 8, D)
    got = [lax.dynamic_index_in_dim(vec, pipe, 0, keepdims=False)]
    for k in (1, 2, 3):
        got.append(swap_z(lax.dynamic_index_in_dim(vec, pipe ^ (k & 1), 0, keepdims=False), k))
    got = jnp.stack(got)
    vec = sum(lax.dynamic_index_in_dim(got, zz ^ j, 0, keepdims=False) for j in range(4))
    across = swap_cores(vec)
    low = jnp.where(core == 0, vec, across)
    high = jnp.where(core == 0, across, vec)
    grad_hidden = jnp.stack([low[6], high[6], low[7], high[7]]).reshape(1, 4 * D)
    grad_gains = jnp.concatenate([low[0:1], low[2:3]])
    grad_shifts = jnp.concatenate([low[1:2], low[3:4]])
    grad_biases = low[4:6]

    def spread(first, second):
        tall = jnp.stack([first, second]).reshape(2, 2, 2, 72, D)

        def for_chip(k):
            rows = lax.dynamic_index_in_dim(tall, pipe ^ (k & 1), 0, keepdims=False)
            rows = lax.dynamic_index_in_dim(rows, zhi ^ (k >> 1), 0, keepdims=False)
            return lax.dynamic_index_in_dim(rows, core, 0, keepdims=False)

        got = jnp.stack([for_chip(0)] + [swap_z(for_chip(k), k) for k in (1, 2, 3)])
        return jnp.stack([lax.dynamic_index_in_dim(got, zz ^ m, 0, keepdims=False) for m in range(4)])

    activations = spread(y0, y1)
    input_grads = spread(dx0, dx1)
    return (
        activations[None],
        input_grads[None],
        grad_qkv[None],
        grad_out[None],
        grad_up[None],
        grad_down[None],
        grad_hidden,
        grad_gains[None],
        grad_shifts[None],
        grad_biases[None],
    )


def solution(mesh):
    fine = Mesh(mesh.devices.reshape(4, 4, 2, 2, 2), MESH_AXES)
    rows = DP + TENSOR
    in_specs = (
        P(None, rows, None),
        P(None, rows, None),
        P(None, DP),
        P(None, DP, None),
        P("pipe", None, None, TENSOR),
        P("pipe", TENSOR, None),
        P("pipe", None, TENSOR),
        P("pipe", TENSOR, None),
        P("pipe", TENSOR),
        P("pipe", None, None),
        P("pipe", None, None),
        P("pipe", None, None),
    )
    out_specs = (
        P("pipe", None, rows, None),
        P("pipe", None, rows, None),
        P("pipe", DP, None, TENSOR),
        P("pipe", TENSOR, DP),
        P("pipe", DP, TENSOR),
        P("pipe", TENSOR, DP),
        P("pipe", None),
        P("pipe", None, None),
        P("pipe", None, None),
        P("pipe", None, None),
    )
    return jax.shard_map(on_device, mesh=fine, in_specs=in_specs, out_specs=out_specs, check_vma=False)
```

```python
from functools import partial

import jax
import jax.numpy as jnp
from jax import lax
from jax.experimental import pallas as pl
from jax.experimental.pallas import tpu as pltpu
from jax.sharding import Mesh
from jax.sharding import PartitionSpec as P

BF = jnp.bfloat16
F32 = jnp.float32
D = 768
BLOCKS = 96
TEXT = 72
ROWS = 288
PAGES = 3
SCALE = 0.125

MESH_AXES = ("y", "x", "pipe", "zhi", "core")
DP = ("y", "x")
TENSOR = ("zhi", "core")


def swap_cores(value):
    return lax.ppermute(value, "core", [(0, 1), (1, 0)])


def swap_z(value, k):
    pairs = []
    for p in range(2):
        for h in range(2):
            other = (2 * h + p) ^ k
            pairs.append((p * 2 + h, (other & 1) * 2 + (other >> 1)))
    return lax.ppermute(value, ("pipe", "zhi"), pairs)


def ring_shift(value, axis_of_core, shift):
    pairs = []
    for y in range(4):
        for x in range(4):
            for c in range(2):
                if axis_of_core[c] == "x":
                    to = (y, (x + shift) % 4)
                else:
                    to = ((y + shift) % 4, x)
                pairs.append(((y * 4 + x) * 2 + c, (to[0] * 4 + to[1]) * 2 + c))
    return lax.ppermute(value, ("y", "x", "core"), pairs)


FIRST = ("x", "y")
SECOND = ("y", "x")


def mm(a, b):
    return lax.dot_general(a, b, (((1,), (0,)), ((), ())), preferred_element_type=F32)


def mt(a, b):
    return lax.dot_general(a, b, (((1,), (1,)), ((), ())), preferred_element_type=F32)


def tm(a, b):
    return lax.dot_general(a, b, (((0,), (0,)), ((), ())), preferred_element_type=F32)


def normed(values):
    centre = values - jnp.mean(values, axis=-1, keepdims=True)
    spread = jnp.mean(centre * centre, axis=-1, keepdims=True)
    inverse = lax.rsqrt(spread + 1e-05)
    return centre * inverse, inverse


def norm_back(grad, unit, inverse, gain):
    scaled = grad * gain
    mean_one = jnp.mean(scaled, axis=-1, keepdims=True)
    mean_two = jnp.mean(scaled * unit, axis=-1, keepdims=True)
    return inverse * (scaled - mean_one - unit * mean_two)


def column_sum(values):
    return jnp.sum(values, axis=0, keepdims=True)


def half_masks():
    lane = lax.broadcasted_iota(jnp.int32, (1, 128), 1)
    low = (lane < 64).astype(F32)
    return low.astype(BF), (1.0 - low).astype(BF)


def ring_slot(d1, j2):
    if d1 == 0:
        return 3
    if d1 == 2:
        return 0 if j2 < 2 else 1
    if d1 == 1:
        return 2 if j2 < 2 else 0
    return 1 if j2 < 2 else 2


def row_of(place, d1, j2):
    step1 = jnp.where(place[3] == 0, 48, 192)
    step2 = jnp.where(place[3] == 0, 192, 48)
    return pl.multiple_of(((place[1] + d1) & 3) * step1 + j2 * step2, 16)


def send_blocks(place, total, outs):
    for d1 in range(4):
        for j2 in range(4):
            outs[ring_slot(d1, j2)][j2] = total[pl.ds(row_of(place, d1, j2), 48), :]


def send_z(place, total, near, far, later, home):
    for k in range(4):
        cols = pl.ds(pl.multiple_of((place[5] ^ k) * 384, 128), 384)
        top, low = total[pl.ds(0, 384), cols], total[pl.ds(384, 384), cols]
        if k == 0:
            home[0:384], home[384:768] = top, low
        elif k == 1:
            near[384:768], later[384:768] = top, low
        elif k == 2:
            near[0:384], far[384:768] = top, low
        else:
            later[0:384], far[0:384] = top, low


def level_kernel(place, own, one, two, three, first, last):
    for d, source in enumerate((own, one, two, three)):
        rows = pl.ds(pl.multiple_of(((place[1] + d) & 3) * 96, 16), 96)
        first[0, rows] = source[0]
        first[1, rows] = source[1]
        last[rows] = source[2]


def join_attn_kernel(layer, place, own, near, across, over, far, held):
    pipe, zhi = place[0], place[4]

    def put(group, half, value):
        held[pl.ds(pl.multiple_of(group * 384 + half * 192, 16), 192)] = value

    @pl.when(pipe == layer)
    def _():
        for group in range(4):
            put(group, zhi, own[group * 192 : group * 192 + 192])
            from_two = across if group < 2 else over
            put(group, 1 - zhi, from_two[group % 2 * 192 : group % 2 * 192 + 192])

    @pl.when(pipe != layer)
    def _():
        for group in range(4):
            put(group, zhi, near[group * 192 : group * 192 + 192])
            put(group, 1 - zhi, far[group * 192 : group * 192 + 192])


def join_ffn_kernel(layer, place, own_up, own_down, *refs):
    parts, held = refs[:-1], refs[-1]
    pipe, i2, zhi = place[0], place[2], place[4]

    def gathered(half, slot):
        for d2 in range(4):
            row = pl.multiple_of(((i2 + d2) & 3) * 384, 16)
            held[half, pl.ds(row, 384)] = parts[d2][slot] if slot < 2 else parts[4 + d2][...]

    @pl.when(pipe == layer)
    def _():
        held[zhi, 0:768] = own_up[...]
        held[zhi, 768:1536] = own_down[...]
        gathered(1 - zhi, 2 * layer)

    @pl.when(pipe != layer)
    def _():
        gathered(zhi, layer)
        gathered(1 - zhi, layer + 1)


def attn_forward_body(x, small, mask_ref, held, a_ref, p_ref, o_ref, scores_ref, probs_ref, part_ref):
    unit, _ = normed(x)
    a_ref[...] = (unit * small[0:1] + small[1:2]).astype(BF)
    p_ref[...] = mt(a_ref[...], held[pl.ds(0, 1152), :]).astype(BF)
    halves = half_masks()
    for page in range(PAGES):
        rows = pl.ds(page * BLOCKS, BLOCKS)
        for pair in range(3):
            q = p_ref[rows, pl.ds(pair * 128, 128)]
            k = p_ref[rows, pl.ds(384 + pair * 128, 128)]
            for n, half in enumerate(halves):
                scores_ref[page, pair * 2 + n] = mt(q, k * half)
    for page in range(PAGES):
        allowed = mask_ref[page] > 0.5
        for head in range(6):
            scores = jnp.where(allowed, scores_ref[page, head] * SCALE, -1e30)
            expo = jnp.exp(scores - jnp.max(scores, axis=-1, keepdims=True))
            probs_ref[page, head] = (expo * (1.0 / jnp.sum(expo, axis=-1, keepdims=True))).astype(BF)
    for page in range(PAGES):
        rows = pl.ds(page * BLOCKS, BLOCKS)
        for pair in range(3):
            v = p_ref[rows, pl.ds(768 + pair * 128, 128)]
            total = mm(probs_ref[page, pair * 2], v * halves[0]) + mm(probs_ref[page, pair * 2 + 1], v * halves[1])
            o_ref[rows, pl.ds(pair * 128, 128)] = total.astype(BF)
    part_ref[...] = mm(o_ref[...], held[pl.ds(1152, 384), :]).astype(BF)


def attn_first_kernel(
    x_ref, small, mask_ref, held, p_ref, part_ref, a_ref, o_ref, scores_ref, probs_ref
):
    attn_forward_body(
        x_ref[...].astype(F32), small, mask_ref, held, a_ref, p_ref, o_ref, scores_ref, probs_ref, part_ref,
    )


def attn_second_kernel(
    mid_ref, mine, other, before, small, mask_ref, held,
    y_ref, p_ref, part_ref, a_ref, o_ref, scores_ref, probs_ref,
):
    total = mine[...].astype(F32) + other[...].astype(F32)
    y_ref[...] = (mid_ref[...] + total + before[5:6]).astype(BF)
    attn_forward_body(
        y_ref[...].astype(F32), small, mask_ref, held, a_ref, p_ref, o_ref, scores_ref, probs_ref, part_ref,
    )


def middle(x_ref, mine, other, small, mid_ref, c_ref):
    mid = x_ref[...].astype(F32) + (mine[...].astype(F32) + other[...].astype(F32)) + small[4:5]
    mid_ref[...] = mid
    unit, _ = normed(mid)
    c_ref[...] = (unit * small[2:3] + small[3:4]).astype(BF)


def gelu_parts(pre):
    cdf = 0.5 * (1.0 + lax.erf(pre * 0.7071067811865476))
    return pre * cdf, cdf + pre * (jnp.exp(-0.5 * pre * pre) * 0.3989422804014327)


def down_product(e_ref, held, part_ref):
    part_ref[...] = (
        mm(e_ref[:, pl.ds(0, 768)], held[0, pl.ds(768, 768), :])
        + mm(e_ref[:, pl.ds(768, 768)], held[1, pl.ds(768, 768), :])
    ).astype(BF)


def up_tile(n, c_ref, held, hidden):
    return mm(c_ref[...], held[n // 3, pl.ds(0, 768), pl.ds(n % 3 * 256, 256)]) + hidden[:, pl.ds(n * 256, 256)]


def ffn_first_kernel(
    x_ref, mine, other, small, hidden, held, mid_ref, pre_ref, part_ref, c_ref, e_ref
):
    middle(x_ref, mine, other, small, mid_ref, c_ref)
    for n in range(6):
        wide = pl.ds(n * 256, 256)
        pre = up_tile(n, c_ref, held, hidden)
        pre_ref[:, wide] = pre
        e_ref[:, wide] = (0.5 * pre * (1.0 + lax.erf(pre * 0.7071067811865476))).astype(BF)
    down_product(e_ref, held, part_ref)


def ffn_back_tile(n, grad, slope, held, du_ref, hidden_ref):
    wide = pl.ds(n * 256, 256)
    grad_e = mt(grad, held[n // 3, pl.ds(768 + n % 3 * 256, 256), :])
    grad_u = (grad_e * slope).astype(BF)
    du_ref[:, wide] = grad_u
    hidden_ref[:, wide] = column_sum(grad_u.astype(F32))


def ffn_back_rest(place, grad_ref, c_ref, e_ref, du_ref, held, back_ref, outs, total):
    back_ref[...] = (
        mt(du_ref[:, pl.ds(0, 768)], held[0, pl.ds(0, 768), :])
        + mt(du_ref[:, pl.ds(768, 768)], held[1, pl.ds(0, 768), :])
    ).astype(BF)
    turned = c_ref[...].T
    for n in range(6):
        wide = pl.ds(n * 256, 256)
        total[:, wide] = mm(turned, du_ref[:, wide]).astype(BF)
    turned = grad_ref[...].T
    for n in range(6):
        total[:, pl.ds(1536 + n * 256, 256)] = mm(turned, e_ref[:, pl.ds(n * 256, 256)]).astype(BF)
    send_blocks(place, total, outs)


def ffn_second_kernel(
    place, x_ref, mine, other, small, hidden, grad_ref, held,
    mid_ref, part_ref, back_ref, hidden_ref, g0, g1, g2, g3, c_ref, e_ref, slope_ref, du_ref, total,
):
    middle(x_ref, mine, other, small, mid_ref, c_ref)
    for n in range(6):
        wide = pl.ds(n * 256, 256)
        value, slope_ref[:, wide] = gelu_parts(up_tile(n, c_ref, held, hidden))
        e_ref[:, wide] = value.astype(BF)
    down_product(e_ref, held, part_ref)
    for n in range(6):
        ffn_back_tile(n, grad_ref[...], slope_ref[:, pl.ds(n * 256, 256)], held, du_ref, hidden_ref)
    ffn_back_rest(place, grad_ref, c_ref, e_ref, du_ref, held, back_ref, (g0, g1, g2, g3), total)


def layer_input_back(mine, other, up_grad, x_ref, small, dx_ref, sums_ref):
    grad = mine[...].astype(F32) + other[...].astype(F32)
    unit, inverse = normed(x_ref[...].astype(F32))
    sums_ref[0:1] = column_sum(grad * unit)
    sums_ref[1:2] = column_sum(grad)
    dx_ref[...] = (up_grad[...] + norm_back(grad, unit, inverse, small[0:1])).astype(BF)


def ffn_back_kernel(
    place, mine, other, up_grad, x_ref, small, below, mid_ref, pre_ref, held,
    dx_ref, back_ref, hidden_ref, sums_ref, g0, g1, g2, g3, c_ref, e_ref, du_ref, total,
):
    layer_input_back(mine, other, up_grad, x_ref, small, dx_ref, sums_ref)
    unit, _ = normed(mid_ref[...])
    c_ref[...] = (unit * below[2:3] + below[3:4]).astype(BF)
    for n in range(6):
        wide = pl.ds(n * 256, 256)
        value, slope = gelu_parts(pre_ref[:, wide])
        e_ref[:, wide] = value.astype(BF)
        ffn_back_tile(n, dx_ref[...], slope, held, du_ref, hidden_ref)
    ffn_back_rest(place, dx_ref, c_ref, e_ref, du_ref, held, back_ref, (g0, g1, g2, g3), total)


def last_kernel(mine, other, up_grad, x_ref, small, dx_ref, sums_ref):
    layer_input_back(mine, other, up_grad, x_ref, small, dx_ref, sums_ref)


def attn_back_kernel(layer, place, *refs):
    if layer == 1:
        end_mine, end_other, y_ref = refs[0], refs[1], refs[11]
        refs = refs[2:11] + refs[12:]
    (mine, other, dy_ref, mid_ref, small, mask_ref, p_ref, x_ref, held,
     dmid_ref, part_ref, sums_ref, near, far, later, home,
     a_ref, dr_ref, do_ref, dp_ref, o_ref, scores, dprobs, probs, dscores, total) = refs
    if layer == 1:
        y_ref[...] = (
            mid_ref[...] + (end_mine[...].astype(F32) + end_other[...].astype(F32)) + small[5:6]
        ).astype(BF)
    grad = mine[...].astype(F32) + other[...].astype(F32)
    dy = dy_ref[...].astype(F32)
    unit, inverse = normed(mid_ref[...])
    sums_ref[0:1] = column_sum(grad * unit)
    sums_ref[1:2] = column_sum(grad)
    dmid = dy + norm_back(grad, unit, inverse, small[2:3])
    dmid_ref[...] = dmid
    sums_ref[2:3] = column_sum(dmid)
    sums_ref[3:4] = column_sum(dy)
    dr_ref[...] = dmid.astype(BF)
    unit, _ = normed(x_ref[...].astype(F32))
    a_ref[...] = (unit * small[0:1] + small[1:2]).astype(BF)
    do_ref[...] = mt(dr_ref[...], held[pl.ds(1152, 384), :]).astype(BF)
    halves = half_masks()
    for page in range(PAGES):
        rows = pl.ds(page * BLOCKS, BLOCKS)
        for pair in range(3):
            q = p_ref[rows, pl.ds(pair * 128, 128)]
            k = p_ref[rows, pl.ds(384 + pair * 128, 128)]
            v = p_ref[rows, pl.ds(768 + pair * 128, 128)]
            do = do_ref[rows, pl.ds(pair * 128, 128)]
            for n, half in enumerate(halves):
                scores[page, pair * 2 + n] = mt(k * half, q)
                dprobs[page, pair * 2 + n] = mt(v * half, do)
    for page in range(PAGES):
        allowed = mask_ref[page] > 0.5
        for head in range(6):
            masked = jnp.where(allowed, scores[page, head] * SCALE, -1e30)
            expo = jnp.exp(masked - jnp.max(masked, axis=0, keepdims=True))
            share = expo * (1.0 / jnp.sum(expo, axis=0, keepdims=True))
            slope = dprobs[page, head]
            inner = jnp.sum(share * slope, axis=0, keepdims=True)
            probs[page, head] = share.astype(BF)
            dscores[page, head] = (share * (slope - inner)).astype(BF)
    for page in range(PAGES):
        rows = pl.ds(page * BLOCKS, BLOCKS)
        for pair in range(3):
            q = p_ref[rows, pl.ds(pair * 128, 128)]
            k = p_ref[rows, pl.ds(384 + pair * 128, 128)]
            v = p_ref[rows, pl.ds(768 + pair * 128, 128)]
            do = do_ref[rows, pl.ds(pair * 128, 128)]

            def both(product, left, right):
                one = product(left[page, pair * 2], right * halves[0])
                return one + product(left[page, pair * 2 + 1], right * halves[1])

            dp_ref[rows, pl.ds(pair * 128, 128)] = (both(tm, dscores, k) * SCALE).astype(BF)
            dp_ref[rows, pl.ds(384 + pair * 128, 128)] = (both(mm, dscores, q) * SCALE).astype(BF)
            dp_ref[rows, pl.ds(768 + pair * 128, 128)] = both(mm, probs, do).astype(BF)
            o_ref[rows, pl.ds(pair * 128, 128)] = both(tm, probs, v).astype(BF)
    part_ref[...] = mm(dp_ref[...], held[pl.ds(0, 1152), :]).astype(BF)
    turned = a_ref[...].T
    for n in range(3):
        cols = pl.ds(n * 384, 384)
        total[:, cols] = mm(turned, dp_ref[:, cols]).astype(BF)
    total[:, pl.ds(1152, 384)] = mm(dr_ref[...].T, o_ref[...]).astype(BF)
    send_z(place, total, near, far, later, home)


def added(left, right):
    return (left.astype(F32) + right.astype(F32)).astype(BF)


def pass_on_kernel(later, plus, minus, on_plus, on_minus):
    half = later.shape[0] // 2
    on_plus[...] = added(later[0:half], plus[0:half])
    on_minus[...] = added(later[half:], minus[half : 2 * half])


def join_kernel(plus, minus, later, got_plus, got_minus, out_plus, out_minus):
    size, half = plus.shape[0], plus.shape[0] // 2
    out_plus[0:size] = plus[...]
    out_minus[0:size] = minus[...]
    out_plus[size : size + half] = added(later[0:half], got_plus[0:half])
    out_minus[size : size + half] = added(later[half:], got_minus[half:size])


def join_z_kernel(near, far, later, got_near, got_far, out_near, out_far):
    out_near[0:768] = near[...]
    out_far[0:768] = far[...]
    out_far[768:1152] = added(later[0:384], got_near[0:384])
    out_near[768:1152] = added(later[384:768], got_far[384:768])


def fold_kernel(place, home1, plus1, minus1, home0, plus0, minus0, last_plus, last_minus, m0, m1, m2, m3, total):
    total[1, 0:2] = (home1[0:2].astype(F32) + minus1[0:2].astype(F32) + plus0[4:6].astype(F32)).astype(BF)
    total[1, 2:4] = (home1[2:4].astype(F32) + plus1[2:4].astype(F32) + minus0[4:6].astype(F32)).astype(BF)
    total[0, 0:2] = (home0[0:2].astype(F32) + minus0[0:2].astype(F32) + last_plus[...].astype(F32)).astype(BF)
    total[0, 2:4] = (home0[2:4].astype(F32) + plus0[2:4].astype(F32) + last_minus[...].astype(F32)).astype(BF)
    for s, out in enumerate((m0, m1, m2, m3)):
        for layer in range(2):
            out[layer] = total[layer, (place[2] + s) & 3]


def put_split(out, first, value):
    count = value.shape[0]
    high = value.astype(BF)
    out[first : first + count] = high
    out[first + count : first + 2 * count] = (value - high.astype(F32)).astype(BF)


def get_split(ref, first, count):
    return ref[first : first + count].astype(F32) + ref[first + count : first + 2 * count].astype(F32)


def fold_z_kernel(place, *refs):
    home1, near1, far1, home0, near0, far0, last_far, last_near = refs[0:8]
    first0, sums0, hidden0, first1, sums1, hidden1 = refs[8:14]
    outs, total, vec = refs[14:18], refs[18], refs[19]

    def three(a, b, c):
        return (a.astype(F32) + b.astype(F32) + c.astype(F32)).astype(BF)

    total[0:384, 384:768] = three(home1[0:384], near1[384:768], far0[768:1152])
    total[384:768, 384:768] = three(home1[384:768], far1[0:384], near0[768:1152])
    total[0:384, 0:384] = three(home0[0:384], near0[384:768], last_far[...])
    total[384:768, 0:384] = three(home0[384:768], far0[0:384], last_near[...])
    for n, part in enumerate((first0, sums0, None, first1, sums1)):
        if part is not None:
            at = (0, 2, 0, 8, 10)[n]
            vec[at : at + part.shape[0]] = part[...]
    for n, part in enumerate((hidden0, hidden1)):
        vec[8 * n + 6 : 8 * n + 7] = part[:, 0:768]
        vec[8 * n + 7 : 8 * n + 8] = part[:, 768:1536]
    for d1 in range(4):
        for j2 in range(4):
            outs[d1][j2 * 48 : j2 * 48 + 48] = total[pl.ds(row_of(place, d1, j2), 48)]
        put_split(outs[d1], 192, vec[...])


def turn_kernel(place, own, one, two, three, m0, m1, m2, m3, total, vecs):
    got = (own, one, two, three)
    total[...] = sum(r[0:192].astype(F32) for r in got).astype(BF)
    for s, r in enumerate(got):
        vecs[(place[1] - s) & 3] = get_split(r, 192, 16)
    vec = (vecs[0] + vecs[1]) + (vecs[2] + vecs[3])
    for s, out in enumerate((m0, m1, m2, m3)):
        row = pl.multiple_of(((place[2] + s) & 3) * 48, 16)
        out[0:48] = total[pl.ds(row, 48)]
        put_split(out, 48, vec)


def pack_kernel(place, *refs):
    def total(four, rows):
        return sum(r[0:rows].astype(F32) for r in four)

    got = refs[4:8]
    ffn0, ffn1, attn = [sum(r[layer].astype(F32) for r in refs[0:4]) for layer in range(2)] + [total(got, 48)]
    outs, staged, vecs = refs[8:12], refs[12], refs[13]
    for s, r in enumerate(got):
        vecs[(place[2] - s) & 3] = get_split(r, 48, 16)
    vec = (vecs[0] + vecs[1]) + (vecs[2] + vecs[3])
    zz = place[5]
    for half in range(2):
        for layer, ffn in ((0, ffn0), (1, ffn1)):
            to = staged.at[2 * half + layer]
            at = layer * 384 + half * 192
            for group in range(4):
                to[0:48, pl.ds(group * 192, 192)] = jnp.where(zz == group, attn[:, at : at + 192], 0.0).astype(BF)
            to[48:96] = ffn[:, half * 768 : half * 768 + 768].astype(BF)
            to[96:144] = ffn[:, 1536 + half * 768 : 1536 + half * 768 + 768].astype(BF)
            put_split(to, 144, vec[8 * layer : 8 * layer + 8])
    for k in range(4):
        outs[k][...] = staged[zz ^ k]


def finish_kernel(place, a, b, c, d, qkv_ref, out_ref, up_ref, down_ref, vec_ref, vecs):
    got = (a, b, c, d)
    total = sum(r[0:144].astype(F32) for r in got)
    for group in range(3):
        qkv_ref[group] = total[0:48, group * 192 : group * 192 + 192]
    out_ref[...] = total[0:48, 576:768]
    up_ref[...] = total[48:96]
    down_ref[...] = total[96:144]
    for k, r in enumerate(got):
        vecs[place[5] ^ k] = get_split(r, 144, 8)
    vec_ref[...] = (vecs[0] + vecs[1]) + (vecs[2] + vecs[3])


VM = pl.BlockSpec(memory_space=pltpu.VMEM)
SM = pl.BlockSpec(memory_space=pltpu.SMEM)
ANY = pl.BlockSpec(memory_space=pl.ANY)


def shape(dims, dtype):
    return jax.ShapeDtypeStruct(dims, dtype)


def call(body, ins, outs, scratch, args, limit=16, after=()):
    count, extra = len(args), len(after)
    if extra:
        inner = body

        def body(*refs):
            return inner(*refs[:count], *refs[count + extra :])

        ins, args = ins + [ANY] * extra, [*args, *after]
    return pl.pallas_call(
        body,
        in_specs=ins,
        out_specs=tuple(spec for spec, _ in outs),
        out_shape=tuple(form for _, form in outs),
        scratch_shapes=scratch,
        compiler_params=pltpu.CompilerParams(vmem_limit_bytes=limit * 1024 * 1024),
        cost_estimate=pl.CostEstimate(flops=1024, bytes_accessed=1024, transcendentals=0),
    )(*args)


ROW_BF = (VM, shape((ROWS, D), BF))
ROW_F32 = (VM, shape((ROWS, D), F32))


def pairs_allowed(flags, valid):
    place = lax.broadcasted_iota(jnp.int32, (BLOCKS,), 0)
    visual = place >= TEXT
    dropped = (flags[:, None] == 1) & visual[None] | (flags[:, None] == 2) & ~visual[None]
    key_ok = (valid == 1) & ~dropped
    same = place[:, None] == place[None, :]
    other = visual[:, None] != visual[None, :]
    cross = same[None] | other[None] & key_ok[:, None, :]
    plain = same[None] | key_ok[:, None, :]
    masks = []
    for allowed in (cross, plain):
        allowed = allowed.astype(F32)
        masks.append((allowed, jnp.swapaxes(allowed, 1, 2)))
    return masks


def on_device(
    block_input, out_cotangent, drop_flags, key_valid, qkv_weight, out_weight, up_weight, down_weight,
    hidden_bias, norm_gains, norm_shifts, out_biases,
):
    y, x = lax.axis_index("y"), lax.axis_index("x")
    pipe, zhi, core = lax.axis_index("pipe"), lax.axis_index("zhi"), lax.axis_index("core")
    zz = 2 * zhi + pipe
    i1 = jnp.where(core == 0, x, y)
    i2 = jnp.where(core == 0, y, x)
    place = jnp.stack([pipe, i1, i2, core, zhi, zz]).astype(jnp.int32)

    packed = jnp.concatenate([
        norm_gains[0, 0:1], norm_shifts[0, 0:1], norm_gains[0, 1:2], norm_shifts[0, 1:2], out_biases[0],
        hidden_bias, jnp.zeros((1, D), F32),
    ])
    terms, rest = [], packed
    for _ in range(3):
        term = lax.reduce_precision(rest, 8, 7)
        terms.append(term.astype(BF))
        rest = rest - term
    packed_low = jnp.concatenate(terms)

    own_attn = jnp.concatenate([jnp.transpose(qkv_weight[0], (1, 2, 0)).reshape(576, D), out_weight[0]])
    own_up, own_down = up_weight[0], down_weight[0]
    number = i2 * 4 + i1
    ffn_slice = jnp.where(
        number < 8,
        lax.dynamic_slice_in_dim(own_up, (number & 7) * 96, 96),
        lax.dynamic_slice_in_dim(own_down, (number & 7) * 96, 96),
    )
    piece = jnp.concatenate([ffn_slice, packed_low])
    from_z = [piece] + [swap_z(piece, k) for k in (1, 2, 3)]
    order = jnp.where(
        pipe == 0,
        jnp.stack([from_z[k][:96] for k in (2, 1, 3)]),
        jnp.stack([from_z[k][:96] for k in (1, 3, 2)]),
    )
    level = [order] + [ring_shift(order, FIRST, 4 - d) for d in (1, 2, 3)]
    first_level, last_level = call(
        level_kernel, [SM] + [VM] * 4, [(VM, shape((2, 384, D), BF)), (VM, shape((384, D), BF))], [],
        [place, *level],
    )
    parts = [first_level] + [ring_shift(first_level, SECOND, 4 - d) for d in (1, 2, 3)]
    last_level, *_ = lax.optimization_barrier((last_level, *parts[1:]))
    more_parts = parts + [last_level] + [ring_shift(last_level, SECOND, 4 - d) for d in (1, 2, 3)]

    own_attn, _ = lax.optimization_barrier((own_attn, order))
    near, far = swap_z(own_attn, 1), swap_z(own_attn, 3)
    diagonal = [swap_z(near[:384], 3), swap_z(far[384:], 1)]

    def whole(k):
        return sum(from_z[k][96 + 8 * n : 104 + 8 * n].astype(F32) for n in range(3))

    full = [whole(k) for k in range(4)]
    small, hidden = [], []
    for layer in range(2):
        same = jnp.where(pipe == layer, full[0], full[1])
        other = jnp.where(pipe == layer, full[2], full[3])
        small.append(same[:6])
        hidden.append(
            jnp.where(
                zhi == 0,
                jnp.concatenate([same[6:7], other[6:7]], axis=1),
                jnp.concatenate([other[6:7], same[6:7]], axis=1),
            )
        )

    both = jnp.stack([block_input, out_cotangent], axis=1)
    kept = lax.dynamic_index_in_dim(both, zz, 0, keepdims=False)
    came = swap_z(lax.dynamic_index_in_dim(both, zz ^ 3, 0, keepdims=False), 3)
    halves = jnp.where(zhi == 0, jnp.stack([kept, came]), jnp.stack([came, kept]))
    across = swap_cores(halves)
    rows = jnp.where(core == 0, jnp.stack([halves, across], 1), jnp.stack([across, halves], 1))
    x0 = rows[:, :, 0].reshape(ROWS, D)
    cotangent = rows[:, :, 1].reshape(ROWS, D)
    flags = lax.dynamic_index_in_dim(drop_flags, zz, 0, keepdims=False)
    valid = lax.dynamic_index_in_dim(key_valid, zz, 0, keepdims=False)
    masks = pairs_allowed(flags, valid)

    attn_whole, ffn_whole = (VM, shape((1536, D), BF)), (VM, shape((2, 1536, D), BF))

    def join_attn(layer):
        (held,) = call(
            partial(join_attn_kernel, layer), [SM] + [VM] * 5, [attn_whole], [],
            [place, own_attn, near, *diagonal, far],
        )
        return held

    def join_ffn(layer, sources, after=()):
        (held,) = call(
            partial(join_ffn_kernel, layer), [SM] + [VM] * (2 + len(sources)), [ffn_whole], [],
            [place, own_up, own_down, *sources], after=after,
        )
        return held

    projected = (VM, shape((ROWS, 1152), BF))
    row_scratch = pltpu.VMEM((ROWS, D), BF)
    head_scratch = pltpu.VMEM((ROWS, 384), BF)
    wide_scratch = pltpu.VMEM((ROWS, 1536), BF)
    scores, probs = pltpu.VMEM((PAGES, 6, BLOCKS, BLOCKS), F32), pltpu.VMEM((PAGES, 6, BLOCKS, BLOCKS), BF)
    attn_scratch = [row_scratch, head_scratch, scores, probs]
    attn_held0, attn_held1 = join_attn(0), join_attn(1)
    p0, part = call(
        attn_first_kernel, [VM] * 4, [projected, ROW_BF], attn_scratch, [x0, small[0], masks[0][0], attn_held0]
    )
    ffn_held0 = join_ffn(0, parts)
    mid0, pre0, part = call(
        ffn_first_kernel, [VM] * 6, [ROW_F32, (VM, shape((ROWS, 1536), F32)), ROW_BF], [row_scratch, wide_scratch],
        [x0, part, swap_cores(part), small[0], hidden[0], ffn_held0],
    )
    y0, p1, part = call(
        attn_second_kernel, [VM] * 7, [ROW_BF, projected, ROW_BF], attn_scratch,
        [mid0, part, swap_cores(part), small[0], small[1], masks[1][0], attn_held1],
    )
    ffn_held1 = join_ffn(1, more_parts, [part])

    hidden_sum = (VM, shape((1, 1536), F32))
    two_sums = (VM, shape((2, D), F32))
    ring_blocks = [(VM, shape((4, 48, 3072), BF))] * 4
    z_blocks = [(VM, shape((D, 384), BF))] * 4
    ffn_total = pltpu.VMEM((D, 3072), BF)
    mid1, part, back, dhidden1, *ffn1 = call(
        ffn_second_kernel, [SM] + [VM] * 7, [ROW_F32, ROW_BF, ROW_BF, hidden_sum] + ring_blocks,
        [row_scratch, wide_scratch, pltpu.VMEM((ROWS, 1536), F32), wide_scratch, ffn_total],
        [place, y0, part, swap_cores(part), small[1], hidden[1], cotangent, ffn_held1], 20,
    )
    plus1, minus1, later1, home1 = ffn1
    plus1, minus1 = ring_shift(plus1, FIRST, 1), ring_shift(minus1, FIRST, 3)

    back_scratch = [
        row_scratch, row_scratch, head_scratch, pltpu.VMEM((ROWS, 1152), BF), head_scratch,
        scores, scores, probs, probs, pltpu.VMEM((D, 1536), BF),
    ]
    back_outs = [ROW_F32, ROW_BF, (VM, shape((4, D), F32))] + z_blocks
    y1, dmid1, back, sums1, near1, far1, later_z1, home_z1 = call(
        partial(attn_back_kernel, 1), [SM] + [VM] * 11, [ROW_BF] + back_outs, back_scratch,
        [place, part, swap_cores(part), back, swap_cores(back), cotangent, mid1, small[1], masks[1][1], p1, y0,
         attn_held1],
    )
    near1, far1 = swap_z(near1, 1), swap_z(far1, 3)
    dx1, back, dhidden0, first1, plus0, minus0, later0, home0 = call(
        ffn_back_kernel, [SM] + [VM] * 9, [ROW_BF, ROW_BF, hidden_sum, two_sums] + ring_blocks,
        [row_scratch, wide_scratch, wide_scratch, ffn_total],
        [place, back, swap_cores(back), dmid1, y0, small[1], small[0], mid0, pre0, ffn_held0], 20,
    )
    six = [(VM, shape((6, 48, 3072), BF))] * 2
    plus0, minus0 = call(join_kernel, [VM] * 5, six, [], [plus0, minus0, later1, plus1, minus1], 20)
    token = plus0
    plus0, minus0 = ring_shift(plus0, FIRST, 1), ring_shift(minus0, FIRST, 3)
    dmid0, back, sums0, near0, far0, later_z0, home_z0 = call(
        partial(attn_back_kernel, 0), [SM] + [VM] * 9, back_outs, back_scratch,
        [place, back, swap_cores(back), dx1, mid0, small[0], masks[0][1], p0, x0, attn_held0], after=[token],
    )
    tall = [(VM, shape((1152, 384), BF))] * 2
    near0, far0 = call(join_z_kernel, [VM] * 5, tall, [], [near0, far0, later_z1, near1, far1])
    token = near0
    near0, far0 = swap_z(near0, 1), swap_z(far0, 3)
    dx0, first0 = call(
        last_kernel, [VM] * 5, [ROW_BF, two_sums], [],
        [back, swap_cores(back), dmid0, x0, small[0]], after=[token],
    )

    pair = [(VM, shape((2, 48, 3072), BF))]
    on_plus, on_minus = call(pass_on_kernel, [VM] * 3, pair * 2, [], [later0, plus0, minus0], after=[first0])
    last_plus, last_minus = ring_shift(on_plus, FIRST, 1), ring_shift(on_minus, FIRST, 3)
    half = [(VM, shape((384, 384), BF))]
    on_far, on_near = call(pass_on_kernel, [VM] * 3, half * 2, [], [later_z0, near0, far0], after=[on_plus])
    last_far, last_near = swap_z(on_far, 3), swap_z(on_near, 1)
    ffn = call(
        fold_kernel, [SM] + [VM] * 8, pair * 4, [pltpu.VMEM((2, 4, 48, 3072), BF)],
        [place, home1, plus1, minus1, home0, plus0, minus0, last_plus, last_minus], after=[on_far],
    )
    token = ffn[0]
    ffn = [ffn[0]] + [ring_shift(ffn[s], SECOND, s) for s in (1, 2, 3)]
    turned = call(
        fold_z_kernel, [SM] + [VM] * 14, [(VM, shape((224, D), BF))] * 4,
        [pltpu.VMEM((D, D), BF), pltpu.VMEM((16, D), F32)],
        [place, home_z1, near1, far1, home_z0, near0, far0, last_far, last_near,
         first0, sums0, dhidden0, first1, sums1, dhidden1], after=[token],
    )
    token = turned[0]
    turned = call(
        turn_kernel, [SM] + [VM] * 4, [(VM, shape((80, D), BF))] * 4,
        [pltpu.VMEM((192, D), BF), pltpu.VMEM((4, 16, D), F32)],
        [place, turned[0]] + [ring_shift(turned[s], FIRST, s) for s in (1, 2, 3)],
    )
    turned = [turned[0]] + [ring_shift(turned[s], SECOND, s) for s in (1, 2, 3)]
    packs = call(
        pack_kernel, [SM] + [VM] * 8, [(VM, shape((160, D), BF))] * 4,
        [pltpu.VMEM((4, 160, D), BF), pltpu.VMEM((4, 16, D), F32)], [place, *ffn, *turned],
    )
    grad_qkv, grad_out, grad_up, grad_down, vec = call(
        finish_kernel, [SM] + [VM] * 4,
        [(VM, shape((3, 48, 192), F32)), (VM, shape((48, 192), F32))] + [(VM, shape((48, D), F32))] * 2
        + [(VM, shape((8, D), F32))], [pltpu.VMEM((4, 8, D), F32)],
        [place, packs[0]] + [swap_z(packs[k], k) for k in (1, 2, 3)],
    )
    grad_qkv = jnp.transpose(grad_qkv, (1, 0, 2))
    grad_out, grad_down = grad_out.T, grad_down.T
    across = swap_cores(vec)
    low = jnp.where(core == 0, vec, across)
    high = jnp.where(core == 0, across, vec)
    grad_hidden = jnp.stack([low[6], high[6], low[7], high[7]]).reshape(1, 4 * D)
    grad_gains = jnp.concatenate([low[0:1], low[2:3]])
    grad_shifts = jnp.concatenate([low[1:2], low[3:4]])
    grad_biases = low[4:6]

    rows, _ = lax.optimization_barrier((jnp.stack([jnp.stack([y0, y1]), jnp.stack([dx0, dx1])]), token))
    rows = rows.reshape(2, 2, 2, 2, 72, D)

    def for_chip(k):
        mine = lax.dynamic_index_in_dim(rows, pipe ^ (k & 1), 1, keepdims=False)
        mine = lax.dynamic_index_in_dim(mine, zhi ^ (k >> 1), 1, keepdims=False)
        return lax.dynamic_index_in_dim(mine, core, 1, keepdims=False)

    got = jnp.stack([for_chip(0)] + [swap_z(for_chip(k), k) for k in (1, 2, 3)])
    got = jnp.stack([lax.dynamic_index_in_dim(got, zz ^ m, 0, keepdims=False) for m in range(4)], axis=1)
    activations, input_grads = got[0], got[1]
    return (
        activations[None],
        input_grads[None],
        grad_qkv[None],
        grad_out[None],
        grad_up[None],
        grad_down[None],
        grad_hidden,
        grad_gains[None],
        grad_shifts[None],
        grad_biases[None],
    )


def solution(mesh):
    fine = Mesh(mesh.devices.reshape(4, 4, 2, 2, 2), MESH_AXES)
    rows = DP + TENSOR
    in_specs = (
        P(None, rows, None),
        P(None, rows, None),
        P(None, DP),
        P(None, DP, None),
        P("pipe", None, None, TENSOR),
        P("pipe", TENSOR, None),
        P("pipe", None, TENSOR),
        P("pipe", TENSOR, None),
        P("pipe", TENSOR),
        P("pipe", None, None),
        P("pipe", None, None),
        P("pipe", None, None),
    )
    out_specs = (
        P("pipe", None, rows, None),
        P("pipe", None, rows, None),
        P("pipe", DP, None, TENSOR),
        P("pipe", TENSOR, DP),
        P("pipe", DP, TENSOR),
        P("pipe", TENSOR, DP),
        P("pipe", None),
        P("pipe", None, None),
        P("pipe", None, None),
        P("pipe", None, None),
    )
    return jax.shard_map(on_device, mesh=fine, in_specs=in_specs, out_specs=out_specs, check_vma=False)
```

```python
from functools import partial

import jax
import jax.numpy as jnp
from jax import lax
from jax.experimental import pallas as pl
from jax.experimental.pallas import tpu as pltpu
from jax.sharding import Mesh
from jax.sharding import PartitionSpec as P

BF = jnp.bfloat16
F32 = jnp.float32
D = 768
BLOCKS = 96
TEXT = 72
ROWS = 288
PAGES = 3
SCALE = 0.125
FACTOR = 3.0
COSTS = {'fold_kernel': 0.7, 'turn_kernel': 0.7, 'pack_kernel': 0.7, 'last_kernel': 0.7, 'join_kernel': 0.7, 'join_ffn_kernel': 0.7, 'level_kernel': 0.7, 'ffn_first_kernel': 2.3, 'attn_second_kernel': 2.4, 'ffn_second_kernel': 3.8, 'ffn_grads_kernel': 3.5, 'attn_back_kernel': 3.7, 'attn_grads_kernel': 2.4, 'ffn_back_kernel': 3.0}

MESH_AXES = ("y", "x", "pipe", "zhi", "core")
DP = ("y", "x")
TENSOR = ("zhi", "core")


def swap_cores(value):
    return lax.ppermute(value, "core", [(0, 1), (1, 0)])


def swap_z(value, k):
    pairs = []
    for p in range(2):
        for h in range(2):
            other = (2 * h + p) ^ k
            pairs.append((p * 2 + h, (other & 1) * 2 + (other >> 1)))
    return lax.ppermute(value, ("pipe", "zhi"), pairs)


def ring_shift(value, axis_of_core, shift):
    pairs = []
    for y in range(4):
        for x in range(4):
            for c in range(2):
                if axis_of_core[c] == "x":
                    to = (y, (x + shift) % 4)
                else:
                    to = ((y + shift) % 4, x)
                pairs.append(((y * 4 + x) * 2 + c, (to[0] * 4 + to[1]) * 2 + c))
    return lax.ppermute(value, ("y", "x", "core"), pairs)


FIRST = ("x", "y")
SECOND = ("y", "x")


def mm(a, b):
    return lax.dot_general(a, b, (((1,), (0,)), ((), ())), preferred_element_type=F32)


def mt(a, b):
    return lax.dot_general(a, b, (((1,), (1,)), ((), ())), preferred_element_type=F32)


def tm(a, b):
    return lax.dot_general(a, b, (((0,), (0,)), ((), ())), preferred_element_type=F32)


def normed(values):
    centre = values - jnp.mean(values, axis=-1, keepdims=True)
    spread = jnp.mean(centre * centre, axis=-1, keepdims=True)
    inverse = lax.rsqrt(spread + 1e-05)
    return centre * inverse, inverse


def norm_back(grad, unit, inverse, gain):
    scaled = grad * gain
    mean_one = jnp.mean(scaled, axis=-1, keepdims=True)
    mean_two = jnp.mean(scaled * unit, axis=-1, keepdims=True)
    return inverse * (scaled - mean_one - unit * mean_two)


def column_sum(values):
    return jnp.sum(values, axis=0, keepdims=True)


def half_masks():
    lane = lax.broadcasted_iota(jnp.int32, (1, 128), 1)
    low = (lane < 64).astype(F32)
    return low.astype(BF), (1.0 - low).astype(BF)


def ring_slot(d1, j2):
    if d1 == 0:
        return 3
    if d1 == 2:
        return 0 if j2 < 2 else 1
    if d1 == 1:
        return 2 if j2 < 2 else 0
    return 1 if j2 < 2 else 2


def row_of(place, d1, j2):
    step1 = jnp.where(place[3] == 0, 48, 192)
    step2 = jnp.where(place[3] == 0, 192, 48)
    return pl.multiple_of(((place[1] + d1) & 3) * step1 + j2 * step2, 16)


def send_blocks(place, total, outs):
    for d1 in range(4):
        for j2 in range(4):
            outs[ring_slot(d1, j2)][j2] = total[pl.ds(row_of(place, d1, j2), 48), :]


def send_z(place, total, near, far, later, home):
    for k in range(4):
        cols = pl.ds(pl.multiple_of((place[5] ^ k) * 384, 128), 384)
        top, low = total[pl.ds(0, 384), cols], total[pl.ds(384, 384), cols]
        if k == 0:
            home[0:384], home[384:768] = top, low
        elif k == 1:
            near[384:768], later[384:768] = top, low
        elif k == 2:
            near[0:384], far[384:768] = top, low
        else:
            later[0:384], far[0:384] = top, low


def level_kernel(place, own, one, two, three, first, last):
    for d, source in enumerate((own, one, two, three)):
        rows = pl.ds(pl.multiple_of(((place[1] + d) & 3) * 96, 16), 96)
        first[0, rows] = source[0]
        first[1, rows] = source[1]
        last[rows] = source[2]


def join_attn_kernel(layer, place, own, near, across, over, far, held):
    pipe, zhi = place[0], place[4]

    def put(group, half, value):
        held[pl.ds(pl.multiple_of(group * 384 + half * 192, 16), 192)] = value

    @pl.when(pipe == layer)
    def _():
        for group in range(4):
            put(group, zhi, own[group * 192 : group * 192 + 192])
            from_two = across if group < 2 else over
            put(group, 1 - zhi, from_two[group % 2 * 192 : group % 2 * 192 + 192])

    @pl.when(pipe != layer)
    def _():
        for group in range(4):
            put(group, zhi, near[group * 192 : group * 192 + 192])
            put(group, 1 - zhi, far[group * 192 : group * 192 + 192])


def join_ffn_kernel(layer, place, own_up, own_down, *refs):
    parts, held = refs[:-1], refs[-1]
    pipe, i2, zhi = place[0], place[2], place[4]

    def gathered(half, slot):
        def put(value, d2, first=0, count=384):
            held[half, pl.ds(pl.multiple_of(((i2 + d2) & 3) * 384 + first, 16), count)] = value

        for n, d2 in enumerate((0, 1, 3)):
            put(parts[n][slot] if slot < 2 else parts[5 + n][...], d2)
        if slot < 2:
            put(parts[3 + slot][...], 2)
        else:
            put(parts[8][...], 2, 0, 192)
            put(parts[9][...], 2, 192, 192)

    @pl.when(pipe == layer)
    def _():
        held[zhi, 0:768] = own_up[...]
        held[zhi, 768:1536] = own_down[...]
        gathered(1 - zhi, 2 * layer)

    @pl.when(pipe != layer)
    def _():
        gathered(zhi, layer)
        gathered(1 - zhi, layer + 1)


def attn_forward_body(x, small, mask_ref, held, a_ref, p_ref, o_ref, scores_ref, probs_ref, part_ref):
    unit, _ = normed(x)
    a_ref[...] = (unit * small[0:1] + small[1:2]).astype(BF)
    p_ref[...] = mt(a_ref[...], held[pl.ds(0, 1152), :]).astype(BF)
    halves = half_masks()
    for page in range(PAGES):
        rows = pl.ds(page * BLOCKS, BLOCKS)
        for pair in range(3):
            q = p_ref[rows, pl.ds(pair * 128, 128)]
            k = p_ref[rows, pl.ds(384 + pair * 128, 128)]
            for n, half in enumerate(halves):
                scores_ref[page, pair * 2 + n] = mt(q, k * half)
    for page in range(PAGES):
        allowed = mask_ref[page] > 0.5
        for head in range(6):
            scores = jnp.where(allowed, scores_ref[page, head] * SCALE, -1e30)
            expo = jnp.exp(scores - jnp.max(scores, axis=-1, keepdims=True))
            probs_ref[page, head] = (expo * (1.0 / jnp.sum(expo, axis=-1, keepdims=True))).astype(BF)
    for page in range(PAGES):
        rows = pl.ds(page * BLOCKS, BLOCKS)
        for pair in range(3):
            v = p_ref[rows, pl.ds(768 + pair * 128, 128)]
            total = mm(probs_ref[page, pair * 2], v * halves[0]) + mm(probs_ref[page, pair * 2 + 1], v * halves[1])
            o_ref[rows, pl.ds(pair * 128, 128)] = total.astype(BF)
    part_ref[...] = mm(o_ref[...], held[pl.ds(1152, 384), :]).astype(BF)


def attn_first_kernel(
    x_ref, small, mask_ref, held, p_ref, part_ref, a_ref, o_ref, scores_ref, probs_ref
):
    attn_forward_body(
        x_ref[...].astype(F32), small, mask_ref, held, a_ref, p_ref, o_ref, scores_ref, probs_ref, part_ref,
    )


def attn_second_kernel(
    mid_ref, mine, other, before, small, mask_ref, held,
    y_ref, p_ref, part_ref, a_ref, o_ref, scores_ref, probs_ref,
):
    total = mine[...].astype(F32) + other[...].astype(F32)
    y_ref[...] = (mid_ref[...] + total + before[5:6]).astype(BF)
    attn_forward_body(
        y_ref[...].astype(F32), small, mask_ref, held, a_ref, p_ref, o_ref, scores_ref, probs_ref, part_ref,
    )


def middle(x_ref, mine, other, small, mid_ref, c_ref):
    mid = x_ref[...].astype(F32) + (mine[...].astype(F32) + other[...].astype(F32)) + small[4:5]
    mid_ref[...] = mid
    unit, _ = normed(mid)
    c_ref[...] = (unit * small[2:3] + small[3:4]).astype(BF)


def gelu_parts(pre):
    cdf = 0.5 * (1.0 + lax.erf(pre * 0.7071067811865476))
    return pre * cdf, cdf + pre * (jnp.exp(-0.5 * pre * pre) * 0.3989422804014327)


def down_product(e_ref, held, part_ref):
    part_ref[...] = (
        mm(e_ref[:, pl.ds(0, 768)], held[0, pl.ds(768, 768), :])
        + mm(e_ref[:, pl.ds(768, 768)], held[1, pl.ds(768, 768), :])
    ).astype(BF)


def up_tile(n, c_ref, held, hidden):
    return mm(c_ref[...], held[n // 3, pl.ds(0, 768), pl.ds(n % 3 * 256, 256)]) + hidden[:, pl.ds(n * 256, 256)]


def ffn_first_kernel(
    x_ref, mine, other, small, hidden, held, mid_ref, pre_ref, part_ref, c_ref, e_ref
):
    middle(x_ref, mine, other, small, mid_ref, c_ref)
    for n in range(6):
        wide = pl.ds(n * 256, 256)
        pre = up_tile(n, c_ref, held, hidden)
        pre_ref[:, wide] = pre
        e_ref[:, wide] = (0.5 * pre * (1.0 + lax.erf(pre * 0.7071067811865476))).astype(BF)
    down_product(e_ref, held, part_ref)


def ffn_back_tile(n, grad, slope, held, du_ref, hidden_ref):
    wide = pl.ds(n * 256, 256)
    grad_e = mt(grad, held[n // 3, pl.ds(768 + n % 3 * 256, 256), :])
    grad_u = (grad_e * slope).astype(BF)
    du_ref[:, wide] = grad_u
    hidden_ref[:, wide] = column_sum(grad_u.astype(F32))


def ffn_back_product(du_ref, held, back_ref):
    back_ref[...] = (
        mt(du_ref[:, pl.ds(0, 768)], held[0, pl.ds(0, 768), :])
        + mt(du_ref[:, pl.ds(768, 768)], held[1, pl.ds(0, 768), :])
    ).astype(BF)


def ffn_grads_kernel(place, c_ref, du_ref, grad_ref, e_ref, g0, g1, g2, g3, total):
    turned = c_ref[...].T
    for n in range(6):
        wide = pl.ds(n * 256, 256)
        total[:, wide] = mm(turned, du_ref[:, wide]).astype(BF)
    turned = grad_ref[...].T
    for n in range(6):
        total[:, pl.ds(1536 + n * 256, 256)] = mm(turned, e_ref[:, pl.ds(n * 256, 256)]).astype(BF)
    send_blocks(place, total, (g0, g1, g2, g3))


def ffn_second_kernel(
    x_ref, mine, other, small, hidden, grad_ref, held,
    mid_ref, part_ref, back_ref, hidden_ref, c_ref, e_ref, du_ref, slope_ref,
):
    middle(x_ref, mine, other, small, mid_ref, c_ref)
    for n in range(6):
        wide = pl.ds(n * 256, 256)
        value, slope_ref[:, wide] = gelu_parts(up_tile(n, c_ref, held, hidden))
        e_ref[:, wide] = value.astype(BF)
    down_product(e_ref, held, part_ref)
    for n in range(6):
        ffn_back_tile(n, grad_ref[...], slope_ref[:, pl.ds(n * 256, 256)], held, du_ref, hidden_ref)
    ffn_back_product(du_ref, held, back_ref)


def layer_input_back(mine, other, up_grad, x_ref, small, dx_ref, sums_ref):
    grad = mine[...].astype(F32) + other[...].astype(F32)
    unit, inverse = normed(x_ref[...].astype(F32))
    sums_ref[0:1] = column_sum(grad * unit)
    sums_ref[1:2] = column_sum(grad)
    dx_ref[...] = (up_grad[...] + norm_back(grad, unit, inverse, small[0:1])).astype(BF)


def ffn_back_kernel(
    mine, other, up_grad, x_ref, small, below, mid_ref, pre_ref, held,
    dx_ref, back_ref, hidden_ref, sums_ref, c_ref, e_ref, du_ref,
):
    layer_input_back(mine, other, up_grad, x_ref, small, dx_ref, sums_ref)
    unit, _ = normed(mid_ref[...])
    c_ref[...] = (unit * below[2:3] + below[3:4]).astype(BF)
    for n in range(6):
        wide = pl.ds(n * 256, 256)
        value, slope = gelu_parts(pre_ref[:, wide])
        e_ref[:, wide] = value.astype(BF)
        ffn_back_tile(n, dx_ref[...], slope, held, du_ref, hidden_ref)
    ffn_back_product(du_ref, held, back_ref)


def last_kernel(mine, other, up_grad, x_ref, small, sums0, hidden0, first1, sums1, hidden1, dx_ref, vec):
    layer_input_back(mine, other, up_grad, x_ref, small, dx_ref, vec)
    vec[2:6] = sums0[...]
    vec[8:10] = first1[...]
    vec[10:14] = sums1[...]
    for n, part in enumerate((hidden0, hidden1)):
        vec[8 * n + 6 : 8 * n + 7] = part[:, 0:768]
        vec[8 * n + 7 : 8 * n + 8] = part[:, 768:1536]


def attn_back_kernel(layer, *refs):
    if layer == 1:
        end_mine, end_other, y_ref = refs[0], refs[1], refs[11]
        refs = refs[2:11] + refs[12:]
    (mine, other, dy_ref, mid_ref, small, mask_ref, p_ref, x_ref, held,
     dmid_ref, part_ref, sums_ref, a_ref, dr_ref, dp_ref, o_ref,
     do_ref, scores, dprobs, probs, dscores) = refs
    if layer == 1:
        y_ref[...] = (
            mid_ref[...] + (end_mine[...].astype(F32) + end_other[...].astype(F32)) + small[5:6]
        ).astype(BF)
    grad = mine[...].astype(F32) + other[...].astype(F32)
    dy = dy_ref[...].astype(F32)
    unit, inverse = normed(mid_ref[...])
    sums_ref[0:1] = column_sum(grad * unit)
    sums_ref[1:2] = column_sum(grad)
    dmid = dy + norm_back(grad, unit, inverse, small[2:3])
    dmid_ref[...] = dmid
    sums_ref[2:3] = column_sum(dmid)
    sums_ref[3:4] = column_sum(dy)
    dr_ref[...] = dmid.astype(BF)
    unit, _ = normed(x_ref[...].astype(F32))
    a_ref[...] = (unit * small[0:1] + small[1:2]).astype(BF)
    do_ref[...] = mt(dr_ref[...], held[pl.ds(1152, 384), :]).astype(BF)
    halves = half_masks()
    for page in range(PAGES):
        rows = pl.ds(page * BLOCKS, BLOCKS)
        for pair in range(3):
            q = p_ref[rows, pl.ds(pair * 128, 128)]
            k = p_ref[rows, pl.ds(384 + pair * 128, 128)]
            v = p_ref[rows, pl.ds(768 + pair * 128, 128)]
            do = do_ref[rows, pl.ds(pair * 128, 128)]
            for n, half in enumerate(halves):
                scores[page, pair * 2 + n] = mt(k * half, q)
                dprobs[page, pair * 2 + n] = mt(v * half, do)
    for page in range(PAGES):
        allowed = mask_ref[page] > 0.5
        for head in range(6):
            masked = jnp.where(allowed, scores[page, head] * SCALE, -1e30)
            expo = jnp.exp(masked - jnp.max(masked, axis=0, keepdims=True))
            share = expo * (1.0 / jnp.sum(expo, axis=0, keepdims=True))
            slope = dprobs[page, head]
            inner = jnp.sum(share * slope, axis=0, keepdims=True)
            probs[page, head] = share.astype(BF)
            dscores[page, head] = (share * (slope - inner)).astype(BF)
    for page in range(PAGES):
        rows = pl.ds(page * BLOCKS, BLOCKS)
        for pair in range(3):
            q = p_ref[rows, pl.ds(pair * 128, 128)]
            k = p_ref[rows, pl.ds(384 + pair * 128, 128)]
            v = p_ref[rows, pl.ds(768 + pair * 128, 128)]
            do = do_ref[rows, pl.ds(pair * 128, 128)]

            def both(product, left, right):
                one = product(left[page, pair * 2], right * halves[0])
                return one + product(left[page, pair * 2 + 1], right * halves[1])

            dp_ref[rows, pl.ds(pair * 128, 128)] = (both(tm, dscores, k) * SCALE).astype(BF)
            dp_ref[rows, pl.ds(384 + pair * 128, 128)] = (both(mm, dscores, q) * SCALE).astype(BF)
            dp_ref[rows, pl.ds(768 + pair * 128, 128)] = both(mm, probs, do).astype(BF)
            o_ref[rows, pl.ds(pair * 128, 128)] = both(tm, probs, v).astype(BF)
    part_ref[...] = mm(dp_ref[...], held[pl.ds(0, 1152), :]).astype(BF)


def attn_grads_kernel(place, a_ref, dp_ref, dr_ref, o_ref, near, far, later, home, total):
    turned = a_ref[...].T
    for n in range(3):
        cols = pl.ds(n * 384, 384)
        total[:, cols] = mm(turned, dp_ref[:, cols]).astype(BF)
    total[:, pl.ds(1152, 384)] = mm(dr_ref[...].T, o_ref[...]).astype(BF)
    send_z(place, total, near, far, later, home)


def added(left, right):
    return (left.astype(F32) + right.astype(F32)).astype(BF)


def added(left, right):
    return (left.astype(F32) + right.astype(F32)).astype(BF)


def arrived(home, plus, minus, total):
    half = home.shape[0] // 2
    total[0:half] = added(home[0:half], minus[0:half])
    total[half : 2 * half] = added(home[half : 2 * half], plus[half : 2 * half])


def pass_on_kernel(later, home, plus, minus, on_plus, on_minus, total):
    half = later.shape[0] // 2
    on_plus[...] = added(later[0:half], plus[0:half])
    on_minus[...] = added(later[half:], minus[half : 2 * half])
    arrived(home, plus, minus, total)


def join_kernel(plus, minus, later, home, got_plus, got_minus, out_plus, out_minus, total):
    size, half = plus.shape[0], plus.shape[0] // 2
    out_plus[0:size] = plus[...]
    out_minus[0:size] = minus[...]
    out_plus[size : size + half] = added(later[0:half], got_plus[0:half])
    out_minus[size : size + half] = added(later[half:], got_minus[half:size])
    arrived(home, got_plus, got_minus, total)


def join_z_kernel(near, far, later, home, got_near, got_far, out_near, out_far, total):
    out_near[0:768] = near[...]
    out_far[0:768] = far[...]
    out_far[768:1152] = added(later[0:384], got_near[0:384])
    out_near[768:1152] = added(later[384:768], got_far[384:768])
    total[0:384] = added(home[0:384], got_near[384:768])
    total[384:768] = added(home[384:768], got_far[0:384])


def pass_on_z_kernel(later, home, near, far, on_far, on_near, total):
    on_far[...] = added(later[0:384], near[0:384])
    on_near[...] = added(later[384:768], far[384:768])
    total[0:384] = added(home[0:384], near[384:768])
    total[384:768] = added(home[384:768], far[0:384])


def fold_kernel(place, some1, some0, plus0, minus0, last_plus, last_minus, plus, minus, later, home, total):
    total[1, 0:2] = added(some1[0:2], plus0[4:6])
    total[1, 2:4] = added(some1[2:4], minus0[4:6])
    total[0, 0:2] = added(some0[0:2], last_plus[...])
    total[0, 2:4] = added(some0[2:4], last_minus[...])

    def block(layer, d):
        return total[layer, (place[2] + d) & 3]

    plus[0], plus[1] = block(0, 2), block(1, 1)
    minus[0], minus[1] = block(0, 3), block(1, 2)
    later[0], later[1] = block(0, 1), block(1, 3)
    home[0], home[1] = block(0, 0), block(1, 0)


def put_split(out, first, value):
    count = value.shape[0]
    high = value.astype(BF)
    out[first : first + count] = high
    out[first + count : first + 2 * count] = (value - high.astype(F32)).astype(BF)


def get_split(ref, first, count):
    return ref[first : first + count].astype(F32) + ref[first + count : first + 2 * count].astype(F32)


def fold_z_kernel(place, *refs):
    some1, some0, near0, far0, last_far, last_near = refs[0:6]
    vec, outs, total = refs[6], refs[7:11], refs[11]
    total[0:384, 384:768] = added(some1[0:384], far0[768:1152])
    total[384:768, 384:768] = added(some1[384:768], near0[768:1152])
    total[0:384, 0:384] = added(some0[0:384], last_far[...])
    total[384:768, 0:384] = added(some0[384:768], last_near[...])
    for d1 in range(4):
        for j2 in range(4):
            outs[d1][j2 * 48 : j2 * 48 + 48] = total[pl.ds(row_of(place, d1, j2), 48)]
        put_split(outs[d1], 192, vec[...])


def turn_kernel(place, own, one, two, three, m0, m1, m2, m3, total, vecs):
    got = (own, one, two, three)
    total[...] = sum(r[0:192].astype(F32) for r in got).astype(BF)
    for s, r in enumerate(got):
        vecs[(place[1] - s) & 3] = get_split(r, 192, 16)
    vec = (vecs[0] + vecs[1]) + (vecs[2] + vecs[3])
    for s, out in enumerate((m0, m1, m2, m3)):
        row = pl.multiple_of(((place[2] + s) & 3) * 48, 16)
        out[0:48] = total[pl.ds(row, 48)]
        put_split(out, 48, vec)


def pack_kernel(place, *refs):
    some, last_plus, last_minus = refs[0:3]
    got, outs, staged, vecs = refs[3:7], refs[7:11], refs[11], refs[12]
    ffn0 = some[0].astype(F32) + last_plus[0].astype(F32)
    ffn1 = some[1].astype(F32) + last_minus[0].astype(F32)
    attn = sum(r[0:48].astype(F32) for r in got)
    for s, r in enumerate(got):
        vecs[(place[2] - s) & 3] = get_split(r, 48, 16)
    vec = (vecs[0] + vecs[1]) + (vecs[2] + vecs[3])
    zz = place[5]
    for half in range(2):
        for layer, ffn in ((0, ffn0), (1, ffn1)):
            to = staged.at[2 * half + layer]
            at = layer * 384 + half * 192
            for group in range(4):
                to[0:48, pl.ds(group * 192, 192)] = jnp.where(zz == group, attn[:, at : at + 192], 0.0).astype(BF)
            to[48:96] = ffn[:, half * 768 : half * 768 + 768].astype(BF)
            to[96:144] = ffn[:, 1536 + half * 768 : 1536 + half * 768 + 768].astype(BF)
            put_split(to, 144, vec[8 * layer : 8 * layer + 8])
    for k in range(4):
        outs[k][...] = staged[zz ^ k]


def finish_kernel(place, a, b, c, d, qkv_ref, out_ref, up_ref, down_ref, vec_ref, vecs):
    got = (a, b, c, d)
    total = sum(r[0:144].astype(F32) for r in got)
    for group in range(3):
        qkv_ref[group] = total[0:48, group * 192 : group * 192 + 192]
    out_ref[...] = total[0:48, 576:768]
    up_ref[...] = total[48:96]
    down_ref[...] = total[96:144]
    for k, r in enumerate(got):
        vecs[place[5] ^ k] = get_split(r, 144, 8)
    vec_ref[...] = (vecs[0] + vecs[1]) + (vecs[2] + vecs[3])


def small_kernel(place, mine, other, hidden_ref, gains_ref, shifts_ref, biases_ref):
    first = place[3] == 0
    low = jnp.where(first, mine[...], other[...])
    high = jnp.where(first, other[...], mine[...])
    for n, row in enumerate((low[6:7], high[6:7], low[7:8], high[7:8])):
        hidden_ref[:, n * 768 : n * 768 + 768] = row
    for n in range(2):
        gains_ref[0, n : n + 1] = low[2 * n : 2 * n + 1]
        shifts_ref[0, n : n + 1] = low[2 * n + 1 : 2 * n + 2]
    biases_ref[0] = low[4:6]


VM = pl.BlockSpec(memory_space=pltpu.VMEM)
SM = pl.BlockSpec(memory_space=pltpu.SMEM)
ANY = pl.BlockSpec(memory_space=pl.ANY)


def shape(dims, dtype):
    return jax.ShapeDtypeStruct(dims, dtype)


def call(body, ins, outs, scratch, args, limit=16, after=()):
    count, extra = len(args), len(after)
    name = getattr(body, 'func', body).__name__
    if extra:
        inner = body

        def body(*refs):
            return inner(*refs[:count], *refs[count + extra :])

        ins, args = ins + [ANY] * extra, [*args, *after]
    return pl.pallas_call(
        body,
        in_specs=ins,
        out_specs=tuple(spec for spec, _ in outs),
        out_shape=tuple(form for _, form in outs),
        scratch_shapes=scratch,
        compiler_params=pltpu.CompilerParams(vmem_limit_bytes=limit * 1024 * 1024),
        cost_estimate=pl.CostEstimate(flops=int(COSTS.get(name, 0.0) * FACTOR * 1e9) + 1024, bytes_accessed=1024, transcendentals=0),
    )(*args)


ROW_BF = (VM, shape((ROWS, D), BF))
ROW_F32 = (VM, shape((ROWS, D), F32))


def pairs_allowed(flags, valid):
    place = lax.broadcasted_iota(jnp.int32, (BLOCKS,), 0)
    visual = place >= TEXT
    dropped = (flags[:, None] == 1) & visual[None] | (flags[:, None] == 2) & ~visual[None]
    key_ok = (valid == 1) & ~dropped
    same = place[:, None] == place[None, :]
    other = visual[:, None] != visual[None, :]
    cross = same[None] | other[None] & key_ok[:, None, :]
    plain = same[None] | key_ok[:, None, :]
    masks = []
    for allowed in (cross, plain):
        allowed = allowed.astype(F32)
        masks.append((allowed, jnp.swapaxes(allowed, 1, 2)))
    return masks


def on_device(
    block_input, out_cotangent, drop_flags, key_valid, qkv_weight, out_weight, up_weight, down_weight,
    hidden_bias, norm_gains, norm_shifts, out_biases,
):
    y, x = lax.axis_index("y"), lax.axis_index("x")
    pipe, zhi, core = lax.axis_index("pipe"), lax.axis_index("zhi"), lax.axis_index("core")
    zz = 2 * zhi + pipe
    i1 = jnp.where(core == 0, x, y)
    i2 = jnp.where(core == 0, y, x)
    place = jnp.stack([pipe, i1, i2, core, zhi, zz]).astype(jnp.int32)

    packed = jnp.concatenate([
        norm_gains[0, 0:1], norm_shifts[0, 0:1], norm_gains[0, 1:2], norm_shifts[0, 1:2], out_biases[0],
        hidden_bias, jnp.zeros((1, D), F32),
    ])
    terms, rest = [], packed
    for _ in range(3):
        term = lax.reduce_precision(rest, 8, 7)
        terms.append(term.astype(BF))
        rest = rest - term
    packed_low = jnp.concatenate(terms)

    own_attn = jnp.concatenate([jnp.transpose(qkv_weight[0], (1, 2, 0)).reshape(576, D), out_weight[0]])
    own_up, own_down = up_weight[0], down_weight[0]
    number = i2 * 4 + i1
    ffn_slice = jnp.where(
        number < 8,
        lax.dynamic_slice_in_dim(own_up, (number & 7) * 96, 96),
        lax.dynamic_slice_in_dim(own_down, (number & 7) * 96, 96),
    )
    piece = jnp.concatenate([ffn_slice, packed_low])
    from_z = [piece] + [swap_z(piece, k) for k in (1, 2, 3)]
    order = jnp.where(
        pipe == 0,
        jnp.stack([from_z[k][:96] for k in (2, 1, 3)]),
        jnp.stack([from_z[k][:96] for k in (1, 3, 2)]),
    )
    level = [order] + [ring_shift(order, FIRST, 4 - d) for d in (1, 2, 3)]
    first_level, last_level = call(
        level_kernel, [SM] + [VM] * 4, [(VM, shape((2, 384, D), BF)), (VM, shape((384, D), BF))], [],
        [place, *level],
    )
    after, before = ring_shift(first_level, SECOND, 3), ring_shift(first_level, SECOND, 1)
    parts = [first_level, after, before, ring_shift(before[0], SECOND, 1), ring_shift(after[1], SECOND, 3)]
    last_level, *_ = lax.optimization_barrier((last_level, after, before))
    after, before = ring_shift(last_level, SECOND, 3), ring_shift(last_level, SECOND, 1)
    more_parts = parts + [
        last_level, after, before, ring_shift(before[:192], SECOND, 1), ring_shift(after[192:], SECOND, 3)
    ]

    both = jnp.stack([block_input, out_cotangent], axis=1)
    given = lax.dynamic_index_in_dim(both, zz ^ 3, 0, keepdims=False)
    near = swap_z(own_attn, 1)
    far = swap_z(jnp.concatenate([own_attn, given.reshape(144, D)]), 3)
    diagonal = [swap_z(near[:384], 3), swap_z(far[384:768], 1)]

    def whole(k):
        return sum(from_z[k][96 + 8 * n : 104 + 8 * n].astype(F32) for n in range(3))

    full = [whole(k) for k in range(4)]
    small, hidden = [], []
    for layer in range(2):
        same = jnp.where(pipe == layer, full[0], full[1])
        other = jnp.where(pipe == layer, full[2], full[3])
        small.append(same[:6])
        hidden.append(
            jnp.where(
                zhi == 0,
                jnp.concatenate([same[6:7], other[6:7]], axis=1),
                jnp.concatenate([other[6:7], same[6:7]], axis=1),
            )
        )

    drop_flags, key_valid, _ = lax.optimization_barrier((drop_flags, key_valid, level[1]))
    kept = lax.dynamic_index_in_dim(both, zz, 0, keepdims=False)
    came = far[768:].reshape(2, 72, D)
    halves = jnp.where(zhi == 0, jnp.stack([kept, came]), jnp.stack([came, kept]))
    across = swap_cores(halves)
    rows = jnp.where(core == 0, jnp.stack([halves, across], 1), jnp.stack([across, halves], 1))
    x0 = rows[:, :, 0].reshape(ROWS, D)
    cotangent = rows[:, :, 1].reshape(ROWS, D)
    flags = lax.dynamic_index_in_dim(drop_flags, zz, 0, keepdims=False)
    valid = lax.dynamic_index_in_dim(key_valid, zz, 0, keepdims=False)
    masks = pairs_allowed(flags, valid)

    attn_whole, ffn_whole = (VM, shape((1536, D), BF)), (VM, shape((2, 1536, D), BF))

    def join_attn(layer):
        (held,) = call(
            partial(join_attn_kernel, layer), [SM] + [VM] * 5, [attn_whole], [],
            [place, own_attn, near, *diagonal, far],
        )
        return held

    def join_ffn(layer, sources, after=()):
        (held,) = call(
            partial(join_ffn_kernel, layer), [SM] + [VM] * (2 + len(sources)), [ffn_whole], [],
            [place, own_up, own_down, *sources], after=after,
        )
        return held

    projected = (VM, shape((ROWS, 1152), BF))
    row_scratch = pltpu.VMEM((ROWS, D), BF)
    head_scratch = pltpu.VMEM((ROWS, 384), BF)
    wide_scratch = pltpu.VMEM((ROWS, 1536), BF)
    scores, probs = pltpu.VMEM((PAGES, 6, BLOCKS, BLOCKS), F32), pltpu.VMEM((PAGES, 6, BLOCKS, BLOCKS), BF)
    attn_scratch = [row_scratch, head_scratch, scores, probs]
    attn_held0, attn_held1 = join_attn(0), join_attn(1)
    p0, part = call(
        attn_first_kernel, [VM] * 4, [projected, ROW_BF], attn_scratch, [x0, small[0], masks[0][0], attn_held0]
    )
    ffn_held0 = join_ffn(0, parts)
    mid0, pre0, part = call(
        ffn_first_kernel, [VM] * 6, [ROW_F32, (VM, shape((ROWS, 1536), F32)), ROW_BF], [row_scratch, wide_scratch],
        [x0, part, swap_cores(part), small[0], hidden[0], ffn_held0],
    )
    y0, p1, part = call(
        attn_second_kernel, [VM] * 7, [ROW_BF, projected, ROW_BF], attn_scratch,
        [mid0, part, swap_cores(part), small[0], small[1], masks[1][0], attn_held1],
    )
    ffn_held1 = join_ffn(1, more_parts, [part])

    hidden_sum = (VM, shape((1, 1536), F32))
    two_sums = (VM, shape((2, D), F32))
    ring_blocks = [(VM, shape((4, 48, 3072), BF))] * 4
    z_blocks = [(VM, shape((D, 384), BF))] * 4
    ffn_total = pltpu.VMEM((D, 3072), BF)
    wide = (VM, shape((ROWS, 1536), BF))
    mid1, part, back, dhidden1, c1, e1, du1 = call(
        ffn_second_kernel, [VM] * 7, [ROW_F32, ROW_BF, ROW_BF, hidden_sum, ROW_BF, wide, wide],
        [pltpu.VMEM((ROWS, 1536), F32)],
        [y0, part, swap_cores(part), small[1], hidden[1], cotangent, ffn_held1],
    )
    plus1, minus1, later1, home1 = call(
        ffn_grads_kernel, [SM] + [VM] * 4, ring_blocks, [ffn_total], [place, c1, du1, cotangent, e1]
    )
    token = later1
    plus1, minus1 = ring_shift(plus1, FIRST, 1), ring_shift(minus1, FIRST, 3)

    back_scratch = [head_scratch, scores, scores, probs, probs]
    back_outs = [ROW_F32, ROW_BF, (VM, shape((4, D), F32)), ROW_BF, ROW_BF, projected, (VM, shape((ROWS, 384), BF))]
    y1, dmid1, back, sums1, a1, dr1, dp1, o1 = call(
        partial(attn_back_kernel, 1), [VM] * 11, [ROW_BF] + back_outs, back_scratch,
        [part, swap_cores(part), back, swap_cores(back), cotangent, mid1, small[1], masks[1][1], p1, y0,
         attn_held1], after=[token],
    )
    attn_total = [pltpu.VMEM((D, 1536), BF)]
    near1, far1, later_z1, home_z1 = call(
        attn_grads_kernel, [SM] + [VM] * 4, z_blocks, attn_total, [place, a1, dp1, dr1, o1]
    )
    token = later_z1
    near1, far1 = swap_z(near1, 1), swap_z(far1, 3)
    dx1, back, dhidden0, first1, c0, e0, du0 = call(
        ffn_back_kernel, [VM] * 9, [ROW_BF, ROW_BF, hidden_sum, two_sums, ROW_BF, wide, wide], [],
        [back, swap_cores(back), dmid1, y0, small[1], small[0], mid0, pre0, ffn_held0], after=[token],
    )
    plus0, minus0, later0, home0 = call(
        ffn_grads_kernel, [SM] + [VM] * 4, ring_blocks, [ffn_total], [place, c0, du0, dx1, e0]
    )
    six, four = [(VM, shape((6, 48, 3072), BF))] * 2, [(VM, shape((4, 48, 3072), BF))]
    plus0, minus0, some1 = call(
        join_kernel, [VM] * 6, six + four, [], [plus0, minus0, later1, home1, plus1, minus1], 20
    )
    token = some1
    plus0, minus0 = ring_shift(plus0, FIRST, 1), ring_shift(minus0, FIRST, 3)
    dmid0, back, sums0, a0, dr0, dp0, o0 = call(
        partial(attn_back_kernel, 0), [VM] * 9, back_outs, back_scratch,
        [back, swap_cores(back), dx1, mid0, small[0], masks[0][1], p0, x0, attn_held0],
        after=[token],
    )
    near0, far0, later_z0, home_z0 = call(
        attn_grads_kernel, [SM] + [VM] * 4, z_blocks, attn_total, [place, a0, dp0, dr0, o0]
    )
    tall = [(VM, shape((1152, 384), BF))] * 2
    near0, far0, some_z1 = call(
        join_z_kernel, [VM] * 6, tall + z_blocks[:1], [], [near0, far0, later_z1, home_z1, near1, far1]
    )
    token = some_z1
    near0, far0 = swap_z(near0, 1), swap_z(far0, 3)
    dx0, vec = call(
        last_kernel, [VM] * 10, [ROW_BF, (VM, shape((16, D), F32))], [],
        [back, swap_cores(back), dmid0, x0, small[0], sums0, dhidden0, first1, sums1, dhidden1], after=[token],
    )

    pair, one = [(VM, shape((2, 48, 3072), BF))], [(VM, shape((1, 48, 3072), BF))]
    on_plus, on_minus, some0 = call(
        pass_on_kernel, [VM] * 4, pair * 2 + four, [], [later0, home0, plus0, minus0], after=[vec]
    )
    last_plus, last_minus = ring_shift(on_plus, FIRST, 1), ring_shift(on_minus, FIRST, 3)
    half = [(VM, shape((384, 384), BF))]
    on_far, on_near, some_z0 = call(
        pass_on_z_kernel, [VM] * 4, half * 2 + z_blocks[:1], [], [later_z0, home_z0, near0, far0], after=[some0]
    )
    last_far, last_near = swap_z(on_far, 3), swap_z(on_near, 1)
    plus, minus, later, home = call(
        fold_kernel, [SM] + [VM] * 6, pair * 4, [pltpu.VMEM((2, 4, 48, 3072), BF)],
        [place, some1, some0, plus0, minus0, last_plus, last_minus], after=[some_z0],
    )
    plus, minus = ring_shift(plus, SECOND, 1), ring_shift(minus, SECOND, 3)
    turned = call(
        fold_z_kernel, [SM] + [VM] * 7, [(VM, shape((224, D), BF))] * 4, [pltpu.VMEM((D, D), BF)],
        [place, some_z1, some_z0, near0, far0, last_far, last_near, vec], after=[home],
    )
    on_plus, on_minus, some = call(
        pass_on_kernel, [VM] * 4, one * 2 + pair, [], [later, home, plus, minus], after=[turned[0]]
    )
    last_plus, last_minus = ring_shift(on_plus, SECOND, 1), ring_shift(on_minus, SECOND, 3)
    turned = call(
        turn_kernel, [SM] + [VM] * 4, [(VM, shape((80, D), BF))] * 4,
        [pltpu.VMEM((192, D), BF), pltpu.VMEM((4, 16, D), F32)],
        [place, turned[0]] + [ring_shift(turned[s], FIRST, s) for s in (1, 2, 3)],
        after=[some, last_plus, last_minus],
    )
    token = (last_plus, last_minus)
    turned = [turned[0]] + [ring_shift(turned[s], SECOND, s) for s in (1, 2, 3)]
    packs = call(
        pack_kernel, [SM] + [VM] * 7, [(VM, shape((160, D), BF))] * 4,
        [pltpu.VMEM((4, 160, D), BF), pltpu.VMEM((4, 16, D), F32)], [place, some, last_plus, last_minus, *turned],
    )
    grad_qkv, grad_out, grad_up, grad_down, vec = call(
        finish_kernel, [SM] + [VM] * 4,
        [(VM, shape((3, 48, 192), F32)), (VM, shape((48, 192), F32))] + [(VM, shape((48, D), F32))] * 2
        + [(VM, shape((8, D), F32))], [pltpu.VMEM((4, 8, D), F32)],
        [place, packs[0]] + [swap_z(packs[k], k) for k in (1, 2, 3)],
    )
    grad_qkv = jnp.transpose(grad_qkv, (1, 0, 2))
    grad_out, grad_down = grad_out.T, grad_down.T
    grad_hidden, grad_gains, grad_shifts, grad_biases = call(
        small_kernel, [SM] + [VM] * 2, [(VM, shape((1, 4 * D), F32))] + [(VM, shape((1, 2, D), F32))] * 3, [],
        [place, vec, swap_cores(vec)],
    )

    rows, *_ = lax.optimization_barrier((jnp.stack([jnp.stack([y0, y1]), jnp.stack([dx0, dx1])]), *token))
    rows = rows.reshape(2, 2, 2, 2, 72, D)

    def for_chip(k):
        mine = lax.dynamic_index_in_dim(rows, pipe ^ (k & 1), 1, keepdims=False)
        mine = lax.dynamic_index_in_dim(mine, zhi ^ (k >> 1), 1, keepdims=False)
        return lax.dynamic_index_in_dim(mine, core, 1, keepdims=False)

    got = jnp.stack([for_chip(0)] + [swap_z(for_chip(k), k) for k in (1, 2, 3)])
    got = jnp.stack([lax.dynamic_index_in_dim(got, zz ^ m, 0, keepdims=False) for m in range(4)], axis=1)
    activations, input_grads = got[0], got[1]
    return (
        activations[None],
        input_grads[None],
        grad_qkv[None],
        grad_out[None],
        grad_up[None],
        grad_down[None],
        grad_hidden,
        grad_gains,
        grad_shifts,
        grad_biases,
    )


def solution(mesh):
    fine = Mesh(mesh.devices.reshape(4, 4, 2, 2, 2), MESH_AXES)
    rows = DP + TENSOR
    in_specs = (
        P(None, rows, None),
        P(None, rows, None),
        P(None, DP),
        P(None, DP, None),
        P("pipe", None, None, TENSOR),
        P("pipe", TENSOR, None),
        P("pipe", None, TENSOR),
        P("pipe", TENSOR, None),
        P("pipe", TENSOR),
        P("pipe", None, None),
        P("pipe", None, None),
        P("pipe", None, None),
    )
    out_specs = (
        P("pipe", None, rows, None),
        P("pipe", None, rows, None),
        P("pipe", DP, None, TENSOR),
        P("pipe", TENSOR, DP),
        P("pipe", DP, TENSOR),
        P("pipe", TENSOR, DP),
        P("pipe", None),
        P("pipe", None, None),
        P("pipe", None, None),
        P("pipe", None, None),
    )
    return jax.shard_map(on_device, mesh=fine, in_specs=in_specs, out_specs=out_specs, check_vma=False)
```

```python
from functools import partial

import jax
import jax.numpy as jnp
from jax import lax
from jax.experimental import pallas as pl
from jax.experimental.pallas import tpu as pltpu
from jax.sharding import Mesh
from jax.sharding import PartitionSpec as P

BF = jnp.bfloat16
F32 = jnp.float32
D = 768
BLOCKS = 96
TEXT = 72
ROWS = 288
PAGES = 3
SCALE = 0.125
FACTOR = 3.0
COSTS = {'fold_z_kernel': 3, 'pass_on_kernel': 1, 'fold_kernel': 0.7, 'turn_kernel': 0.7, 'pack_kernel': 0.7, 'last_kernel': 0.7, 'join_kernel': 0.7, 'join_ffn_kernel': 0.7, 'level_kernel': 0.7, 'ffn_first_kernel': 2.3, 'attn_second_kernel': 2.4, 'ffn_second_kernel': 3.8, 'ffn_grads_kernel': 3.5, 'attn_back_kernel': 3.7, 'attn_grads_kernel': 2.4, 'ffn_back_kernel': 3.0}

MESH_AXES = ("y", "x", "pipe", "zhi", "core")
DP = ("y", "x")
TENSOR = ("zhi", "core")


def swap_cores(value):
    return lax.ppermute(value, "core", [(0, 1), (1, 0)])


def swap_z(value, k):
    pairs = []
    for p in range(2):
        for h in range(2):
            other = (2 * h + p) ^ k
            pairs.append((p * 2 + h, (other & 1) * 2 + (other >> 1)))
    return lax.ppermute(value, ("pipe", "zhi"), pairs)


def exchange_z(value):
    return lax.all_to_all(value, ("pipe", "zhi"), 0, 0, tiled=True)


def ring_shift(value, axis_of_core, shift):
    pairs = []
    for y in range(4):
        for x in range(4):
            for c in range(2):
                if axis_of_core[c] == "x":
                    to = (y, (x + shift) % 4)
                else:
                    to = ((y + shift) % 4, x)
                pairs.append(((y * 4 + x) * 2 + c, (to[0] * 4 + to[1]) * 2 + c))
    return lax.ppermute(value, ("y", "x", "core"), pairs)


FIRST = ("x", "y")
SECOND = ("y", "x")


def mm(a, b):
    return lax.dot_general(a, b, (((1,), (0,)), ((), ())), preferred_element_type=F32)


def mt(a, b):
    return lax.dot_general(a, b, (((1,), (1,)), ((), ())), preferred_element_type=F32)


def tm(a, b):
    return lax.dot_general(a, b, (((0,), (0,)), ((), ())), preferred_element_type=F32)


def normed(values):
    centre = values - jnp.mean(values, axis=-1, keepdims=True)
    spread = jnp.mean(centre * centre, axis=-1, keepdims=True)
    inverse = lax.rsqrt(spread + 1e-05)
    return centre * inverse, inverse


def norm_back(grad, unit, inverse, gain):
    scaled = grad * gain
    mean_one = jnp.mean(scaled, axis=-1, keepdims=True)
    mean_two = jnp.mean(scaled * unit, axis=-1, keepdims=True)
    return inverse * (scaled - mean_one - unit * mean_two)


def column_sum(values):
    return jnp.sum(values, axis=0, keepdims=True)


def half_masks():
    lane = lax.broadcasted_iota(jnp.int32, (1, 128), 1)
    low = (lane < 64).astype(F32)
    return low.astype(BF), (1.0 - low).astype(BF)


def ring_slot(d1, j2):
    if d1 == 0:
        return 3
    if d1 == 2:
        return 0 if j2 < 2 else 1
    if d1 == 1:
        return 2 if j2 < 2 else 0
    return 1 if j2 < 2 else 2


def row_of(place, d1, j2):
    step1 = jnp.where(place[3] == 0, 48, 192)
    step2 = jnp.where(place[3] == 0, 192, 48)
    return pl.multiple_of(((place[1] + d1) & 3) * step1 + j2 * step2, 16)


def send_blocks(place, total, outs):
    for d1 in range(4):
        for j2 in range(4):
            outs[ring_slot(d1, j2)][j2] = total[pl.ds(row_of(place, d1, j2), 48), :]


def send_z(place, total, near, far, later, home):
    for k in range(4):
        cols = pl.ds(pl.multiple_of((place[5] ^ k) * 384, 128), 384)
        top, low = total[pl.ds(0, 384), cols], total[pl.ds(384, 384), cols]
        if k == 0:
            home[0:384], home[384:768] = top, low
        elif k == 1:
            near[384:768], later[384:768] = top, low
        elif k == 2:
            near[0:384], far[384:768] = top, low
        else:
            later[0:384], far[0:384] = top, low


def level_kernel(place, own, one, two, three, first, last):
    for d, source in enumerate((own, one, two, three)):
        rows = pl.ds(pl.multiple_of(((place[1] + d) & 3) * 96, 16), 96)
        first[0, rows] = source[0]
        first[1, rows] = source[1]
        last[rows] = source[2]


def join_attn_kernel(layer, place, own, near, across, over, far, held):
    pipe, zhi = place[0], place[4]

    def put(group, half, value):
        held[pl.ds(pl.multiple_of(group * 384 + half * 192, 16), 192)] = value

    @pl.when(pipe == layer)
    def _():
        for group in range(4):
            put(group, zhi, own[group * 192 : group * 192 + 192])
            from_two = across if group < 2 else over
            put(group, 1 - zhi, from_two[group % 2 * 192 : group % 2 * 192 + 192])

    @pl.when(pipe != layer)
    def _():
        for group in range(4):
            put(group, zhi, near[group * 192 : group * 192 + 192])
            put(group, 1 - zhi, far[group * 192 : group * 192 + 192])


def join_ffn_kernel(layer, place, own_up, own_down, *refs):
    parts, held = refs[:-1], refs[-1]
    pipe, i2, zhi = place[0], place[2], place[4]

    def gathered(half, slot):
        def put(value, d2, first=0, count=384):
            held[half, pl.ds(pl.multiple_of(((i2 + d2) & 3) * 384 + first, 16), count)] = value

        for n, d2 in enumerate((0, 1, 3)):
            put(parts[n][slot] if slot < 2 else parts[5 + n][...], d2)
        if slot < 2:
            put(parts[3 + slot][...], 2)
        else:
            put(parts[8][...], 2, 0, 192)
            put(parts[9][...], 2, 192, 192)

    @pl.when(pipe == layer)
    def _():
        held[zhi, 0:768] = own_up[...]
        held[zhi, 768:1536] = own_down[...]
        gathered(1 - zhi, 2 * layer)

    @pl.when(pipe != layer)
    def _():
        gathered(zhi, layer)
        gathered(1 - zhi, layer + 1)


def attn_forward_body(x, small, mask_ref, held, a_ref, p_ref, o_ref, scores_ref, probs_ref, part_ref):
    unit, _ = normed(x)
    a_ref[...] = (unit * small[0:1] + small[1:2]).astype(BF)
    p_ref[...] = mt(a_ref[...], held[pl.ds(0, 1152), :]).astype(BF)
    halves = half_masks()
    for page in range(PAGES):
        rows = pl.ds(page * BLOCKS, BLOCKS)
        for pair in range(3):
            q = p_ref[rows, pl.ds(pair * 128, 128)]
            k = p_ref[rows, pl.ds(384 + pair * 128, 128)]
            for n, half in enumerate(halves):
                scores_ref[page, pair * 2 + n] = mt(q, k * half)
    for page in range(PAGES):
        allowed = mask_ref[page] > 0.5
        for head in range(6):
            scores = jnp.where(allowed, scores_ref[page, head] * SCALE, -1e30)
            expo = jnp.exp(scores - jnp.max(scores, axis=-1, keepdims=True))
            probs_ref[page, head] = (expo * (1.0 / jnp.sum(expo, axis=-1, keepdims=True))).astype(BF)
    for page in range(PAGES):
        rows = pl.ds(page * BLOCKS, BLOCKS)
        for pair in range(3):
            v = p_ref[rows, pl.ds(768 + pair * 128, 128)]
            total = mm(probs_ref[page, pair * 2], v * halves[0]) + mm(probs_ref[page, pair * 2 + 1], v * halves[1])
            o_ref[rows, pl.ds(pair * 128, 128)] = total.astype(BF)
    part_ref[...] = mm(o_ref[...], held[pl.ds(1152, 384), :]).astype(BF)


def attn_first_kernel(
    x_ref, small, mask_ref, held, p_ref, part_ref, a_ref, o_ref, scores_ref, probs_ref
):
    attn_forward_body(
        x_ref[...].astype(F32), small, mask_ref, held, a_ref, p_ref, o_ref, scores_ref, probs_ref, part_ref,
    )


def attn_second_kernel(
    mid_ref, mine, other, before, small, mask_ref, held,
    y_ref, p_ref, part_ref, a_ref, o_ref, scores_ref, probs_ref,
):
    total = mine[...].astype(F32) + other[...].astype(F32)
    y_ref[...] = (mid_ref[...] + total + before[5:6]).astype(BF)
    attn_forward_body(
        y_ref[...].astype(F32), small, mask_ref, held, a_ref, p_ref, o_ref, scores_ref, probs_ref, part_ref,
    )


def middle(x_ref, mine, other, small, mid_ref, c_ref):
    mid = x_ref[...].astype(F32) + (mine[...].astype(F32) + other[...].astype(F32)) + small[4:5]
    mid_ref[...] = mid
    unit, _ = normed(mid)
    c_ref[...] = (unit * small[2:3] + small[3:4]).astype(BF)


def gelu_parts(pre):
    cdf = 0.5 * (1.0 + lax.erf(pre * 0.7071067811865476))
    return pre * cdf, cdf + pre * (jnp.exp(-0.5 * pre * pre) * 0.3989422804014327)


def down_product(e_ref, held, part_ref):
    part_ref[...] = (
        mm(e_ref[:, pl.ds(0, 768)], held[0, pl.ds(768, 768), :])
        + mm(e_ref[:, pl.ds(768, 768)], held[1, pl.ds(768, 768), :])
    ).astype(BF)


def up_tile(n, c_ref, held, hidden):
    return mm(c_ref[...], held[n // 3, pl.ds(0, 768), pl.ds(n % 3 * 256, 256)]) + hidden[:, pl.ds(n * 256, 256)]


def ffn_first_kernel(
    x_ref, mine, other, small, hidden, held, mid_ref, pre_ref, part_ref, c_ref, e_ref
):
    middle(x_ref, mine, other, small, mid_ref, c_ref)
    for n in range(6):
        wide = pl.ds(n * 256, 256)
        pre = up_tile(n, c_ref, held, hidden)
        pre_ref[:, wide] = pre
        e_ref[:, wide] = (0.5 * pre * (1.0 + lax.erf(pre * 0.7071067811865476))).astype(BF)
    down_product(e_ref, held, part_ref)


def ffn_back_tile(n, grad, slope, held, du_ref, hidden_ref):
    wide = pl.ds(n * 256, 256)
    grad_e = mt(grad, held[n // 3, pl.ds(768 + n % 3 * 256, 256), :])
    grad_u = (grad_e * slope).astype(BF)
    du_ref[:, wide] = grad_u
    hidden_ref[:, wide] = column_sum(grad_u.astype(F32))


def ffn_back_product(du_ref, held, back_ref):
    back_ref[...] = (
        mt(du_ref[:, pl.ds(0, 768)], held[0, pl.ds(0, 768), :])
        + mt(du_ref[:, pl.ds(768, 768)], held[1, pl.ds(0, 768), :])
    ).astype(BF)


def ffn_grads_kernel(place, c_ref, du_ref, grad_ref, e_ref, g0, g1, g2, g3, total):
    turned = c_ref[...].T
    for n in range(6):
        wide = pl.ds(n * 256, 256)
        total[:, wide] = mm(turned, du_ref[:, wide]).astype(BF)
    turned = grad_ref[...].T
    for n in range(6):
        total[:, pl.ds(1536 + n * 256, 256)] = mm(turned, e_ref[:, pl.ds(n * 256, 256)]).astype(BF)
    send_blocks(place, total, (g0, g1, g2, g3))


def ffn_second_kernel(
    x_ref, mine, other, small, hidden, grad_ref, held,
    mid_ref, part_ref, back_ref, hidden_ref, c_ref, e_ref, du_ref, slope_ref,
):
    middle(x_ref, mine, other, small, mid_ref, c_ref)
    for n in range(6):
        wide = pl.ds(n * 256, 256)
        value, slope_ref[:, wide] = gelu_parts(up_tile(n, c_ref, held, hidden))
        e_ref[:, wide] = value.astype(BF)
    down_product(e_ref, held, part_ref)
    for n in range(6):
        ffn_back_tile(n, grad_ref[...], slope_ref[:, pl.ds(n * 256, 256)], held, du_ref, hidden_ref)
    ffn_back_product(du_ref, held, back_ref)


def layer_input_back(mine, other, up_grad, x_ref, small, dx_ref, sums_ref):
    grad = mine[...].astype(F32) + other[...].astype(F32)
    unit, inverse = normed(x_ref[...].astype(F32))
    sums_ref[0:1] = column_sum(grad * unit)
    sums_ref[1:2] = column_sum(grad)
    dx_ref[...] = (up_grad[...] + norm_back(grad, unit, inverse, small[0:1])).astype(BF)


def ffn_back_kernel(
    mine, other, up_grad, x_ref, small, below, mid_ref, pre_ref, held,
    dx_ref, back_ref, hidden_ref, sums_ref, c_ref, e_ref, du_ref,
):
    layer_input_back(mine, other, up_grad, x_ref, small, dx_ref, sums_ref)
    unit, _ = normed(mid_ref[...])
    c_ref[...] = (unit * below[2:3] + below[3:4]).astype(BF)
    for n in range(6):
        wide = pl.ds(n * 256, 256)
        value, slope = gelu_parts(pre_ref[:, wide])
        e_ref[:, wide] = value.astype(BF)
        ffn_back_tile(n, dx_ref[...], slope, held, du_ref, hidden_ref)
    ffn_back_product(du_ref, held, back_ref)


def last_kernel(mine, other, up_grad, x_ref, small, sums0, hidden0, first1, sums1, hidden1, dx_ref, vec):
    layer_input_back(mine, other, up_grad, x_ref, small, dx_ref, vec)
    vec[2:6] = sums0[...]
    vec[8:10] = first1[...]
    vec[10:14] = sums1[...]
    for n, part in enumerate((hidden0, hidden1)):
        vec[8 * n + 6 : 8 * n + 7] = part[:, 0:768]
        vec[8 * n + 7 : 8 * n + 8] = part[:, 768:1536]


def attn_back_kernel(layer, *refs):
    if layer == 1:
        end_mine, end_other, y_ref = refs[0], refs[1], refs[11]
        refs = refs[2:11] + refs[12:]
    (mine, other, dy_ref, mid_ref, small, mask_ref, p_ref, x_ref, held,
     dmid_ref, part_ref, sums_ref, a_ref, dr_ref, dp_ref, o_ref,
     do_ref, scores, dprobs, probs, dscores) = refs
    if layer == 1:
        y_ref[...] = (
            mid_ref[...] + (end_mine[...].astype(F32) + end_other[...].astype(F32)) + small[5:6]
        ).astype(BF)
    grad = mine[...].astype(F32) + other[...].astype(F32)
    dy = dy_ref[...].astype(F32)
    unit, inverse = normed(mid_ref[...])
    sums_ref[0:1] = column_sum(grad * unit)
    sums_ref[1:2] = column_sum(grad)
    dmid = dy + norm_back(grad, unit, inverse, small[2:3])
    dmid_ref[...] = dmid
    sums_ref[2:3] = column_sum(dmid)
    sums_ref[3:4] = column_sum(dy)
    dr_ref[...] = dmid.astype(BF)
    unit, _ = normed(x_ref[...].astype(F32))
    a_ref[...] = (unit * small[0:1] + small[1:2]).astype(BF)
    do_ref[...] = mt(dr_ref[...], held[pl.ds(1152, 384), :]).astype(BF)
    halves = half_masks()
    for page in range(PAGES):
        rows = pl.ds(page * BLOCKS, BLOCKS)
        for pair in range(3):
            q = p_ref[rows, pl.ds(pair * 128, 128)]
            k = p_ref[rows, pl.ds(384 + pair * 128, 128)]
            v = p_ref[rows, pl.ds(768 + pair * 128, 128)]
            do = do_ref[rows, pl.ds(pair * 128, 128)]
            for n, half in enumerate(halves):
                scores[page, pair * 2 + n] = mt(k * half, q)
                dprobs[page, pair * 2 + n] = mt(v * half, do)
    for page in range(PAGES):
        allowed = mask_ref[page] > 0.5
        for head in range(6):
            masked = jnp.where(allowed, scores[page, head] * SCALE, -1e30)
            expo = jnp.exp(masked - jnp.max(masked, axis=0, keepdims=True))
            share = expo * (1.0 / jnp.sum(expo, axis=0, keepdims=True))
            slope = dprobs[page, head]
            inner = jnp.sum(share * slope, axis=0, keepdims=True)
            probs[page, head] = share.astype(BF)
            dscores[page, head] = (share * (slope - inner)).astype(BF)
    for page in range(PAGES):
        rows = pl.ds(page * BLOCKS, BLOCKS)
        for pair in range(3):
            q = p_ref[rows, pl.ds(pair * 128, 128)]
            k = p_ref[rows, pl.ds(384 + pair * 128, 128)]
            v = p_ref[rows, pl.ds(768 + pair * 128, 128)]
            do = do_ref[rows, pl.ds(pair * 128, 128)]

            def both(product, left, right):
                one = product(left[page, pair * 2], right * halves[0])
                return one + product(left[page, pair * 2 + 1], right * halves[1])

            dp_ref[rows, pl.ds(pair * 128, 128)] = (both(tm, dscores, k) * SCALE).astype(BF)
            dp_ref[rows, pl.ds(384 + pair * 128, 128)] = (both(mm, dscores, q) * SCALE).astype(BF)
            dp_ref[rows, pl.ds(768 + pair * 128, 128)] = both(mm, probs, do).astype(BF)
            o_ref[rows, pl.ds(pair * 128, 128)] = both(tm, probs, v).astype(BF)
    part_ref[...] = mm(dp_ref[...], held[pl.ds(0, 1152), :]).astype(BF)


def attn_grads_kernel(place, a_ref, dp_ref, dr_ref, o_ref, near, far, later, home, total):
    turned = a_ref[...].T
    for n in range(3):
        cols = pl.ds(n * 384, 384)
        total[:, cols] = mm(turned, dp_ref[:, cols]).astype(BF)
    total[:, pl.ds(1152, 384)] = mm(dr_ref[...].T, o_ref[...]).astype(BF)
    send_z(place, total, near, far, later, home)


def added(left, right):
    return (left.astype(F32) + right.astype(F32)).astype(BF)


def added(left, right):
    return (left.astype(F32) + right.astype(F32)).astype(BF)


def arrived(home, plus, minus, total):
    half = home.shape[0] // 2
    total[0:half] = added(home[0:half], minus[0:half])
    total[half : 2 * half] = added(home[half : 2 * half], plus[half : 2 * half])


def pass_on_kernel(later, home, plus, minus, on_plus, on_minus, total):
    half = later.shape[0] // 2
    on_plus[...] = added(later[0:half], plus[0:half])
    on_minus[...] = added(later[half:], minus[half : 2 * half])
    arrived(home, plus, minus, total)


def join_kernel(plus, minus, later, home, got_plus, got_minus, out_plus, out_minus, total):
    size, half = plus.shape[0], plus.shape[0] // 2
    out_plus[0:size] = plus[...]
    out_minus[0:size] = minus[...]
    out_plus[size : size + half] = added(later[0:half], got_plus[0:half])
    out_minus[size : size + half] = added(later[half:], got_minus[half:size])
    arrived(home, got_plus, got_minus, total)


def join_z_kernel(near, far, later, home, got_near, got_far, out_near, out_far, total):
    out_near[0:768] = near[...]
    out_far[0:768] = far[...]
    out_far[768:1152] = added(later[0:384], got_near[0:384])
    out_near[768:1152] = added(later[384:768], got_far[384:768])
    total[0:384] = added(home[0:384], got_near[384:768])
    total[384:768] = added(home[384:768], got_far[0:384])


def pass_on_z_kernel(later, home, near, far, on_far, on_near, total):
    on_far[...] = added(later[0:384], near[0:384])
    on_near[...] = added(later[384:768], far[384:768])
    total[0:384] = added(home[0:384], near[384:768])
    total[384:768] = added(home[384:768], far[0:384])


def fold_kernel(place, some1, some0, plus0, minus0, last_plus, last_minus, plus, minus, later, home, total):
    total[1, 0:2] = added(some1[0:2], plus0[4:6])
    total[1, 2:4] = added(some1[2:4], minus0[4:6])
    total[0, 0:2] = added(some0[0:2], last_plus[...])
    total[0, 2:4] = added(some0[2:4], last_minus[...])

    def block(layer, d):
        return total[layer, (place[2] + d) & 3]

    plus[0], plus[1] = block(0, 2), block(1, 1)
    minus[0], minus[1] = block(0, 3), block(1, 2)
    later[0], later[1] = block(0, 1), block(1, 3)
    home[0], home[1] = block(0, 0), block(1, 0)


def put_split(out, first, value):
    count = value.shape[0]
    high = value.astype(BF)
    out[first : first + count] = high
    out[first + count : first + 2 * count] = (value - high.astype(F32)).astype(BF)


def get_split(ref, first, count):
    return ref[first : first + count].astype(F32) + ref[first + count : first + 2 * count].astype(F32)


def fold_z_kernel(place, *refs):
    some1, some0, near0, far0, last_far, last_near = refs[0:6]
    vec, outs, total = refs[6], refs[7:11], refs[11]
    total[0:384, 384:768] = added(some1[0:384], far0[768:1152])
    total[384:768, 384:768] = added(some1[384:768], near0[768:1152])
    total[0:384, 0:384] = added(some0[0:384], last_far[...])
    total[384:768, 0:384] = added(some0[384:768], last_near[...])
    for d1 in range(4):
        for j2 in range(4):
            outs[d1][j2 * 48 : j2 * 48 + 48] = total[pl.ds(row_of(place, d1, j2), 48)]
        put_split(outs[d1], 192, vec[...])


def turn_kernel(place, own, one, two, three, m0, m1, m2, m3, total, vecs):
    got = (own, one, two, three)
    total[...] = sum(r[0:192].astype(F32) for r in got).astype(BF)
    for s, r in enumerate(got):
        vecs[(place[1] - s) & 3] = get_split(r, 192, 16)
    vec = (vecs[0] + vecs[1]) + (vecs[2] + vecs[3])
    for s, out in enumerate((m0, m1, m2, m3)):
        row = pl.multiple_of(((place[2] + s) & 3) * 48, 16)
        out[0:48] = total[pl.ds(row, 48)]
        put_split(out, 48, vec)


def pack_kernel(place, *refs):
    some, last_plus, last_minus = refs[0:3]
    got, outs, staged, vecs = refs[3:7], refs[7:11], refs[11], refs[12]
    ffn0 = some[0].astype(F32) + last_plus[0].astype(F32)
    ffn1 = some[1].astype(F32) + last_minus[0].astype(F32)
    attn = sum(r[0:48].astype(F32) for r in got)
    for s, r in enumerate(got):
        vecs[(place[2] - s) & 3] = get_split(r, 48, 16)
    vec = (vecs[0] + vecs[1]) + (vecs[2] + vecs[3])
    zz = place[5]
    for half in range(2):
        for layer, ffn in ((0, ffn0), (1, ffn1)):
            to = staged.at[2 * half + layer]
            at = layer * 384 + half * 192
            for group in range(4):
                to[0:48, pl.ds(group * 192, 192)] = jnp.where(zz == group, attn[:, at : at + 192], 0.0).astype(BF)
            to[48:96] = ffn[:, half * 768 : half * 768 + 768].astype(BF)
            to[96:144] = ffn[:, 1536 + half * 768 : 1536 + half * 768 + 768].astype(BF)
            put_split(to, 144, vec[8 * layer : 8 * layer + 8])
    for k in range(4):
        outs[k][...] = staged[zz ^ k]


def finish_kernel(place, a, b, c, d, qkv_ref, out_ref, up_ref, down_ref, vec_ref, vecs):
    got = (a, b, c, d)
    total = sum(r[0:144].astype(F32) for r in got)
    for group in range(3):
        qkv_ref[group] = total[0:48, group * 192 : group * 192 + 192]
    out_ref[...] = total[0:48, 576:768]
    up_ref[...] = total[48:96]
    down_ref[...] = total[96:144]
    for k, r in enumerate(got):
        vecs[place[5] ^ k] = get_split(r, 144, 8)
    vec_ref[...] = (vecs[0] + vecs[1]) + (vecs[2] + vecs[3])


def rows_kernel(place, y0, dx0, y1, dx1, out):
    for layer, pair in enumerate(((y0, dx0), (y1, dx1))):
        for half in range(2):
            for n in range(2):
                out[2 * layer + half, n] = pair[n][2 * half + place[3]]


def by_batch_kernel(got, first, second):
    for batch, q in enumerate((0, 2, 1, 3)):
        first[batch] = got[q, 0]
        second[batch] = got[q, 1]


def small_kernel(place, mine, other, hidden_ref, gains_ref, shifts_ref, biases_ref):
    first = place[3] == 0
    low = jnp.where(first, mine[...], other[...])
    high = jnp.where(first, other[...], mine[...])
    for n, row in enumerate((low[6:7], high[6:7], low[7:8], high[7:8])):
        hidden_ref[:, n * 768 : n * 768 + 768] = row
    for n in range(2):
        gains_ref[0, n : n + 1] = low[2 * n : 2 * n + 1]
        shifts_ref[0, n : n + 1] = low[2 * n + 1 : 2 * n + 2]
    biases_ref[0] = low[4:6]


VM = pl.BlockSpec(memory_space=pltpu.VMEM)
SM = pl.BlockSpec(memory_space=pltpu.SMEM)
ANY = pl.BlockSpec(memory_space=pl.ANY)


def shape(dims, dtype):
    return jax.ShapeDtypeStruct(dims, dtype)


def call(body, ins, outs, scratch, args, limit=16, after=()):
    count, extra = len(args), len(after)
    name = getattr(body, 'func', body).__name__
    if extra:
        inner = body

        def body(*refs):
            return inner(*refs[:count], *refs[count + extra :])

        ins, args = ins + [ANY] * extra, [*args, *after]
    return pl.pallas_call(
        body,
        in_specs=ins,
        out_specs=tuple(spec for spec, _ in outs),
        out_shape=tuple(form for _, form in outs),
        scratch_shapes=scratch,
        compiler_params=pltpu.CompilerParams(vmem_limit_bytes=limit * 1024 * 1024),
        cost_estimate=pl.CostEstimate(flops=int(COSTS.get(name, 0.0) * FACTOR * 1e9) + 1024, bytes_accessed=1024, transcendentals=0),
    )(*args)


ROW_BF = (VM, shape((ROWS, D), BF))
ROW_F32 = (VM, shape((ROWS, D), F32))


def pairs_allowed(flags, valid):
    place = lax.broadcasted_iota(jnp.int32, (BLOCKS,), 0)
    visual = place >= TEXT
    dropped = (flags[:, None] == 1) & visual[None] | (flags[:, None] == 2) & ~visual[None]
    key_ok = (valid == 1) & ~dropped
    same = place[:, None] == place[None, :]
    other = visual[:, None] != visual[None, :]
    cross = same[None] | other[None] & key_ok[:, None, :]
    plain = same[None] | key_ok[:, None, :]
    masks = []
    for allowed in (cross, plain):
        allowed = allowed.astype(F32)
        masks.append((allowed, jnp.swapaxes(allowed, 1, 2)))
    return masks


def on_device(
    block_input, out_cotangent, drop_flags, key_valid, qkv_weight, out_weight, up_weight, down_weight,
    hidden_bias, norm_gains, norm_shifts, out_biases,
):
    y, x = lax.axis_index("y"), lax.axis_index("x")
    pipe, zhi, core = lax.axis_index("pipe"), lax.axis_index("zhi"), lax.axis_index("core")
    zz = 2 * zhi + pipe
    i1 = jnp.where(core == 0, x, y)
    i2 = jnp.where(core == 0, y, x)
    place = jnp.stack([pipe, i1, i2, core, zhi, zz]).astype(jnp.int32)

    packed = jnp.concatenate([
        norm_gains[0, 0:1], norm_shifts[0, 0:1], norm_gains[0, 1:2], norm_shifts[0, 1:2], out_biases[0],
        hidden_bias, jnp.zeros((1, D), F32),
    ])
    terms, rest = [], packed
    for _ in range(3):
        term = lax.reduce_precision(rest, 8, 7)
        terms.append(term.astype(BF))
        rest = rest - term
    packed_low = jnp.concatenate(terms)

    own_attn = jnp.concatenate([jnp.transpose(qkv_weight[0], (1, 2, 0)).reshape(576, D), out_weight[0]])
    own_up, own_down = up_weight[0], down_weight[0]
    number = i2 * 4 + i1
    ffn_slice = jnp.where(
        number < 8,
        lax.dynamic_slice_in_dim(own_up, (number & 7) * 96, 96),
        lax.dynamic_slice_in_dim(own_down, (number & 7) * 96, 96),
    )
    piece = jnp.concatenate([ffn_slice, packed_low])
    from_z = [piece] + [swap_z(piece, k) for k in (1, 2, 3)]
    order = jnp.where(
        pipe == 0,
        jnp.stack([from_z[k][:96] for k in (2, 1, 3)]),
        jnp.stack([from_z[k][:96] for k in (1, 3, 2)]),
    )
    level = [order] + [ring_shift(order, FIRST, 4 - d) for d in (1, 2, 3)]
    first_level, last_level = call(
        level_kernel, [SM] + [VM] * 4, [(VM, shape((2, 384, D), BF)), (VM, shape((384, D), BF))], [],
        [place, *level],
    )
    after, before = ring_shift(first_level, SECOND, 3), ring_shift(first_level, SECOND, 1)
    parts = [first_level, after, before, ring_shift(before[0], SECOND, 1), ring_shift(after[1], SECOND, 3)]
    last_level, *_ = lax.optimization_barrier((last_level, after, before))
    after, before = ring_shift(last_level, SECOND, 3), ring_shift(last_level, SECOND, 1)
    more_parts = parts + [
        last_level, after, before, ring_shift(before[:192], SECOND, 1), ring_shift(after[192:], SECOND, 3)
    ]

    given = lax.dynamic_index_in_dim(block_input, zz ^ 3, 0, keepdims=False)
    near = swap_z(own_attn, 1)
    far = swap_z(jnp.concatenate([own_attn, given]), 3)
    diagonal = [swap_z(near[:384], 3), swap_z(far[384:768], 1)]

    def whole(k):
        return sum(from_z[k][96 + 8 * n : 104 + 8 * n].astype(F32) for n in range(3))

    full = [whole(k) for k in range(4)]
    small, hidden = [], []
    for layer in range(2):
        same = jnp.where(pipe == layer, full[0], full[1])
        other = jnp.where(pipe == layer, full[2], full[3])
        small.append(same[:6])
        hidden.append(
            jnp.where(
                zhi == 0,
                jnp.concatenate([same[6:7], other[6:7]], axis=1),
                jnp.concatenate([other[6:7], same[6:7]], axis=1),
            )
        )

    drop_flags, key_valid, _ = lax.optimization_barrier((drop_flags, key_valid, level[1]))

    def all_rows(kept, came):
        halves = jnp.where(zhi == 0, jnp.stack([kept, came]), jnp.stack([came, kept]))
        across = swap_cores(halves)
        rows = jnp.where(core == 0, jnp.stack([halves, across], 1), jnp.stack([across, halves], 1))
        return rows.reshape(ROWS, D)

    x0 = all_rows(lax.dynamic_index_in_dim(block_input, zz, 0, keepdims=False), far[768:])
    out_cotangent, *_ = lax.optimization_barrier((out_cotangent, *parts[1:3]))
    cotangent = all_rows(
        lax.dynamic_index_in_dim(out_cotangent, zz, 0, keepdims=False),
        swap_z(lax.dynamic_index_in_dim(out_cotangent, zz ^ 3, 0, keepdims=False), 3),
    )
    flags = lax.dynamic_index_in_dim(drop_flags, zz, 0, keepdims=False)
    valid = lax.dynamic_index_in_dim(key_valid, zz, 0, keepdims=False)
    masks = pairs_allowed(flags, valid)

    attn_whole, ffn_whole = (VM, shape((1536, D), BF)), (VM, shape((2, 1536, D), BF))

    def join_attn(layer):
        (held,) = call(
            partial(join_attn_kernel, layer), [SM] + [VM] * 5, [attn_whole], [],
            [place, own_attn, near, *diagonal, far],
        )
        return held

    def join_ffn(layer, sources, after=()):
        (held,) = call(
            partial(join_ffn_kernel, layer), [SM] + [VM] * (2 + len(sources)), [ffn_whole], [],
            [place, own_up, own_down, *sources], after=after,
        )
        return held

    projected = (VM, shape((ROWS, 1152), BF))
    row_scratch = pltpu.VMEM((ROWS, D), BF)
    head_scratch = pltpu.VMEM((ROWS, 384), BF)
    wide_scratch = pltpu.VMEM((ROWS, 1536), BF)
    scores, probs = pltpu.VMEM((PAGES, 6, BLOCKS, BLOCKS), F32), pltpu.VMEM((PAGES, 6, BLOCKS, BLOCKS), BF)
    attn_scratch = [row_scratch, head_scratch, scores, probs]
    attn_held0, attn_held1 = join_attn(0), join_attn(1)
    p0, part = call(
        attn_first_kernel, [VM] * 4, [projected, ROW_BF], attn_scratch, [x0, small[0], masks[0][0], attn_held0]
    )
    ffn_held0 = join_ffn(0, parts)
    mid0, pre0, part = call(
        ffn_first_kernel, [VM] * 6, [ROW_F32, (VM, shape((ROWS, 1536), F32)), ROW_BF], [row_scratch, wide_scratch],
        [x0, part, swap_cores(part), small[0], hidden[0], ffn_held0],
    )
    y0, p1, part = call(
        attn_second_kernel, [VM] * 7, [ROW_BF, projected, ROW_BF], attn_scratch,
        [mid0, part, swap_cores(part), small[0], small[1], masks[1][0], attn_held1],
    )
    ffn_held1 = join_ffn(1, more_parts, [part])

    hidden_sum = (VM, shape((1, 1536), F32))
    two_sums = (VM, shape((2, D), F32))
    ring_blocks = [(VM, shape((4, 48, 3072), BF))] * 4
    z_blocks = [(VM, shape((D, 384), BF))] * 4
    ffn_total = pltpu.VMEM((D, 3072), BF)
    wide = (VM, shape((ROWS, 1536), BF))
    mid1, part, back, dhidden1, c1, e1, du1 = call(
        ffn_second_kernel, [VM] * 7, [ROW_F32, ROW_BF, ROW_BF, hidden_sum, ROW_BF, wide, wide],
        [pltpu.VMEM((ROWS, 1536), F32)],
        [y0, part, swap_cores(part), small[1], hidden[1], cotangent, ffn_held1],
    )
    plus1, minus1, later1, home1 = call(
        ffn_grads_kernel, [SM] + [VM] * 4, ring_blocks, [ffn_total], [place, c1, du1, cotangent, e1]
    )
    token = later1
    plus1, minus1 = ring_shift(plus1, FIRST, 1), ring_shift(minus1, FIRST, 3)

    back_scratch = [head_scratch, scores, scores, probs, probs]
    back_outs = [ROW_F32, ROW_BF, (VM, shape((4, D), F32)), ROW_BF, ROW_BF, projected, (VM, shape((ROWS, 384), BF))]
    y1, dmid1, back, sums1, a1, dr1, dp1, o1 = call(
        partial(attn_back_kernel, 1), [VM] * 11, [ROW_BF] + back_outs, back_scratch,
        [part, swap_cores(part), back, swap_cores(back), cotangent, mid1, small[1], masks[1][1], p1, y0,
         attn_held1], after=[token],
    )
    attn_total = [pltpu.VMEM((D, 1536), BF)]
    near1, far1, later_z1, home_z1 = call(
        attn_grads_kernel, [SM] + [VM] * 4, z_blocks, attn_total, [place, a1, dp1, dr1, o1]
    )
    token = later_z1
    near1, far1 = swap_z(near1, 1), swap_z(far1, 3)
    dx1, back, dhidden0, first1, c0, e0, du0 = call(
        ffn_back_kernel, [VM] * 9, [ROW_BF, ROW_BF, hidden_sum, two_sums, ROW_BF, wide, wide], [],
        [back, swap_cores(back), dmid1, y0, small[1], small[0], mid0, pre0, ffn_held0], after=[token],
    )
    plus0, minus0, later0, home0 = call(
        ffn_grads_kernel, [SM] + [VM] * 4, ring_blocks, [ffn_total], [place, c0, du0, dx1, e0]
    )
    six, four = [(VM, shape((6, 48, 3072), BF))] * 2, [(VM, shape((4, 48, 3072), BF))]
    plus0, minus0, some1 = call(
        join_kernel, [VM] * 6, six + four, [], [plus0, minus0, later1, home1, plus1, minus1], 20
    )
    token = some1
    plus0, minus0 = ring_shift(plus0, FIRST, 1), ring_shift(minus0, FIRST, 3)
    dmid0, back, sums0, a0, dr0, dp0, o0 = call(
        partial(attn_back_kernel, 0), [VM] * 9, back_outs, back_scratch,
        [back, swap_cores(back), dx1, mid0, small[0], masks[0][1], p0, x0, attn_held0],
        after=[token],
    )
    near0, far0, later_z0, home_z0 = call(
        attn_grads_kernel, [SM] + [VM] * 4, z_blocks, attn_total, [place, a0, dp0, dr0, o0]
    )
    tall = [(VM, shape((1152, 384), BF))] * 2
    near0, far0, some_z1 = call(
        join_z_kernel, [VM] * 6, tall + z_blocks[:1], [], [near0, far0, later_z1, home_z1, near1, far1]
    )
    token = some_z1
    near0, far0 = swap_z(near0, 1), swap_z(far0, 3)
    dx0, vec = call(
        last_kernel, [VM] * 10, [ROW_BF, (VM, shape((16, D), F32))], [],
        [back, swap_cores(back), dmid0, x0, small[0], sums0, dhidden0, first1, sums1, dhidden1], after=[token],
    )

    pair, one = [(VM, shape((2, 48, 3072), BF))], [(VM, shape((1, 48, 3072), BF))]
    on_plus, on_minus, some0 = call(
        pass_on_kernel, [VM] * 4, pair * 2 + four, [], [later0, home0, plus0, minus0], after=[vec]
    )
    last_plus, last_minus = ring_shift(on_plus, FIRST, 1), ring_shift(on_minus, FIRST, 3)
    half = [(VM, shape((384, 384), BF))]
    on_far, on_near, some_z0 = call(
        pass_on_z_kernel, [VM] * 4, half * 2 + z_blocks[:1], [], [later_z0, home_z0, near0, far0], after=[some0]
    )
    last_far, last_near = swap_z(on_far, 3), swap_z(on_near, 1)
    plus, minus, later, home = call(
        fold_kernel, [SM] + [VM] * 6, pair * 4, [pltpu.VMEM((2, 4, 48, 3072), BF)],
        [place, some1, some0, plus0, minus0, last_plus, last_minus], after=[some_z0],
    )
    plus, minus = ring_shift(plus, SECOND, 1), ring_shift(minus, SECOND, 3)
    turned = call(
        fold_z_kernel, [SM] + [VM] * 7, [(VM, shape((224, D), BF))] * 4, [pltpu.VMEM((D, D), BF)],
        [place, some_z1, some_z0, near0, far0, last_far, last_near, vec], after=[home],
    )
    token = turned[0]
    on_plus, on_minus, some = call(
        pass_on_kernel, [VM] * 4, one * 2 + pair, [], [later, home, plus, minus], after=[turned[0]]
    )
    last_plus, last_minus = ring_shift(on_plus, SECOND, 1), ring_shift(on_minus, SECOND, 3)
    turned = call(
        turn_kernel, [SM] + [VM] * 4, [(VM, shape((80, D), BF))] * 4,
        [pltpu.VMEM((192, D), BF), pltpu.VMEM((4, 16, D), F32)],
        [place, turned[0]] + [ring_shift(turned[s], FIRST, s) for s in (1, 2, 3)],
        after=[some],
    )
    turned = [turned[0]] + [ring_shift(turned[s], SECOND, s) for s in (1, 2, 3)]
    packs = call(
        pack_kernel, [SM] + [VM] * 7, [(VM, shape((160, D), BF))] * 4,
        [pltpu.VMEM((4, 160, D), BF), pltpu.VMEM((4, 16, D), F32)], [place, some, last_plus, last_minus, *turned],
    )
    grad_qkv, grad_out, grad_up, grad_down, vec = call(
        finish_kernel, [SM] + [VM] * 4,
        [(VM, shape((3, 48, 192), F32)), (VM, shape((48, 192), F32))] + [(VM, shape((48, D), F32))] * 2
        + [(VM, shape((8, D), F32))], [pltpu.VMEM((4, 8, D), F32)],
        [place, packs[0]] + [swap_z(packs[k], k) for k in (1, 2, 3)],
    )
    grad_qkv = jnp.transpose(grad_qkv, (1, 0, 2))
    grad_out, grad_down = grad_out.T, grad_down.T
    grad_hidden, grad_gains, grad_shifts, grad_biases = call(
        small_kernel, [SM] + [VM] * 2, [(VM, shape((1, 4 * D), F32))] + [(VM, shape((1, 2, D), F32))] * 3, [],
        [place, vec, swap_cores(vec)],
    )

    quarters = [value.reshape(4, 72, D) for value in (y0, dx0, y1, dx1)]
    (rows,) = call(
        rows_kernel, [SM] + [VM] * 4, [(VM, shape((4, 2, 72, D), BF))], [], [place, *quarters], after=[token]
    )
    activations, input_grads = call(
        by_batch_kernel, [VM], [(VM, shape((4, 72, D), BF))] * 2, [], [exchange_z(rows)]
    )
    return (
        activations[None],
        input_grads[None],
        grad_qkv[None],
        grad_out[None],
        grad_up[None],
        grad_down[None],
        grad_hidden,
        grad_gains,
        grad_shifts,
        grad_biases,
    )


def solution(mesh):
    fine = Mesh(mesh.devices.reshape(4, 4, 2, 2, 2), MESH_AXES)
    rows = DP + TENSOR
    in_specs = (
        P(None, rows, None),
        P(None, rows, None),
        P(None, DP),
        P(None, DP, None),
        P("pipe", None, None, TENSOR),
        P("pipe", TENSOR, None),
        P("pipe", None, TENSOR),
        P("pipe", TENSOR, None),
        P("pipe", TENSOR),
        P("pipe", None, None),
        P("pipe", None, None),
        P("pipe", None, None),
    )
    out_specs = (
        P("pipe", None, rows, None),
        P("pipe", None, rows, None),
        P("pipe", DP, None, TENSOR),
        P("pipe", TENSOR, DP),
        P("pipe", DP, TENSOR),
        P("pipe", TENSOR, DP),
        P("pipe", None),
        P("pipe", None, None),
        P("pipe", None, None),
        P("pipe", None, None),
    )
    return jax.shard_map(on_device, mesh=fine, in_specs=in_specs, out_specs=out_specs, check_vma=False)
```

```python
from functools import partial

import jax
import jax.numpy as jnp
from jax import lax
from jax.experimental import pallas as pl
from jax.experimental.pallas import tpu as pltpu
from jax.sharding import Mesh
from jax.sharding import PartitionSpec as P

BF = jnp.bfloat16
F32 = jnp.float32
D = 768
BLOCKS = 96
TEXT = 72
ROWS = 288
PAGES = 3
SCALE = 0.125
FACTOR = 3.0
COSTS = {'fold_z_kernel': 3, 'pass_on_kernel': 1, 'fold_kernel': 0.7, 'turn_kernel': 0.7, 'pack_kernel': 0.7, 'last_kernel': 0.7, 'join_kernel': 0.7, 'join_ffn_kernel': 3, 'level_kernel': 0.7, 'ffn_first_kernel': 2.3, 'attn_second_kernel': 2.4, 'ffn_second_kernel': 3.8, 'ffn_grads_kernel': 3.5, 'attn_back_kernel': 3.7, 'attn_grads_kernel': 2.4, 'ffn_back_kernel': 3.0}

MESH_AXES = ("y", "x", "pipe", "zhi", "core")
DP = ("y", "x")
TENSOR = ("zhi", "core")


def swap_cores(value):
    return lax.ppermute(value, "core", [(0, 1), (1, 0)])


def swap_z(value, k):
    pairs = []
    for p in range(2):
        for h in range(2):
            other = (2 * h + p) ^ k
            pairs.append((p * 2 + h, (other & 1) * 2 + (other >> 1)))
    return lax.ppermute(value, ("pipe", "zhi"), pairs)


def exchange_z(value):
    return lax.all_to_all(value, ("pipe", "zhi"), 0, 0, tiled=True)


def ring_shift(value, axis_of_core, shift):
    pairs = []
    for y in range(4):
        for x in range(4):
            for c in range(2):
                if axis_of_core[c] == "x":
                    to = (y, (x + shift) % 4)
                else:
                    to = ((y + shift) % 4, x)
                pairs.append(((y * 4 + x) * 2 + c, (to[0] * 4 + to[1]) * 2 + c))
    return lax.ppermute(value, ("y", "x", "core"), pairs)


FIRST = ("x", "y")
SECOND = ("y", "x")


def mm(a, b):
    return lax.dot_general(a, b, (((1,), (0,)), ((), ())), preferred_element_type=F32)


def mt(a, b):
    return lax.dot_general(a, b, (((1,), (1,)), ((), ())), preferred_element_type=F32)


def tm(a, b):
    return lax.dot_general(a, b, (((0,), (0,)), ((), ())), preferred_element_type=F32)


def normed(values):
    centre = values - jnp.mean(values, axis=-1, keepdims=True)
    spread = jnp.mean(centre * centre, axis=-1, keepdims=True)
    inverse = lax.rsqrt(spread + 1e-05)
    return centre * inverse, inverse


def norm_back(grad, unit, inverse, gain):
    scaled = grad * gain
    mean_one = jnp.mean(scaled, axis=-1, keepdims=True)
    mean_two = jnp.mean(scaled * unit, axis=-1, keepdims=True)
    return inverse * (scaled - mean_one - unit * mean_two)


def column_sum(values):
    return jnp.sum(values, axis=0, keepdims=True)


def half_masks():
    lane = lax.broadcasted_iota(jnp.int32, (1, 128), 1)
    low = (lane < 64).astype(F32)
    return low.astype(BF), (1.0 - low).astype(BF)


def ring_slot(d1, j2):
    if d1 == 0:
        return 3
    if d1 == 2:
        return 0 if j2 < 2 else 1
    if d1 == 1:
        return 2 if j2 < 2 else 0
    return 1 if j2 < 2 else 2


def row_of(place, d1, j2):
    step1 = jnp.where(place[3] == 0, 48, 192)
    step2 = jnp.where(place[3] == 0, 192, 48)
    return pl.multiple_of(((place[1] + d1) & 3) * step1 + j2 * step2, 16)


def send_blocks(place, total, outs):
    for d1 in range(4):
        for j2 in range(4):
            outs[ring_slot(d1, j2)][j2] = total[pl.ds(row_of(place, d1, j2), 48), :]


def send_z(place, total, near, far, later, home):
    for k in range(4):
        cols = pl.ds(pl.multiple_of((place[5] ^ k) * 384, 128), 384)
        top, low = total[pl.ds(0, 384), cols], total[pl.ds(384, 384), cols]
        if k == 0:
            home[0:384], home[384:768] = top, low
        elif k == 1:
            near[384:768], later[384:768] = top, low
        elif k == 2:
            near[0:384], far[384:768] = top, low
        else:
            later[0:384], far[0:384] = top, low


def level_kernel(place, own, one, two, three, first, last):
    for d, source in enumerate((own, one, two, three)):
        rows = pl.ds(pl.multiple_of(((place[1] + d) & 3) * 96, 16), 96)
        first[0, rows] = source[0]
        first[1, rows] = source[1]
        last[rows] = source[2]


def join_attn_kernel(layer, place, own, near, across, over, far, held):
    pipe, zhi = place[0], place[4]

    def put(group, half, value):
        held[pl.ds(pl.multiple_of(group * 384 + half * 192, 16), 192)] = value

    @pl.when(pipe == layer)
    def _():
        for group in range(4):
            put(group, zhi, own[group * 192 : group * 192 + 192])
            from_two = across if group < 2 else over
            put(group, 1 - zhi, from_two[group % 2 * 192 : group % 2 * 192 + 192])

    @pl.when(pipe != layer)
    def _():
        for group in range(4):
            put(group, zhi, near[group * 192 : group * 192 + 192])
            put(group, 1 - zhi, far[group * 192 : group * 192 + 192])


def join_ffn_kernel(layer, place, own_up, own_down, *refs):
    parts, held = refs[:-1], refs[-1]
    pipe, i2, zhi = place[0], place[2], place[4]

    def gathered(half, slot):
        def put(value, d2, first=0, count=384):
            held[half, pl.ds(pl.multiple_of(((i2 + d2) & 3) * 384 + first, 16), count)] = value

        for n, d2 in enumerate((0, 1, 3)):
            put(parts[n][slot] if slot < 2 else parts[5 + n][...], d2)
        if slot < 2:
            put(parts[3 + slot][...], 2)
        else:
            put(parts[8][...], 2, 0, 192)
            put(parts[9][...], 2, 192, 192)

    @pl.when(pipe == layer)
    def _():
        held[zhi, 0:768] = own_up[...]
        held[zhi, 768:1536] = own_down[...]
        gathered(1 - zhi, 2 * layer)

    @pl.when(pipe != layer)
    def _():
        gathered(zhi, layer)
        gathered(1 - zhi, layer + 1)


def attn_forward_body(x, small, mask_ref, held, a_ref, p_ref, o_ref, scores_ref, probs_ref, part_ref):
    unit, _ = normed(x)
    a_ref[...] = (unit * small[0:1] + small[1:2]).astype(BF)
    p_ref[...] = mt(a_ref[...], held[pl.ds(0, 1152), :]).astype(BF)
    halves = half_masks()
    for page in range(PAGES):
        rows = pl.ds(page * BLOCKS, BLOCKS)
        for pair in range(3):
            q = p_ref[rows, pl.ds(pair * 128, 128)]
            k = p_ref[rows, pl.ds(384 + pair * 128, 128)]
            for n, half in enumerate(halves):
                scores_ref[page, pair * 2 + n] = mt(q, k * half)
    for page in range(PAGES):
        allowed = mask_ref[page] > 0.5
        for head in range(6):
            scores = jnp.where(allowed, scores_ref[page, head] * SCALE, -1e30)
            expo = jnp.exp(scores - jnp.max(scores, axis=-1, keepdims=True))
            probs_ref[page, head] = (expo * (1.0 / jnp.sum(expo, axis=-1, keepdims=True))).astype(BF)
    for page in range(PAGES):
        rows = pl.ds(page * BLOCKS, BLOCKS)
        for pair in range(3):
            v = p_ref[rows, pl.ds(768 + pair * 128, 128)]
            total = mm(probs_ref[page, pair * 2], v * halves[0]) + mm(probs_ref[page, pair * 2 + 1], v * halves[1])
            o_ref[rows, pl.ds(pair * 128, 128)] = total.astype(BF)
    part_ref[...] = mm(o_ref[...], held[pl.ds(1152, 384), :]).astype(BF)


def attn_first_kernel(
    x_ref, small, mask_ref, held, p_ref, part_ref, a_ref, o_ref, scores_ref, probs_ref
):
    attn_forward_body(
        x_ref[...].astype(F32), small, mask_ref, held, a_ref, p_ref, o_ref, scores_ref, probs_ref, part_ref,
    )


def attn_second_kernel(
    mid_ref, mine, other, before, small, mask_ref, held,
    y_ref, p_ref, part_ref, a_ref, o_ref, scores_ref, probs_ref,
):
    total = mine[...].astype(F32) + other[...].astype(F32)
    y_ref[...] = (mid_ref[...] + total + before[5:6]).astype(BF)
    attn_forward_body(
        y_ref[...].astype(F32), small, mask_ref, held, a_ref, p_ref, o_ref, scores_ref, probs_ref, part_ref,
    )


def middle(x_ref, mine, other, small, mid_ref, c_ref):
    mid = x_ref[...].astype(F32) + (mine[...].astype(F32) + other[...].astype(F32)) + small[4:5]
    mid_ref[...] = mid
    unit, _ = normed(mid)
    c_ref[...] = (unit * small[2:3] + small[3:4]).astype(BF)


def gelu_parts(pre):
    cdf = 0.5 * (1.0 + lax.erf(pre * 0.7071067811865476))
    return pre * cdf, cdf + pre * (jnp.exp(-0.5 * pre * pre) * 0.3989422804014327)


def down_product(e_ref, held, part_ref):
    part_ref[...] = (
        mm(e_ref[:, pl.ds(0, 768)], held[0, pl.ds(768, 768), :])
        + mm(e_ref[:, pl.ds(768, 768)], held[1, pl.ds(768, 768), :])
    ).astype(BF)


def up_tile(n, c_ref, held, hidden):
    return mm(c_ref[...], held[n // 3, pl.ds(0, 768), pl.ds(n % 3 * 256, 256)]) + hidden[:, pl.ds(n * 256, 256)]


def ffn_first_kernel(
    x_ref, mine, other, small, hidden, held, mid_ref, pre_ref, part_ref, c_ref, e_ref
):
    middle(x_ref, mine, other, small, mid_ref, c_ref)
    for n in range(6):
        wide = pl.ds(n * 256, 256)
        pre = up_tile(n, c_ref, held, hidden)
        pre_ref[:, wide] = pre
        e_ref[:, wide] = (0.5 * pre * (1.0 + lax.erf(pre * 0.7071067811865476))).astype(BF)
    down_product(e_ref, held, part_ref)


def ffn_back_tile(n, grad, slope, held, du_ref, hidden_ref):
    wide = pl.ds(n * 256, 256)
    grad_e = mt(grad, held[n // 3, pl.ds(768 + n % 3 * 256, 256), :])
    grad_u = (grad_e * slope).astype(BF)
    du_ref[:, wide] = grad_u
    hidden_ref[:, wide] = column_sum(grad_u.astype(F32))


def ffn_back_product(du_ref, held, back_ref):
    back_ref[...] = (
        mt(du_ref[:, pl.ds(0, 768)], held[0, pl.ds(0, 768), :])
        + mt(du_ref[:, pl.ds(768, 768)], held[1, pl.ds(0, 768), :])
    ).astype(BF)


def ffn_grads_kernel(place, c_ref, du_ref, grad_ref, e_ref, g0, g1, g2, g3, total):
    turned = c_ref[...].T
    for n in range(6):
        wide = pl.ds(n * 256, 256)
        total[:, wide] = mm(turned, du_ref[:, wide]).astype(BF)
    turned = grad_ref[...].T
    for n in range(6):
        total[:, pl.ds(1536 + n * 256, 256)] = mm(turned, e_ref[:, pl.ds(n * 256, 256)]).astype(BF)
    send_blocks(place, total, (g0, g1, g2, g3))


def ffn_second_kernel(
    x_ref, mine, other, small, hidden, grad_ref, held,
    mid_ref, part_ref, back_ref, hidden_ref, c_ref, e_ref, du_ref, slope_ref,
):
    middle(x_ref, mine, other, small, mid_ref, c_ref)
    for n in range(6):
        wide = pl.ds(n * 256, 256)
        value, slope_ref[:, wide] = gelu_parts(up_tile(n, c_ref, held, hidden))
        e_ref[:, wide] = value.astype(BF)
    down_product(e_ref, held, part_ref)
    for n in range(6):
        ffn_back_tile(n, grad_ref[...], slope_ref[:, pl.ds(n * 256, 256)], held, du_ref, hidden_ref)
    ffn_back_product(du_ref, held, back_ref)


def layer_input_back(mine, other, up_grad, x_ref, small, dx_ref, sums_ref):
    grad = mine[...].astype(F32) + other[...].astype(F32)
    unit, inverse = normed(x_ref[...].astype(F32))
    sums_ref[0:1] = column_sum(grad * unit)
    sums_ref[1:2] = column_sum(grad)
    dx_ref[...] = (up_grad[...] + norm_back(grad, unit, inverse, small[0:1])).astype(BF)


def ffn_back_kernel(
    mine, other, up_grad, x_ref, small, below, mid_ref, pre_ref, held,
    dx_ref, back_ref, hidden_ref, sums_ref, c_ref, e_ref, du_ref,
):
    layer_input_back(mine, other, up_grad, x_ref, small, dx_ref, sums_ref)
    unit, _ = normed(mid_ref[...])
    c_ref[...] = (unit * below[2:3] + below[3:4]).astype(BF)
    for n in range(6):
        wide = pl.ds(n * 256, 256)
        value, slope = gelu_parts(pre_ref[:, wide])
        e_ref[:, wide] = value.astype(BF)
        ffn_back_tile(n, dx_ref[...], slope, held, du_ref, hidden_ref)
    ffn_back_product(du_ref, held, back_ref)


def last_kernel(mine, other, up_grad, x_ref, small, sums0, hidden0, first1, sums1, hidden1, dx_ref, vec):
    layer_input_back(mine, other, up_grad, x_ref, small, dx_ref, vec)
    vec[2:6] = sums0[...]
    vec[8:10] = first1[...]
    vec[10:14] = sums1[...]
    for n, part in enumerate((hidden0, hidden1)):
        vec[8 * n + 6 : 8 * n + 7] = part[:, 0:768]
        vec[8 * n + 7 : 8 * n + 8] = part[:, 768:1536]


def attn_back_kernel(layer, *refs):
    if layer == 1:
        end_mine, end_other, y_ref = refs[0], refs[1], refs[11]
        refs = refs[2:11] + refs[12:]
    (mine, other, dy_ref, mid_ref, small, mask_ref, p_ref, x_ref, held,
     dmid_ref, part_ref, sums_ref, a_ref, dr_ref, dp_ref, o_ref,
     do_ref, scores, dprobs, probs, dscores) = refs
    if layer == 1:
        y_ref[...] = (
            mid_ref[...] + (end_mine[...].astype(F32) + end_other[...].astype(F32)) + small[5:6]
        ).astype(BF)
    grad = mine[...].astype(F32) + other[...].astype(F32)
    dy = dy_ref[...].astype(F32)
    unit, inverse = normed(mid_ref[...])
    sums_ref[0:1] = column_sum(grad * unit)
    sums_ref[1:2] = column_sum(grad)
    dmid = dy + norm_back(grad, unit, inverse, small[2:3])
    dmid_ref[...] = dmid
    sums_ref[2:3] = column_sum(dmid)
    sums_ref[3:4] = column_sum(dy)
    dr_ref[...] = dmid.astype(BF)
    unit, _ = normed(x_ref[...].astype(F32))
    a_ref[...] = (unit * small[0:1] + small[1:2]).astype(BF)
    do_ref[...] = mt(dr_ref[...], held[pl.ds(1152, 384), :]).astype(BF)
    halves = half_masks()
    for page in range(PAGES):
        rows = pl.ds(page * BLOCKS, BLOCKS)
        for pair in range(3):
            q = p_ref[rows, pl.ds(pair * 128, 128)]
            k = p_ref[rows, pl.ds(384 + pair * 128, 128)]
            v = p_ref[rows, pl.ds(768 + pair * 128, 128)]
            do = do_ref[rows, pl.ds(pair * 128, 128)]
            for n, half in enumerate(halves):
                scores[page, pair * 2 + n] = mt(k * half, q)
                dprobs[page, pair * 2 + n] = mt(v * half, do)
    for page in range(PAGES):
        allowed = mask_ref[page] > 0.5
        for head in range(6):
            masked = jnp.where(allowed, scores[page, head] * SCALE, -1e30)
            expo = jnp.exp(masked - jnp.max(masked, axis=0, keepdims=True))
            share = expo * (1.0 / jnp.sum(expo, axis=0, keepdims=True))
            slope = dprobs[page, head]
            inner = jnp.sum(share * slope, axis=0, keepdims=True)
            probs[page, head] = share.astype(BF)
            dscores[page, head] = (share * (slope - inner)).astype(BF)
    for page in range(PAGES):
        rows = pl.ds(page * BLOCKS, BLOCKS)
        for pair in range(3):
            q = p_ref[rows, pl.ds(pair * 128, 128)]
            k = p_ref[rows, pl.ds(384 + pair * 128, 128)]
            v = p_ref[rows, pl.ds(768 + pair * 128, 128)]
            do = do_ref[rows, pl.ds(pair * 128, 128)]

            def both(product, left, right):
                one = product(left[page, pair * 2], right * halves[0])
                return one + product(left[page, pair * 2 + 1], right * halves[1])

            dp_ref[rows, pl.ds(pair * 128, 128)] = (both(tm, dscores, k) * SCALE).astype(BF)
            dp_ref[rows, pl.ds(384 + pair * 128, 128)] = (both(mm, dscores, q) * SCALE).astype(BF)
            dp_ref[rows, pl.ds(768 + pair * 128, 128)] = both(mm, probs, do).astype(BF)
            o_ref[rows, pl.ds(pair * 128, 128)] = both(tm, probs, v).astype(BF)
    part_ref[...] = mm(dp_ref[...], held[pl.ds(0, 1152), :]).astype(BF)


def attn_grads_kernel(place, a_ref, dp_ref, dr_ref, o_ref, near, far, later, home, total):
    turned = a_ref[...].T
    for n in range(3):
        cols = pl.ds(n * 384, 384)
        total[:, cols] = mm(turned, dp_ref[:, cols]).astype(BF)
    total[:, pl.ds(1152, 384)] = mm(dr_ref[...].T, o_ref[...]).astype(BF)
    send_z(place, total, near, far, later, home)


def added(left, right):
    return (left.astype(F32) + right.astype(F32)).astype(BF)


def added(left, right):
    return (left.astype(F32) + right.astype(F32)).astype(BF)


def arrived(home, plus, minus, total):
    half = home.shape[0] // 2
    total[0:half] = added(home[0:half], minus[0:half])
    total[half : 2 * half] = added(home[half : 2 * half], plus[half : 2 * half])


def pass_on_kernel(later, home, plus, minus, on_plus, on_minus, total):
    half = later.shape[0] // 2
    on_plus[...] = added(later[0:half], plus[0:half])
    on_minus[...] = added(later[half:], minus[half : 2 * half])
    arrived(home, plus, minus, total)


def join_kernel(plus, minus, later, home, got_plus, got_minus, out_plus, out_minus, total):
    size, half = plus.shape[0], plus.shape[0] // 2
    out_plus[0:size] = plus[...]
    out_minus[0:size] = minus[...]
    out_plus[size : size + half] = added(later[0:half], got_plus[0:half])
    out_minus[size : size + half] = added(later[half:], got_minus[half:size])
    arrived(home, got_plus, got_minus, total)


def join_z_kernel(near, far, later, home, got_near, got_far, out_near, out_far, total):
    out_near[0:768] = near[...]
    out_far[0:768] = far[...]
    out_far[768:1152] = added(later[0:384], got_near[0:384])
    out_near[768:1152] = added(later[384:768], got_far[384:768])
    total[0:384] = added(home[0:384], got_near[384:768])
    total[384:768] = added(home[384:768], got_far[0:384])


def pass_on_z_kernel(later, home, near, far, on_far, on_near, total):
    on_far[...] = added(later[0:384], near[0:384])
    on_near[...] = added(later[384:768], far[384:768])
    total[0:384] = added(home[0:384], near[384:768])
    total[384:768] = added(home[384:768], far[0:384])


def fold_kernel(place, some1, some0, plus0, minus0, last_plus, last_minus, plus, minus, later, home, total):
    total[1, 0:2] = added(some1[0:2], plus0[4:6])
    total[1, 2:4] = added(some1[2:4], minus0[4:6])
    total[0, 0:2] = added(some0[0:2], last_plus[...])
    total[0, 2:4] = added(some0[2:4], last_minus[...])

    def block(layer, d):
        return total[layer, (place[2] + d) & 3]

    plus[0], plus[1] = block(0, 2), block(1, 1)
    minus[0], minus[1] = block(0, 3), block(1, 2)
    later[0], later[1] = block(0, 1), block(1, 3)
    home[0], home[1] = block(0, 0), block(1, 0)


def put_split(out, first, value):
    count = value.shape[0]
    high = value.astype(BF)
    out[first : first + count] = high
    out[first + count : first + 2 * count] = (value - high.astype(F32)).astype(BF)


def get_split(ref, first, count):
    return ref[first : first + count].astype(F32) + ref[first + count : first + 2 * count].astype(F32)


def fold_z_kernel(place, *refs):
    some1, some0, near0, far0, last_far, last_near = refs[0:6]
    vec, outs, total = refs[6], refs[7:11], refs[11]
    total[0:384, 384:768] = added(some1[0:384], far0[768:1152])
    total[384:768, 384:768] = added(some1[384:768], near0[768:1152])
    total[0:384, 0:384] = added(some0[0:384], last_far[...])
    total[384:768, 0:384] = added(some0[384:768], last_near[...])
    for d1 in range(4):
        for j2 in range(4):
            outs[d1][j2 * 48 : j2 * 48 + 48] = total[pl.ds(row_of(place, d1, j2), 48)]
        put_split(outs[d1], 192, vec[...])


def turn_kernel(place, own, one, two, three, m0, m1, m2, m3, total, vecs):
    got = (own, one, two, three)
    total[...] = sum(r[0:192].astype(F32) for r in got).astype(BF)
    for s, r in enumerate(got):
        vecs[(place[1] - s) & 3] = get_split(r, 192, 16)
    vec = (vecs[0] + vecs[1]) + (vecs[2] + vecs[3])
    for s, out in enumerate((m0, m1, m2, m3)):
        row = pl.multiple_of(((place[2] + s) & 3) * 48, 16)
        out[0:48] = total[pl.ds(row, 48)]
        put_split(out, 48, vec)


def pack_kernel(place, *refs):
    some, last_plus, last_minus = refs[0:3]
    got, outs, staged, vecs = refs[3:7], refs[7:11], refs[11], refs[12]
    ffn0 = some[0].astype(F32) + last_plus[0].astype(F32)
    ffn1 = some[1].astype(F32) + last_minus[0].astype(F32)
    attn = sum(r[0:48].astype(F32) for r in got)
    for s, r in enumerate(got):
        vecs[(place[2] - s) & 3] = get_split(r, 48, 16)
    vec = (vecs[0] + vecs[1]) + (vecs[2] + vecs[3])
    zz = place[5]
    for half in range(2):
        for layer, ffn in ((0, ffn0), (1, ffn1)):
            to = staged.at[2 * half + layer]
            at = layer * 384 + half * 192
            for group in range(4):
                to[0:48, pl.ds(group * 192, 192)] = jnp.where(zz == group, attn[:, at : at + 192], 0.0).astype(BF)
            to[48:96] = ffn[:, half * 768 : half * 768 + 768].astype(BF)
            to[96:144] = ffn[:, 1536 + half * 768 : 1536 + half * 768 + 768].astype(BF)
            put_split(to, 144, vec[8 * layer : 8 * layer + 8])
    for k in range(4):
        outs[k][...] = staged[zz ^ k]


def finish_kernel(place, a, b, c, d, qkv_ref, out_ref, up_ref, down_ref, vec_ref, vecs):
    got = (a, b, c, d)
    total = sum(r[0:144].astype(F32) for r in got)
    for group in range(3):
        qkv_ref[group] = total[0:48, group * 192 : group * 192 + 192]
    out_ref[...] = total[0:48, 576:768]
    up_ref[...] = total[48:96]
    down_ref[...] = total[96:144]
    for k, r in enumerate(got):
        vecs[place[5] ^ k] = get_split(r, 144, 8)
    vec_ref[...] = (vecs[0] + vecs[1]) + (vecs[2] + vecs[3])


def rows_kernel(place, y0, dx0, y1, dx1, out):
    for layer, pair in enumerate(((y0, dx0), (y1, dx1))):
        for half in range(2):
            for n in range(2):
                out[2 * layer + half, n] = pair[n][2 * half + place[3]]


def by_batch_kernel(got, first, second):
    for batch, q in enumerate((0, 2, 1, 3)):
        first[batch] = got[q, 0]
        second[batch] = got[q, 1]


def small_kernel(place, mine, other, hidden_ref, gains_ref, shifts_ref, biases_ref):
    first = place[3] == 0
    low = jnp.where(first, mine[...], other[...])
    high = jnp.where(first, other[...], mine[...])
    for n, row in enumerate((low[6:7], high[6:7], low[7:8], high[7:8])):
        hidden_ref[:, n * 768 : n * 768 + 768] = row
    for n in range(2):
        gains_ref[0, n : n + 1] = low[2 * n : 2 * n + 1]
        shifts_ref[0, n : n + 1] = low[2 * n + 1 : 2 * n + 2]
    biases_ref[0] = low[4:6]


VM = pl.BlockSpec(memory_space=pltpu.VMEM)
SM = pl.BlockSpec(memory_space=pltpu.SMEM)
ANY = pl.BlockSpec(memory_space=pl.ANY)


def shape(dims, dtype):
    return jax.ShapeDtypeStruct(dims, dtype)


def call(body, ins, outs, scratch, args, limit=16, after=()):
    count, extra = len(args), len(after)
    name = getattr(body, 'func', body).__name__
    if extra:
        inner = body

        def body(*refs):
            return inner(*refs[:count], *refs[count + extra :])

        ins, args = ins + [ANY] * extra, [*args, *after]
    return pl.pallas_call(
        body,
        in_specs=ins,
        out_specs=tuple(spec for spec, _ in outs),
        out_shape=tuple(form for _, form in outs),
        scratch_shapes=scratch,
        compiler_params=pltpu.CompilerParams(vmem_limit_bytes=limit * 1024 * 1024),
        cost_estimate=pl.CostEstimate(flops=int(COSTS.get(name, 0.0) * FACTOR * 1e9) + 1024, bytes_accessed=1024, transcendentals=0),
    )(*args)


ROW_BF = (VM, shape((ROWS, D), BF))
ROW_F32 = (VM, shape((ROWS, D), F32))


def pairs_allowed(flags, valid):
    place = lax.broadcasted_iota(jnp.int32, (BLOCKS,), 0)
    visual = place >= TEXT
    dropped = (flags[:, None] == 1) & visual[None] | (flags[:, None] == 2) & ~visual[None]
    key_ok = (valid == 1) & ~dropped
    same = place[:, None] == place[None, :]
    other = visual[:, None] != visual[None, :]
    cross = same[None] | other[None] & key_ok[:, None, :]
    plain = same[None] | key_ok[:, None, :]
    masks = []
    for allowed in (cross, plain):
        allowed = allowed.astype(F32)
        masks.append((allowed, jnp.swapaxes(allowed, 1, 2)))
    return masks


def on_device(
    block_input, out_cotangent, drop_flags, key_valid, qkv_weight, out_weight, up_weight, down_weight,
    hidden_bias, norm_gains, norm_shifts, out_biases,
):
    y, x = lax.axis_index("y"), lax.axis_index("x")
    pipe, zhi, core = lax.axis_index("pipe"), lax.axis_index("zhi"), lax.axis_index("core")
    zz = 2 * zhi + pipe
    i1 = jnp.where(core == 0, x, y)
    i2 = jnp.where(core == 0, y, x)
    place = jnp.stack([pipe, i1, i2, core, zhi, zz]).astype(jnp.int32)

    packed = jnp.concatenate([
        norm_gains[0, 0:1], norm_shifts[0, 0:1], norm_gains[0, 1:2], norm_shifts[0, 1:2], out_biases[0],
        hidden_bias, jnp.zeros((1, D), F32),
    ])
    terms, rest = [], packed
    for _ in range(3):
        term = lax.reduce_precision(rest, 8, 7)
        terms.append(term.astype(BF))
        rest = rest - term
    packed_low = jnp.concatenate(terms)

    own_attn = jnp.concatenate([jnp.transpose(qkv_weight[0], (1, 2, 0)).reshape(576, D), out_weight[0]])
    own_up, own_down = up_weight[0], down_weight[0]
    number = i2 * 4 + i1
    ffn_slice = jnp.where(
        number < 8,
        lax.dynamic_slice_in_dim(own_up, (number & 7) * 96, 96),
        lax.dynamic_slice_in_dim(own_down, (number & 7) * 96, 96),
    )
    piece = jnp.concatenate([ffn_slice, packed_low])
    from_z = [piece] + [swap_z(piece, k) for k in (1, 2, 3)]
    order = jnp.where(
        pipe == 0,
        jnp.stack([from_z[k][:96] for k in (2, 1, 3)]),
        jnp.stack([from_z[k][:96] for k in (1, 3, 2)]),
    )
    level = [order] + [ring_shift(order, FIRST, 4 - d) for d in (1, 2, 3)]
    first_level, last_level = call(
        level_kernel, [SM] + [VM] * 4, [(VM, shape((2, 384, D), BF)), (VM, shape((384, D), BF))], [],
        [place, *level],
    )
    after, before = ring_shift(first_level, SECOND, 3), ring_shift(first_level, SECOND, 1)
    parts = [first_level, after, before, ring_shift(before[0], SECOND, 1), ring_shift(after[1], SECOND, 3)]
    last_level, *_ = lax.optimization_barrier((last_level, after, before))
    after, before = ring_shift(last_level, SECOND, 3), ring_shift(last_level, SECOND, 1)
    more_parts = parts + [
        last_level, after, before, ring_shift(before[:192], SECOND, 1), ring_shift(after[192:], SECOND, 3)
    ]

    given = lax.dynamic_index_in_dim(block_input, zz ^ 3, 0, keepdims=False)
    near = swap_z(own_attn, 1)
    far = swap_z(jnp.concatenate([own_attn, given]), 3)
    diagonal = [swap_z(near[:384], 3), swap_z(far[384:768], 1)]

    def whole(k):
        return sum(from_z[k][96 + 8 * n : 104 + 8 * n].astype(F32) for n in range(3))

    full = [whole(k) for k in range(4)]
    small, hidden = [], []
    for layer in range(2):
        same = jnp.where(pipe == layer, full[0], full[1])
        other = jnp.where(pipe == layer, full[2], full[3])
        small.append(same[:6])
        hidden.append(
            jnp.where(
                zhi == 0,
                jnp.concatenate([same[6:7], other[6:7]], axis=1),
                jnp.concatenate([other[6:7], same[6:7]], axis=1),
            )
        )

    drop_flags, key_valid, _ = lax.optimization_barrier((drop_flags, key_valid, level[1]))

    def all_rows(kept, came):
        halves = jnp.where(zhi == 0, jnp.stack([kept, came]), jnp.stack([came, kept]))
        across = swap_cores(halves)
        rows = jnp.where(core == 0, jnp.stack([halves, across], 1), jnp.stack([across, halves], 1))
        return rows.reshape(ROWS, D)

    x0 = all_rows(lax.dynamic_index_in_dim(block_input, zz, 0, keepdims=False), far[768:])
    out_cotangent, *_ = lax.optimization_barrier((out_cotangent, *parts[1:3]))
    cotangent = all_rows(
        lax.dynamic_index_in_dim(out_cotangent, zz, 0, keepdims=False),
        swap_z(lax.dynamic_index_in_dim(out_cotangent, zz ^ 3, 0, keepdims=False), 3),
    )
    flags = lax.dynamic_index_in_dim(drop_flags, zz, 0, keepdims=False)
    valid = lax.dynamic_index_in_dim(key_valid, zz, 0, keepdims=False)
    masks = pairs_allowed(flags, valid)

    attn_whole, ffn_whole = (VM, shape((1536, D), BF)), (VM, shape((2, 1536, D), BF))

    def join_attn(layer):
        (held,) = call(
            partial(join_attn_kernel, layer), [SM] + [VM] * 5, [attn_whole], [],
            [place, own_attn, near, *diagonal, far],
        )
        return held

    def join_ffn(layer, sources, after=()):
        (held,) = call(
            partial(join_ffn_kernel, layer), [SM] + [VM] * (2 + len(sources)), [ffn_whole], [],
            [place, own_up, own_down, *sources], after=after,
        )
        return held

    projected = (VM, shape((ROWS, 1152), BF))
    row_scratch = pltpu.VMEM((ROWS, D), BF)
    head_scratch = pltpu.VMEM((ROWS, 384), BF)
    wide_scratch = pltpu.VMEM((ROWS, 1536), BF)
    scores, probs = pltpu.VMEM((PAGES, 6, BLOCKS, BLOCKS), F32), pltpu.VMEM((PAGES, 6, BLOCKS, BLOCKS), BF)
    attn_scratch = [row_scratch, head_scratch, scores, probs]
    attn_held0, attn_held1 = join_attn(0), join_attn(1)
    p0, part = call(
        attn_first_kernel, [VM] * 4, [projected, ROW_BF], attn_scratch, [x0, small[0], masks[0][0], attn_held0]
    )
    ffn_held0 = join_ffn(0, parts)
    mid0, pre0, part = call(
        ffn_first_kernel, [VM] * 6, [ROW_F32, (VM, shape((ROWS, 1536), F32)), ROW_BF], [row_scratch, wide_scratch],
        [x0, part, swap_cores(part), small[0], hidden[0], ffn_held0],
    )
    y0, p1, part = call(
        attn_second_kernel, [VM] * 7, [ROW_BF, projected, ROW_BF], attn_scratch,
        [mid0, part, swap_cores(part), small[0], small[1], masks[1][0], attn_held1],
    )
    ffn_held1 = join_ffn(1, more_parts, [part])

    hidden_sum = (VM, shape((1, 1536), F32))
    two_sums = (VM, shape((2, D), F32))
    ring_blocks = [(VM, shape((4, 48, 3072), BF))] * 4
    z_blocks = [(VM, shape((D, 384), BF))] * 4
    ffn_total = pltpu.VMEM((D, 3072), BF)
    wide = (VM, shape((ROWS, 1536), BF))
    mid1, part, back, dhidden1, c1, e1, du1 = call(
        ffn_second_kernel, [VM] * 7, [ROW_F32, ROW_BF, ROW_BF, hidden_sum, ROW_BF, wide, wide],
        [pltpu.VMEM((ROWS, 1536), F32)],
        [y0, part, swap_cores(part), small[1], hidden[1], cotangent, ffn_held1],
    )
    plus1, minus1, later1, home1 = call(
        ffn_grads_kernel, [SM] + [VM] * 4, ring_blocks, [ffn_total], [place, c1, du1, cotangent, e1]
    )
    token = later1
    plus1, minus1 = ring_shift(plus1, FIRST, 1), ring_shift(minus1, FIRST, 3)

    back_scratch = [head_scratch, scores, scores, probs, probs]
    back_outs = [ROW_F32, ROW_BF, (VM, shape((4, D), F32)), ROW_BF, ROW_BF, projected, (VM, shape((ROWS, 384), BF))]
    y1, dmid1, back, sums1, a1, dr1, dp1, o1 = call(
        partial(attn_back_kernel, 1), [VM] * 11, [ROW_BF] + back_outs, back_scratch,
        [part, swap_cores(part), back, swap_cores(back), cotangent, mid1, small[1], masks[1][1], p1, y0,
         attn_held1], after=[token],
    )
    attn_total = [pltpu.VMEM((D, 1536), BF)]
    near1, far1, later_z1, home_z1 = call(
        attn_grads_kernel, [SM] + [VM] * 4, z_blocks, attn_total, [place, a1, dp1, dr1, o1]
    )
    token = later_z1
    near1, far1 = swap_z(near1, 1), swap_z(far1, 3)
    dx1, back, dhidden0, first1, c0, e0, du0 = call(
        ffn_back_kernel, [VM] * 9, [ROW_BF, ROW_BF, hidden_sum, two_sums, ROW_BF, wide, wide], [],
        [back, swap_cores(back), dmid1, y0, small[1], small[0], mid0, pre0, ffn_held0], after=[token],
    )
    plus0, minus0, later0, home0 = call(
        ffn_grads_kernel, [SM] + [VM] * 4, ring_blocks, [ffn_total], [place, c0, du0, dx1, e0]
    )
    six, four = [(VM, shape((6, 48, 3072), BF))] * 2, [(VM, shape((4, 48, 3072), BF))]
    plus0, minus0, some1 = call(
        join_kernel, [VM] * 6, six + four, [], [plus0, minus0, later1, home1, plus1, minus1], 20
    )
    token = some1
    plus0, minus0 = ring_shift(plus0, FIRST, 1), ring_shift(minus0, FIRST, 3)
    dmid0, back, sums0, a0, dr0, dp0, o0 = call(
        partial(attn_back_kernel, 0), [VM] * 9, back_outs, back_scratch,
        [back, swap_cores(back), dx1, mid0, small[0], masks[0][1], p0, x0, attn_held0],
        after=[token],
    )
    near0, far0, later_z0, home_z0 = call(
        attn_grads_kernel, [SM] + [VM] * 4, z_blocks, attn_total, [place, a0, dp0, dr0, o0]
    )
    tall = [(VM, shape((1152, 384), BF))] * 2
    near0, far0, some_z1 = call(
        join_z_kernel, [VM] * 6, tall + z_blocks[:1], [], [near0, far0, later_z1, home_z1, near1, far1]
    )
    token = some_z1
    near0, far0 = swap_z(near0, 1), swap_z(far0, 3)
    dx0, vec = call(
        last_kernel, [VM] * 10, [ROW_BF, (VM, shape((16, D), F32))], [],
        [back, swap_cores(back), dmid0, x0, small[0], sums0, dhidden0, first1, sums1, dhidden1], after=[token],
    )

    pair, one = [(VM, shape((2, 48, 3072), BF))], [(VM, shape((1, 48, 3072), BF))]
    on_plus, on_minus, some0 = call(
        pass_on_kernel, [VM] * 4, pair * 2 + four, [], [later0, home0, plus0, minus0], after=[vec]
    )
    last_plus, last_minus = ring_shift(on_plus, FIRST, 1), ring_shift(on_minus, FIRST, 3)
    half = [(VM, shape((384, 384), BF))]
    on_far, on_near, some_z0 = call(
        pass_on_z_kernel, [VM] * 4, half * 2 + z_blocks[:1], [], [later_z0, home_z0, near0, far0], after=[some0]
    )
    last_far, last_near = swap_z(on_far, 3), swap_z(on_near, 1)
    plus, minus, later, home = call(
        fold_kernel, [SM] + [VM] * 6, pair * 4, [pltpu.VMEM((2, 4, 48, 3072), BF)],
        [place, some1, some0, plus0, minus0, last_plus, last_minus], after=[some_z0],
    )
    plus, minus = ring_shift(plus, SECOND, 1), ring_shift(minus, SECOND, 3)
    turned = call(
        fold_z_kernel, [SM] + [VM] * 7, [(VM, shape((224, D), BF))] * 4, [pltpu.VMEM((D, D), BF)],
        [place, some_z1, some_z0, near0, far0, last_far, last_near, vec], after=[home],
    )
    token = turned[0]
    on_plus, on_minus, some = call(
        pass_on_kernel, [VM] * 4, one * 2 + pair, [], [later, home, plus, minus], after=[turned[0]]
    )
    last_plus, last_minus = ring_shift(on_plus, SECOND, 1), ring_shift(on_minus, SECOND, 3)
    turned = call(
        turn_kernel, [SM] + [VM] * 4, [(VM, shape((80, D), BF))] * 4,
        [pltpu.VMEM((192, D), BF), pltpu.VMEM((4, 16, D), F32)],
        [place, turned[0]] + [ring_shift(turned[s], FIRST, s) for s in (1, 2, 3)],
        after=[some],
    )
    turned = [turned[0]] + [ring_shift(turned[s], SECOND, s) for s in (1, 2, 3)]
    packs = call(
        pack_kernel, [SM] + [VM] * 7, [(VM, shape((160, D), BF))] * 4,
        [pltpu.VMEM((4, 160, D), BF), pltpu.VMEM((4, 16, D), F32)], [place, some, last_plus, last_minus, *turned],
    )
    grad_qkv, grad_out, grad_up, grad_down, vec = call(
        finish_kernel, [SM] + [VM] * 4,
        [(VM, shape((3, 48, 192), F32)), (VM, shape((48, 192), F32))] + [(VM, shape((48, D), F32))] * 2
        + [(VM, shape((8, D), F32))], [pltpu.VMEM((4, 8, D), F32)],
        [place, packs[0]] + [swap_z(packs[k], k) for k in (1, 2, 3)],
    )
    grad_qkv = jnp.transpose(grad_qkv, (1, 0, 2))
    grad_out, grad_down = grad_out.T, grad_down.T
    grad_hidden, grad_gains, grad_shifts, grad_biases = call(
        small_kernel, [SM] + [VM] * 2, [(VM, shape((1, 4 * D), F32))] + [(VM, shape((1, 2, D), F32))] * 3, [],
        [place, vec, swap_cores(vec)],
    )

    quarters = [value.reshape(4, 72, D) for value in (y0, dx0, y1, dx1)]
    (rows,) = call(
        rows_kernel, [SM] + [VM] * 4, [(VM, shape((4, 2, 72, D), BF))], [], [place, *quarters], after=[token]
    )
    activations, input_grads = call(
        by_batch_kernel, [VM], [(VM, shape((4, 72, D), BF))] * 2, [], [exchange_z(rows)]
    )
    return (
        activations[None],
        input_grads[None],
        grad_qkv[None],
        grad_out[None],
        grad_up[None],
        grad_down[None],
        grad_hidden,
        grad_gains,
        grad_shifts,
        grad_biases,
    )


def solution(mesh):
    fine = Mesh(mesh.devices.reshape(4, 4, 2, 2, 2), MESH_AXES)
    rows = DP + TENSOR
    in_specs = (
        P(None, rows, None),
        P(None, rows, None),
        P(None, DP),
        P(None, DP, None),
        P("pipe", None, None, TENSOR),
        P("pipe", TENSOR, None),
        P("pipe", None, TENSOR),
        P("pipe", TENSOR, None),
        P("pipe", TENSOR),
        P("pipe", None, None),
        P("pipe", None, None),
        P("pipe", None, None),
    )
    out_specs = (
        P("pipe", None, rows, None),
        P("pipe", None, rows, None),
        P("pipe", DP, None, TENSOR),
        P("pipe", TENSOR, DP),
        P("pipe", DP, TENSOR),
        P("pipe", TENSOR, DP),
        P("pipe", None),
        P("pipe", None, None),
        P("pipe", None, None),
        P("pipe", None, None),
    )
    return jax.shard_map(on_device, mesh=fine, in_specs=in_specs, out_specs=out_specs, check_vma=False)
```

```python
from functools import partial

import jax
import jax.numpy as jnp
from jax import lax
from jax.experimental import pallas as pl
from jax.experimental.pallas import tpu as pltpu
from jax.sharding import Mesh
from jax.sharding import PartitionSpec as P

BF = jnp.bfloat16
F32 = jnp.float32
D = 768
BLOCKS = 96
TEXT = 72
ROWS = 288
PAGES = 3
SCALE = 0.125
FACTOR = 3.0
COSTS = {'fold_z_kernel': 3, 'pass_on_kernel': 1, 'fold_kernel': 0.7, 'turn_kernel': 0.7, 'pack_kernel': 0.7, 'last_kernel': 0.7, 'join_kernel': 0.7, 'join_ffn_kernel': 3, 'level_kernel': 0.7, 'ffn_first_kernel': 2.3, 'attn_second_kernel': 2.4, 'ffn_second_kernel': 3.8, 'ffn_grads_kernel': 3.5, 'attn_back_kernel': 3.7, 'attn_grads_kernel': 2.4, 'ffn_back_kernel': 3.0}

MESH_AXES = ("y", "x", "pipe", "zhi", "core")
DP = ("y", "x")
TENSOR = ("zhi", "core")


def swap_cores(value):
    return lax.ppermute(value, "core", [(0, 1), (1, 0)])


def swap_z(value, k):
    pairs = []
    for p in range(2):
        for h in range(2):
            other = (2 * h + p) ^ k
            pairs.append((p * 2 + h, (other & 1) * 2 + (other >> 1)))
    return lax.ppermute(value, ("pipe", "zhi"), pairs)


def exchange_z(value):
    return lax.all_to_all(value, ("pipe", "zhi"), 0, 0, tiled=True)


def ring_shift(value, axis_of_core, shift):
    pairs = []
    for y in range(4):
        for x in range(4):
            for c in range(2):
                if axis_of_core[c] == "x":
                    to = (y, (x + shift) % 4)
                else:
                    to = ((y + shift) % 4, x)
                pairs.append(((y * 4 + x) * 2 + c, (to[0] * 4 + to[1]) * 2 + c))
    return lax.ppermute(value, ("y", "x", "core"), pairs)


FIRST = ("x", "y")
SECOND = ("y", "x")


def mm(a, b):
    return lax.dot_general(a, b, (((1,), (0,)), ((), ())), preferred_element_type=F32)


def mt(a, b):
    return lax.dot_general(a, b, (((1,), (1,)), ((), ())), preferred_element_type=F32)


def tm(a, b):
    return lax.dot_general(a, b, (((0,), (0,)), ((), ())), preferred_element_type=F32)


def normed(values):
    centre = values - jnp.mean(values, axis=-1, keepdims=True)
    spread = jnp.mean(centre * centre, axis=-1, keepdims=True)
    inverse = lax.rsqrt(spread + 1e-05)
    return centre * inverse, inverse


def norm_back(grad, unit, inverse, gain):
    scaled = grad * gain
    mean_one = jnp.mean(scaled, axis=-1, keepdims=True)
    mean_two = jnp.mean(scaled * unit, axis=-1, keepdims=True)
    return inverse * (scaled - mean_one - unit * mean_two)


def column_sum(values):
    return jnp.sum(values, axis=0, keepdims=True)


def half_masks():
    lane = lax.broadcasted_iota(jnp.int32, (1, 128), 1)
    low = (lane < 64).astype(F32)
    return low.astype(BF), (1.0 - low).astype(BF)


def ring_slot(d1, j2):
    if d1 == 0:
        return 3
    if d1 == 2:
        return 0 if j2 < 2 else 1
    if d1 == 1:
        return 2 if j2 < 2 else 0
    return 1 if j2 < 2 else 2


def row_of(place, d1, j2):
    step1 = jnp.where(place[3] == 0, 48, 192)
    step2 = jnp.where(place[3] == 0, 192, 48)
    return pl.multiple_of(((place[1] + d1) & 3) * step1 + j2 * step2, 16)


def send_blocks(place, total, outs):
    for d1 in range(4):
        for j2 in range(4):
            outs[ring_slot(d1, j2)][j2] = total[pl.ds(row_of(place, d1, j2), 48), :]


def send_z(place, total, near, far, later, home):
    for k in range(4):
        cols = pl.ds(pl.multiple_of((place[5] ^ k) * 384, 128), 384)
        top, low = total[pl.ds(0, 384), cols], total[pl.ds(384, 384), cols]
        if k == 0:
            home[0:384], home[384:768] = top, low
        elif k == 1:
            near[384:768], later[384:768] = top, low
        elif k == 2:
            near[0:384], far[384:768] = top, low
        else:
            later[0:384], far[0:384] = top, low


def level_kernel(place, own, one, two, three, first, last):
    for d, source in enumerate((own, one, two, three)):
        rows = pl.ds(pl.multiple_of(((place[1] + d) & 3) * 96, 16), 96)
        first[0, rows] = source[0]
        first[1, rows] = source[1]
        last[rows] = source[2]


def join_attn_kernel(layer, place, own, near, across, over, far, held):
    pipe, zhi = place[0], place[4]

    def put(group, half, value):
        held[pl.ds(pl.multiple_of(group * 384 + half * 192, 16), 192)] = value

    @pl.when(pipe == layer)
    def _():
        for group in range(4):
            put(group, zhi, own[group * 192 : group * 192 + 192])
            from_two = across if group < 2 else over
            put(group, 1 - zhi, from_two[group % 2 * 192 : group % 2 * 192 + 192])

    @pl.when(pipe != layer)
    def _():
        for group in range(4):
            put(group, zhi, near[group * 192 : group * 192 + 192])
            put(group, 1 - zhi, far[group * 192 : group * 192 + 192])


def join_ffn_kernel(layer, place, own_up, own_down, *refs):
    parts, held = refs[:-1], refs[-1]
    pipe, i2, zhi = place[0], place[2], place[4]

    def gathered(half, slot):
        def put(value, d2, first=0, count=384):
            held[half, pl.ds(pl.multiple_of(((i2 + d2) & 3) * 384 + first, 16), count)] = value

        for n, d2 in enumerate((0, 1, 3)):
            put(parts[n][slot] if slot < 2 else parts[5 + n][...], d2)
        if slot < 2:
            put(parts[3 + slot][...], 2)
        else:
            put(parts[8][...], 2, 0, 192)
            put(parts[9][...], 2, 192, 192)

    @pl.when(pipe == layer)
    def _():
        held[zhi, 0:768] = own_up[...]
        held[zhi, 768:1536] = own_down[...]
        gathered(1 - zhi, 2 * layer)

    @pl.when(pipe != layer)
    def _():
        gathered(zhi, layer)
        gathered(1 - zhi, layer + 1)


def attn_forward_body(x, small, mask_ref, held, a_ref, p_ref, o_ref, scores_ref, probs_ref, part_ref):
    unit, _ = normed(x)
    a_ref[...] = (unit * small[0:1] + small[1:2]).astype(BF)
    p_ref[...] = mt(a_ref[...], held[pl.ds(0, 1152), :]).astype(BF)
    halves = half_masks()
    for page in range(PAGES):
        rows = pl.ds(page * BLOCKS, BLOCKS)
        for pair in range(3):
            q = p_ref[rows, pl.ds(pair * 128, 128)]
            k = p_ref[rows, pl.ds(384 + pair * 128, 128)]
            for n, half in enumerate(halves):
                scores_ref[page, pair * 2 + n] = mt(q, k * half)
    for page in range(PAGES):
        allowed = mask_ref[page] > 0.5
        for head in range(6):
            scores = jnp.where(allowed, scores_ref[page, head] * SCALE, -1e30)
            expo = jnp.exp(scores - jnp.max(scores, axis=-1, keepdims=True))
            probs_ref[page, head] = (expo * (1.0 / jnp.sum(expo, axis=-1, keepdims=True))).astype(BF)
    for page in range(PAGES):
        rows = pl.ds(page * BLOCKS, BLOCKS)
        for pair in range(3):
            v = p_ref[rows, pl.ds(768 + pair * 128, 128)]
            total = mm(probs_ref[page, pair * 2], v * halves[0]) + mm(probs_ref[page, pair * 2 + 1], v * halves[1])
            o_ref[rows, pl.ds(pair * 128, 128)] = total.astype(BF)
    part_ref[...] = mm(o_ref[...], held[pl.ds(1152, 384), :]).astype(BF)


def attn_first_kernel(
    x_ref, small, mask_ref, held, p_ref, part_ref, a_ref, o_ref, scores_ref, probs_ref
):
    attn_forward_body(
        x_ref[...].astype(F32), small, mask_ref, held, a_ref, p_ref, o_ref, scores_ref, probs_ref, part_ref,
    )


def attn_second_kernel(
    mid_ref, mine, other, before, small, mask_ref, held,
    y_ref, p_ref, part_ref, a_ref, o_ref, scores_ref, probs_ref,
):
    total = mine[...].astype(F32) + other[...].astype(F32)
    y_ref[...] = (mid_ref[...] + total + before[5:6]).astype(BF)
    attn_forward_body(
        y_ref[...].astype(F32), small, mask_ref, held, a_ref, p_ref, o_ref, scores_ref, probs_ref, part_ref,
    )


def middle(x_ref, mine, other, small, mid_ref, c_ref):
    mid = x_ref[...].astype(F32) + (mine[...].astype(F32) + other[...].astype(F32)) + small[4:5]
    mid_ref[...] = mid
    unit, _ = normed(mid)
    c_ref[...] = (unit * small[2:3] + small[3:4]).astype(BF)


def gelu_parts(pre):
    cdf = 0.5 * (1.0 + lax.erf(pre * 0.7071067811865476))
    return pre * cdf, cdf + pre * (jnp.exp(-0.5 * pre * pre) * 0.3989422804014327)


def down_product(e_ref, held, part_ref):
    part_ref[...] = (
        mm(e_ref[:, pl.ds(0, 768)], held[0, pl.ds(768, 768), :])
        + mm(e_ref[:, pl.ds(768, 768)], held[1, pl.ds(768, 768), :])
    ).astype(BF)


def up_tile(n, c_ref, held, hidden):
    return mm(c_ref[...], held[n // 3, pl.ds(0, 768), pl.ds(n % 3 * 256, 256)]) + hidden[:, pl.ds(n * 256, 256)]


def ffn_first_kernel(
    x_ref, mine, other, small, hidden, held, mid_ref, pre_ref, part_ref, c_ref, e_ref
):
    middle(x_ref, mine, other, small, mid_ref, c_ref)
    for n in range(6):
        wide = pl.ds(n * 256, 256)
        pre = up_tile(n, c_ref, held, hidden)
        pre_ref[:, wide] = pre
        e_ref[:, wide] = (0.5 * pre * (1.0 + lax.erf(pre * 0.7071067811865476))).astype(BF)
    down_product(e_ref, held, part_ref)


def ffn_back_tile(n, grad, slope, held, du_ref, hidden_ref):
    wide = pl.ds(n * 256, 256)
    grad_e = mt(grad, held[n // 3, pl.ds(768 + n % 3 * 256, 256), :])
    grad_u = (grad_e * slope).astype(BF)
    du_ref[:, wide] = grad_u
    hidden_ref[:, wide] = column_sum(grad_u.astype(F32))


def ffn_back_product(du_ref, held, back_ref):
    back_ref[...] = (
        mt(du_ref[:, pl.ds(0, 768)], held[0, pl.ds(0, 768), :])
        + mt(du_ref[:, pl.ds(768, 768)], held[1, pl.ds(0, 768), :])
    ).astype(BF)


def ffn_grads_kernel(place, c_ref, du_ref, grad_ref, e_ref, g0, g1, g2, g3, total):
    turned = c_ref[...].T
    for n in range(6):
        wide = pl.ds(n * 256, 256)
        total[:, wide] = mm(turned, du_ref[:, wide]).astype(BF)
    turned = grad_ref[...].T
    for n in range(6):
        total[:, pl.ds(1536 + n * 256, 256)] = mm(turned, e_ref[:, pl.ds(n * 256, 256)]).astype(BF)
    send_blocks(place, total, (g0, g1, g2, g3))


def ffn_second_kernel(
    x_ref, mine, other, small, hidden, grad_ref, held,
    mid_ref, part_ref, back_ref, hidden_ref, c_ref, e_ref, du_ref, slope_ref,
):
    middle(x_ref, mine, other, small, mid_ref, c_ref)
    for n in range(6):
        wide = pl.ds(n * 256, 256)
        value, slope_ref[:, wide] = gelu_parts(up_tile(n, c_ref, held, hidden))
        e_ref[:, wide] = value.astype(BF)
    down_product(e_ref, held, part_ref)
    for n in range(6):
        ffn_back_tile(n, grad_ref[...], slope_ref[:, pl.ds(n * 256, 256)], held, du_ref, hidden_ref)
    ffn_back_product(du_ref, held, back_ref)


def layer_input_back(mine, other, up_grad, x_ref, small, dx_ref, sums_ref):
    grad = mine[...].astype(F32) + other[...].astype(F32)
    unit, inverse = normed(x_ref[...].astype(F32))
    sums_ref[0:1] = column_sum(grad * unit)
    sums_ref[1:2] = column_sum(grad)
    dx_ref[...] = (up_grad[...] + norm_back(grad, unit, inverse, small[0:1])).astype(BF)


def ffn_back_kernel(
    mine, other, up_grad, x_ref, small, below, mid_ref, pre_ref, held,
    dx_ref, back_ref, hidden_ref, sums_ref, c_ref, e_ref, du_ref,
):
    layer_input_back(mine, other, up_grad, x_ref, small, dx_ref, sums_ref)
    unit, _ = normed(mid_ref[...])
    c_ref[...] = (unit * below[2:3] + below[3:4]).astype(BF)
    for n in range(6):
        wide = pl.ds(n * 256, 256)
        value, slope = gelu_parts(pre_ref[:, wide])
        e_ref[:, wide] = value.astype(BF)
        ffn_back_tile(n, dx_ref[...], slope, held, du_ref, hidden_ref)
    ffn_back_product(du_ref, held, back_ref)


def last_kernel(mine, other, up_grad, x_ref, small, sums0, hidden0, first1, sums1, hidden1, dx_ref, vec):
    layer_input_back(mine, other, up_grad, x_ref, small, dx_ref, vec)
    vec[2:6] = sums0[...]
    vec[8:10] = first1[...]
    vec[10:14] = sums1[...]
    for n, part in enumerate((hidden0, hidden1)):
        vec[8 * n + 6 : 8 * n + 7] = part[:, 0:768]
        vec[8 * n + 7 : 8 * n + 8] = part[:, 768:1536]


def attn_back_kernel(layer, *refs):
    if layer == 1:
        end_mine, end_other, y_ref = refs[0], refs[1], refs[11]
        refs = refs[2:11] + refs[12:]
    (mine, other, dy_ref, mid_ref, small, mask_ref, p_ref, x_ref, held,
     dmid_ref, part_ref, sums_ref, a_ref, dr_ref, dp_ref, o_ref,
     do_ref, scores, dprobs, probs, dscores) = refs
    if layer == 1:
        y_ref[...] = (
            mid_ref[...] + (end_mine[...].astype(F32) + end_other[...].astype(F32)) + small[5:6]
        ).astype(BF)
    grad = mine[...].astype(F32) + other[...].astype(F32)
    dy = dy_ref[...].astype(F32)
    unit, inverse = normed(mid_ref[...])
    sums_ref[0:1] = column_sum(grad * unit)
    sums_ref[1:2] = column_sum(grad)
    dmid = dy + norm_back(grad, unit, inverse, small[2:3])
    dmid_ref[...] = dmid
    sums_ref[2:3] = column_sum(dmid)
    sums_ref[3:4] = column_sum(dy)
    dr_ref[...] = dmid.astype(BF)
    unit, _ = normed(x_ref[...].astype(F32))
    a_ref[...] = (unit * small[0:1] + small[1:2]).astype(BF)
    do_ref[...] = mt(dr_ref[...], held[pl.ds(1152, 384), :]).astype(BF)
    halves = half_masks()
    for page in range(PAGES):
        rows = pl.ds(page * BLOCKS, BLOCKS)
        for pair in range(3):
            q = p_ref[rows, pl.ds(pair * 128, 128)]
            k = p_ref[rows, pl.ds(384 + pair * 128, 128)]
            v = p_ref[rows, pl.ds(768 + pair * 128, 128)]
            do = do_ref[rows, pl.ds(pair * 128, 128)]
            for n, half in enumerate(halves):
                scores[page, pair * 2 + n] = mt(k * half, q)
                dprobs[page, pair * 2 + n] = mt(v * half, do)
    for page in range(PAGES):
        allowed = mask_ref[page] > 0.5
        for head in range(6):
            masked = jnp.where(allowed, scores[page, head] * SCALE, -1e30)
            expo = jnp.exp(masked - jnp.max(masked, axis=0, keepdims=True))
            share = expo * (1.0 / jnp.sum(expo, axis=0, keepdims=True))
            slope = dprobs[page, head]
            inner = jnp.sum(share * slope, axis=0, keepdims=True)
            probs[page, head] = share.astype(BF)
            dscores[page, head] = (share * (slope - inner)).astype(BF)
    for page in range(PAGES):
        rows = pl.ds(page * BLOCKS, BLOCKS)
        for pair in range(3):
            q = p_ref[rows, pl.ds(pair * 128, 128)]
            k = p_ref[rows, pl.ds(384 + pair * 128, 128)]
            v = p_ref[rows, pl.ds(768 + pair * 128, 128)]
            do = do_ref[rows, pl.ds(pair * 128, 128)]

            def both(product, left, right):
                one = product(left[page, pair * 2], right * halves[0])
                return one + product(left[page, pair * 2 + 1], right * halves[1])

            dp_ref[rows, pl.ds(pair * 128, 128)] = (both(tm, dscores, k) * SCALE).astype(BF)
            dp_ref[rows, pl.ds(384 + pair * 128, 128)] = (both(mm, dscores, q) * SCALE).astype(BF)
            dp_ref[rows, pl.ds(768 + pair * 128, 128)] = both(mm, probs, do).astype(BF)
            o_ref[rows, pl.ds(pair * 128, 128)] = both(tm, probs, v).astype(BF)
    part_ref[...] = mm(dp_ref[...], held[pl.ds(0, 1152), :]).astype(BF)


def attn_grads_kernel(place, a_ref, dp_ref, dr_ref, o_ref, near, far, later, home, total):
    turned = a_ref[...].T
    for n in range(3):
        cols = pl.ds(n * 384, 384)
        total[:, cols] = mm(turned, dp_ref[:, cols]).astype(BF)
    total[:, pl.ds(1152, 384)] = mm(dr_ref[...].T, o_ref[...]).astype(BF)
    send_z(place, total, near, far, later, home)


def added(left, right):
    return (left.astype(F32) + right.astype(F32)).astype(BF)


def added(left, right):
    return (left.astype(F32) + right.astype(F32)).astype(BF)


def arrived(home, plus, minus, total):
    half = home.shape[0] // 2
    total[0:half] = added(home[0:half], minus[0:half])
    total[half : 2 * half] = added(home[half : 2 * half], plus[half : 2 * half])


def pass_on_kernel(later, home, plus, minus, on_plus, on_minus, total):
    half = later.shape[0] // 2
    on_plus[...] = added(later[0:half], plus[0:half])
    on_minus[...] = added(later[half:], minus[half : 2 * half])
    arrived(home, plus, minus, total)


def join_kernel(plus, minus, later, home, got_plus, got_minus, out_plus, out_minus, total):
    size, half = plus.shape[0], plus.shape[0] // 2
    out_plus[0:size] = plus[...]
    out_minus[0:size] = minus[...]
    out_plus[size : size + half] = added(later[0:half], got_plus[0:half])
    out_minus[size : size + half] = added(later[half:], got_minus[half:size])
    arrived(home, got_plus, got_minus, total)


def join_z_kernel(near, far, later, home, got_near, got_far, out_near, out_far, total):
    out_near[0:768] = near[...]
    out_far[0:768] = far[...]
    out_far[768:1152] = added(later[0:384], got_near[0:384])
    out_near[768:1152] = added(later[384:768], got_far[384:768])
    total[0:384] = added(home[0:384], got_near[384:768])
    total[384:768] = added(home[384:768], got_far[0:384])


def pass_on_z_kernel(later, home, near, far, on_far, on_near, total):
    on_far[...] = added(later[0:384], near[0:384])
    on_near[...] = added(later[384:768], far[384:768])
    total[0:384] = added(home[0:384], near[384:768])
    total[384:768] = added(home[384:768], far[0:384])


def fold_kernel(place, some1, some0, plus0, minus0, last_plus, last_minus, plus, minus, later, home, total):
    total[1, 0:2] = added(some1[0:2], plus0[4:6])
    total[1, 2:4] = added(some1[2:4], minus0[4:6])
    total[0, 0:2] = added(some0[0:2], last_plus[...])
    total[0, 2:4] = added(some0[2:4], last_minus[...])

    def block(layer, d):
        return total[layer, (place[2] + d) & 3]

    plus[0], plus[1] = block(0, 2), block(1, 1)
    minus[0], minus[1] = block(0, 3), block(1, 2)
    later[0], later[1] = block(0, 1), block(1, 3)
    home[0], home[1] = block(0, 0), block(1, 0)


def put_split(out, first, value):
    count = value.shape[0]
    high = value.astype(BF)
    out[first : first + count] = high
    out[first + count : first + 2 * count] = (value - high.astype(F32)).astype(BF)


def get_split(ref, first, count):
    return ref[first : first + count].astype(F32) + ref[first + count : first + 2 * count].astype(F32)


def fold_z_kernel(place, *refs):
    some1, some0, near0, far0, last_far, last_near = refs[0:6]
    vec, outs, total = refs[6], refs[7:11], refs[11]
    total[0:384, 384:768] = added(some1[0:384], far0[768:1152])
    total[384:768, 384:768] = added(some1[384:768], near0[768:1152])
    total[0:384, 0:384] = added(some0[0:384], last_far[...])
    total[384:768, 0:384] = added(some0[384:768], last_near[...])
    for d1 in range(4):
        for j2 in range(4):
            outs[d1][j2 * 48 : j2 * 48 + 48] = total[pl.ds(row_of(place, d1, j2), 48)]
        put_split(outs[d1], 192, vec[...])


def turn_kernel(place, own, one, two, three, m0, m1, m2, m3, total, vecs):
    got = (own, one, two, three)
    total[...] = sum(r[0:192].astype(F32) for r in got).astype(BF)
    for s, r in enumerate(got):
        vecs[(place[1] - s) & 3] = get_split(r, 192, 16)
    vec = (vecs[0] + vecs[1]) + (vecs[2] + vecs[3])
    for s, out in enumerate((m0, m1, m2, m3)):
        row = pl.multiple_of(((place[2] + s) & 3) * 48, 16)
        out[0:48] = total[pl.ds(row, 48)]
        put_split(out, 48, vec)


def pack_kernel(place, *refs):
    some, last_plus, last_minus = refs[0:3]
    got, outs, staged, vecs = refs[3:7], refs[7:11], refs[11], refs[12]
    ffn0 = some[0].astype(F32) + last_plus[0].astype(F32)
    ffn1 = some[1].astype(F32) + last_minus[0].astype(F32)
    attn = sum(r[0:48].astype(F32) for r in got)
    for s, r in enumerate(got):
        vecs[(place[2] - s) & 3] = get_split(r, 48, 16)
    vec = (vecs[0] + vecs[1]) + (vecs[2] + vecs[3])
    zz = place[5]
    for half in range(2):
        for layer, ffn in ((0, ffn0), (1, ffn1)):
            to = staged.at[2 * half + layer]
            at = layer * 384 + half * 192
            for group in range(4):
                to[0:48, pl.ds(group * 192, 192)] = jnp.where(zz == group, attn[:, at : at + 192], 0.0).astype(BF)
            to[48:96] = ffn[:, half * 768 : half * 768 + 768].astype(BF)
            to[96:144] = ffn[:, 1536 + half * 768 : 1536 + half * 768 + 768].astype(BF)
            put_split(to, 144, vec[8 * layer : 8 * layer + 8])
    for k in range(4):
        outs[k][...] = staged[zz ^ k]


def finish_kernel(place, a, b, c, d, qkv_ref, out_ref, up_ref, down_ref, vec_ref, vecs):
    got = (a, b, c, d)
    total = sum(r[0:144].astype(F32) for r in got)
    for group in range(3):
        qkv_ref[group] = total[0:48, group * 192 : group * 192 + 192]
    out_ref[...] = total[0:48, 576:768]
    up_ref[...] = total[48:96]
    down_ref[...] = total[96:144]
    for k, r in enumerate(got):
        vecs[place[5] ^ k] = get_split(r, 144, 8)
    vec_ref[...] = (vecs[0] + vecs[1]) + (vecs[2] + vecs[3])


def rows_kernel(place, y0, dx0, y1, dx1, out):
    for layer, pair in enumerate(((y0, dx0), (y1, dx1))):
        for half in range(2):
            for n in range(2):
                out[2 * layer + half, n] = pair[n][2 * half + place[3]]


def by_batch_kernel(got, first, second):
    for batch, q in enumerate((0, 2, 1, 3)):
        first[batch] = got[q, 0]
        second[batch] = got[q, 1]


def small_kernel(place, mine, other, hidden_ref, gains_ref, shifts_ref, biases_ref):
    first = place[3] == 0
    low = jnp.where(first, mine[...], other[...])
    high = jnp.where(first, other[...], mine[...])
    for n, row in enumerate((low[6:7], high[6:7], low[7:8], high[7:8])):
        hidden_ref[:, n * 768 : n * 768 + 768] = row
    for n in range(2):
        gains_ref[0, n : n + 1] = low[2 * n : 2 * n + 1]
        shifts_ref[0, n : n + 1] = low[2 * n + 1 : 2 * n + 2]
    biases_ref[0] = low[4:6]


VM = pl.BlockSpec(memory_space=pltpu.VMEM)
SM = pl.BlockSpec(memory_space=pltpu.SMEM)
ANY = pl.BlockSpec(memory_space=pl.ANY)


def shape(dims, dtype):
    return jax.ShapeDtypeStruct(dims, dtype)


def call(body, ins, outs, scratch, args, limit=16, after=()):
    count, extra = len(args), len(after)
    name = getattr(body, 'func', body).__name__
    if extra:
        inner = body

        def body(*refs):
            return inner(*refs[:count], *refs[count + extra :])

        ins, args = ins + [ANY] * extra, [*args, *after]
    return pl.pallas_call(
        body,
        in_specs=ins,
        out_specs=tuple(spec for spec, _ in outs),
        out_shape=tuple(form for _, form in outs),
        scratch_shapes=scratch,
        compiler_params=pltpu.CompilerParams(vmem_limit_bytes=limit * 1024 * 1024),
        cost_estimate=pl.CostEstimate(flops=int(COSTS.get(name, 0.0) * FACTOR * 1e9) + 1024, bytes_accessed=1024, transcendentals=0),
    )(*args)


ROW_BF = (VM, shape((ROWS, D), BF))
ROW_F32 = (VM, shape((ROWS, D), F32))


def pairs_allowed(flags, valid):
    place = lax.broadcasted_iota(jnp.int32, (BLOCKS,), 0)
    visual = place >= TEXT
    dropped = (flags[:, None] == 1) & visual[None] | (flags[:, None] == 2) & ~visual[None]
    key_ok = (valid == 1) & ~dropped
    same = place[:, None] == place[None, :]
    other = visual[:, None] != visual[None, :]
    cross = same[None] | other[None] & key_ok[:, None, :]
    plain = same[None] | key_ok[:, None, :]
    masks = []
    for allowed in (cross, plain):
        allowed = allowed.astype(F32)
        masks.append((allowed, jnp.swapaxes(allowed, 1, 2)))
    return masks


def on_device(
    block_input, out_cotangent, drop_flags, key_valid, qkv_weight, out_weight, up_weight, down_weight,
    hidden_bias, norm_gains, norm_shifts, out_biases,
):
    y, x = lax.axis_index("y"), lax.axis_index("x")
    pipe, zhi, core = lax.axis_index("pipe"), lax.axis_index("zhi"), lax.axis_index("core")
    zz = 2 * zhi + pipe
    i1 = jnp.where(core == 0, x, y)
    i2 = jnp.where(core == 0, y, x)
    place = jnp.stack([pipe, i1, i2, core, zhi, zz]).astype(jnp.int32)

    packed = jnp.concatenate([
        norm_gains[0, 0:1], norm_shifts[0, 0:1], norm_gains[0, 1:2], norm_shifts[0, 1:2], out_biases[0],
        hidden_bias, jnp.zeros((1, D), F32),
    ])
    terms, rest = [], packed
    for _ in range(3):
        term = lax.reduce_precision(rest, 8, 7)
        terms.append(term.astype(BF))
        rest = rest - term
    packed_low = jnp.concatenate(terms)

    own_up, own_down = up_weight[0], down_weight[0]
    number = i2 * 4 + i1
    ffn_slice = jnp.where(
        number < 8,
        lax.dynamic_slice_in_dim(own_up, (number & 7) * 96, 96),
        lax.dynamic_slice_in_dim(own_down, (number & 7) * 96, 96),
    )
    piece = jnp.concatenate([ffn_slice, packed_low])
    from_z = [piece] + [swap_z(piece, k) for k in (1, 2, 3)]
    order = jnp.where(
        pipe == 0,
        jnp.stack([from_z[k][:96] for k in (2, 1, 3)]),
        jnp.stack([from_z[k][:96] for k in (1, 3, 2)]),
    )
    level = [order] + [ring_shift(order, FIRST, 4 - d) for d in (1, 2, 3)]
    first_level, last_level = call(
        level_kernel, [SM] + [VM] * 4, [(VM, shape((2, 384, D), BF)), (VM, shape((384, D), BF))], [],
        [place, *level],
    )
    after, before = ring_shift(first_level, SECOND, 3), ring_shift(first_level, SECOND, 1)
    parts = [first_level, after, before, ring_shift(before[0], SECOND, 1), ring_shift(after[1], SECOND, 3)]
    last_level, *_ = lax.optimization_barrier((last_level, after, before))
    after, before = ring_shift(last_level, SECOND, 3), ring_shift(last_level, SECOND, 1)
    more_parts = parts + [
        last_level, after, before, ring_shift(before[:192], SECOND, 1), ring_shift(after[192:], SECOND, 3)
    ]

    given = lax.dynamic_index_in_dim(block_input, zz ^ 3, 0, keepdims=False)
    qkv_weight, out_weight, _ = lax.optimization_barrier((qkv_weight, out_weight, piece))
    own_attn = jnp.concatenate([jnp.transpose(qkv_weight[0], (1, 2, 0)).reshape(576, D), out_weight[0]])
    near = swap_z(own_attn, 1)
    far = swap_z(jnp.concatenate([own_attn, given]), 3)
    diagonal = [swap_z(near[:384], 3), swap_z(far[384:768], 1)]

    def whole(k):
        return sum(from_z[k][96 + 8 * n : 104 + 8 * n].astype(F32) for n in range(3))

    full = [whole(k) for k in range(4)]
    small, hidden = [], []
    for layer in range(2):
        same = jnp.where(pipe == layer, full[0], full[1])
        other = jnp.where(pipe == layer, full[2], full[3])
        small.append(same[:6])
        hidden.append(
            jnp.where(
                zhi == 0,
                jnp.concatenate([same[6:7], other[6:7]], axis=1),
                jnp.concatenate([other[6:7], same[6:7]], axis=1),
            )
        )

    drop_flags, key_valid, _ = lax.optimization_barrier((drop_flags, key_valid, level[1]))

    def all_rows(kept, came):
        halves = jnp.where(zhi == 0, jnp.stack([kept, came]), jnp.stack([came, kept]))
        across = swap_cores(halves)
        rows = jnp.where(core == 0, jnp.stack([halves, across], 1), jnp.stack([across, halves], 1))
        return rows.reshape(ROWS, D)

    x0 = all_rows(lax.dynamic_index_in_dim(block_input, zz, 0, keepdims=False), far[768:])
    out_cotangent, *_ = lax.optimization_barrier((out_cotangent, *parts[1:3]))
    cotangent = all_rows(
        lax.dynamic_index_in_dim(out_cotangent, zz, 0, keepdims=False),
        swap_z(lax.dynamic_index_in_dim(out_cotangent, zz ^ 3, 0, keepdims=False), 3),
    )
    flags = lax.dynamic_index_in_dim(drop_flags, zz, 0, keepdims=False)
    valid = lax.dynamic_index_in_dim(key_valid, zz, 0, keepdims=False)
    masks = pairs_allowed(flags, valid)

    attn_whole, ffn_whole = (VM, shape((1536, D), BF)), (VM, shape((2, 1536, D), BF))

    def join_attn(layer):
        (held,) = call(
            partial(join_attn_kernel, layer), [SM] + [VM] * 5, [attn_whole], [],
            [place, own_attn, near, *diagonal, far],
        )
        return held

    def join_ffn(layer, sources, after=()):
        (held,) = call(
            partial(join_ffn_kernel, layer), [SM] + [VM] * (2 + len(sources)), [ffn_whole], [],
            [place, own_up, own_down, *sources], after=after,
        )
        return held

    projected = (VM, shape((ROWS, 1152), BF))
    row_scratch = pltpu.VMEM((ROWS, D), BF)
    head_scratch = pltpu.VMEM((ROWS, 384), BF)
    wide_scratch = pltpu.VMEM((ROWS, 1536), BF)
    scores, probs = pltpu.VMEM((PAGES, 6, BLOCKS, BLOCKS), F32), pltpu.VMEM((PAGES, 6, BLOCKS, BLOCKS), BF)
    attn_scratch = [row_scratch, head_scratch, scores, probs]
    attn_held0, attn_held1 = join_attn(0), join_attn(1)
    p0, part = call(
        attn_first_kernel, [VM] * 4, [projected, ROW_BF], attn_scratch, [x0, small[0], masks[0][0], attn_held0]
    )
    ffn_held0 = join_ffn(0, parts)
    mid0, pre0, part = call(
        ffn_first_kernel, [VM] * 6, [ROW_F32, (VM, shape((ROWS, 1536), F32)), ROW_BF], [row_scratch, wide_scratch],
        [x0, part, swap_cores(part), small[0], hidden[0], ffn_held0],
    )
    y0, p1, part = call(
        attn_second_kernel, [VM] * 7, [ROW_BF, projected, ROW_BF], attn_scratch,
        [mid0, part, swap_cores(part), small[0], small[1], masks[1][0], attn_held1],
    )
    ffn_held1 = join_ffn(1, more_parts, [part])

    hidden_sum = (VM, shape((1, 1536), F32))
    two_sums = (VM, shape((2, D), F32))
    ring_blocks = [(VM, shape((4, 48, 3072), BF))] * 4
    z_blocks = [(VM, shape((D, 384), BF))] * 4
    ffn_total = pltpu.VMEM((D, 3072), BF)
    wide = (VM, shape((ROWS, 1536), BF))
    mid1, part, back, dhidden1, c1, e1, du1 = call(
        ffn_second_kernel, [VM] * 7, [ROW_F32, ROW_BF, ROW_BF, hidden_sum, ROW_BF, wide, wide],
        [pltpu.VMEM((ROWS, 1536), F32)],
        [y0, part, swap_cores(part), small[1], hidden[1], cotangent, ffn_held1],
    )
    plus1, minus1, later1, home1 = call(
        ffn_grads_kernel, [SM] + [VM] * 4, ring_blocks, [ffn_total], [place, c1, du1, cotangent, e1]
    )
    token = later1
    plus1, minus1 = ring_shift(plus1, FIRST, 1), ring_shift(minus1, FIRST, 3)

    back_scratch = [head_scratch, scores, scores, probs, probs]
    back_outs = [ROW_F32, ROW_BF, (VM, shape((4, D), F32)), ROW_BF, ROW_BF, projected, (VM, shape((ROWS, 384), BF))]
    y1, dmid1, back, sums1, a1, dr1, dp1, o1 = call(
        partial(attn_back_kernel, 1), [VM] * 11, [ROW_BF] + back_outs, back_scratch,
        [part, swap_cores(part), back, swap_cores(back), cotangent, mid1, small[1], masks[1][1], p1, y0,
         attn_held1], after=[token],
    )
    attn_total = [pltpu.VMEM((D, 1536), BF)]
    near1, far1, later_z1, home_z1 = call(
        attn_grads_kernel, [SM] + [VM] * 4, z_blocks, attn_total, [place, a1, dp1, dr1, o1]
    )
    token = later_z1
    near1, far1 = swap_z(near1, 1), swap_z(far1, 3)
    dx1, back, dhidden0, first1, c0, e0, du0 = call(
        ffn_back_kernel, [VM] * 9, [ROW_BF, ROW_BF, hidden_sum, two_sums, ROW_BF, wide, wide], [],
        [back, swap_cores(back), dmid1, y0, small[1], small[0], mid0, pre0, ffn_held0], after=[token],
    )
    plus0, minus0, later0, home0 = call(
        ffn_grads_kernel, [SM] + [VM] * 4, ring_blocks, [ffn_total], [place, c0, du0, dx1, e0]
    )
    six, four = [(VM, shape((6, 48, 3072), BF))] * 2, [(VM, shape((4, 48, 3072), BF))]
    plus0, minus0, some1 = call(
        join_kernel, [VM] * 6, six + four, [], [plus0, minus0, later1, home1, plus1, minus1], 20
    )
    token = some1
    plus0, minus0 = ring_shift(plus0, FIRST, 1), ring_shift(minus0, FIRST, 3)
    dmid0, back, sums0, a0, dr0, dp0, o0 = call(
        partial(attn_back_kernel, 0), [VM] * 9, back_outs, back_scratch,
        [back, swap_cores(back), dx1, mid0, small[0], masks[0][1], p0, x0, attn_held0],
        after=[token],
    )
    near0, far0, later_z0, home_z0 = call(
        attn_grads_kernel, [SM] + [VM] * 4, z_blocks, attn_total, [place, a0, dp0, dr0, o0]
    )
    tall = [(VM, shape((1152, 384), BF))] * 2
    near0, far0, some_z1 = call(
        join_z_kernel, [VM] * 6, tall + z_blocks[:1], [], [near0, far0, later_z1, home_z1, near1, far1]
    )
    token = some_z1
    near0, far0 = swap_z(near0, 1), swap_z(far0, 3)
    dx0, vec = call(
        last_kernel, [VM] * 10, [ROW_BF, (VM, shape((16, D), F32))], [],
        [back, swap_cores(back), dmid0, x0, small[0], sums0, dhidden0, first1, sums1, dhidden1], after=[token],
    )

    pair, one = [(VM, shape((2, 48, 3072), BF))], [(VM, shape((1, 48, 3072), BF))]
    on_plus, on_minus, some0 = call(
        pass_on_kernel, [VM] * 4, pair * 2 + four, [], [later0, home0, plus0, minus0], after=[vec]
    )
    last_plus, last_minus = ring_shift(on_plus, FIRST, 1), ring_shift(on_minus, FIRST, 3)
    half = [(VM, shape((384, 384), BF))]
    on_far, on_near, some_z0 = call(
        pass_on_z_kernel, [VM] * 4, half * 2 + z_blocks[:1], [], [later_z0, home_z0, near0, far0], after=[some0]
    )
    last_far, last_near = swap_z(on_far, 3), swap_z(on_near, 1)
    plus, minus, later, home = call(
        fold_kernel, [SM] + [VM] * 6, pair * 4, [pltpu.VMEM((2, 4, 48, 3072), BF)],
        [place, some1, some0, plus0, minus0, last_plus, last_minus], after=[some_z0],
    )
    plus, minus = ring_shift(plus, SECOND, 1), ring_shift(minus, SECOND, 3)
    turned = call(
        fold_z_kernel, [SM] + [VM] * 7, [(VM, shape((224, D), BF))] * 4, [pltpu.VMEM((D, D), BF)],
        [place, some_z1, some_z0, near0, far0, last_far, last_near, vec], after=[home],
    )
    token = turned[0]
    on_plus, on_minus, some = call(
        pass_on_kernel, [VM] * 4, one * 2 + pair, [], [later, home, plus, minus], after=[turned[0]]
    )
    last_plus, last_minus = ring_shift(on_plus, SECOND, 1), ring_shift(on_minus, SECOND, 3)
    turned = call(
        turn_kernel, [SM] + [VM] * 4, [(VM, shape((80, D), BF))] * 4,
        [pltpu.VMEM((192, D), BF), pltpu.VMEM((4, 16, D), F32)],
        [place, turned[0]] + [ring_shift(turned[s], FIRST, s) for s in (1, 2, 3)],
        after=[some],
    )
    turned = [turned[0]] + [ring_shift(turned[s], SECOND, s) for s in (1, 2, 3)]
    packs = call(
        pack_kernel, [SM] + [VM] * 7, [(VM, shape((160, D), BF))] * 4,
        [pltpu.VMEM((4, 160, D), BF), pltpu.VMEM((4, 16, D), F32)], [place, some, last_plus, last_minus, *turned],
    )
    grad_qkv, grad_out, grad_up, grad_down, vec = call(
        finish_kernel, [SM] + [VM] * 4,
        [(VM, shape((3, 48, 192), F32)), (VM, shape((48, 192), F32))] + [(VM, shape((48, D), F32))] * 2
        + [(VM, shape((8, D), F32))], [pltpu.VMEM((4, 8, D), F32)],
        [place, packs[0]] + [swap_z(packs[k], k) for k in (1, 2, 3)],
    )
    grad_qkv = jnp.transpose(grad_qkv, (1, 0, 2))
    grad_out, grad_down = grad_out.T, grad_down.T
    grad_hidden, grad_gains, grad_shifts, grad_biases = call(
        small_kernel, [SM] + [VM] * 2, [(VM, shape((1, 4 * D), F32))] + [(VM, shape((1, 2, D), F32))] * 3, [],
        [place, vec, swap_cores(vec)],
    )

    quarters = [value.reshape(4, 72, D) for value in (y0, dx0, y1, dx1)]
    (rows,) = call(
        rows_kernel, [SM] + [VM] * 4, [(VM, shape((4, 2, 72, D), BF))], [], [place, *quarters], after=[token]
    )
    activations, input_grads = call(
        by_batch_kernel, [VM], [(VM, shape((4, 72, D), BF))] * 2, [], [exchange_z(rows)]
    )
    return (
        activations[None],
        input_grads[None],
        grad_qkv[None],
        grad_out[None],
        grad_up[None],
        grad_down[None],
        grad_hidden,
        grad_gains,
        grad_shifts,
        grad_biases,
    )


def solution(mesh):
    fine = Mesh(mesh.devices.reshape(4, 4, 2, 2, 2), MESH_AXES)
    rows = DP + TENSOR
    in_specs = (
        P(None, rows, None),
        P(None, rows, None),
        P(None, DP),
        P(None, DP, None),
        P("pipe", None, None, TENSOR),
        P("pipe", TENSOR, None),
        P("pipe", None, TENSOR),
        P("pipe", TENSOR, None),
        P("pipe", TENSOR),
        P("pipe", None, None),
        P("pipe", None, None),
        P("pipe", None, None),
    )
    out_specs = (
        P("pipe", None, rows, None),
        P("pipe", None, rows, None),
        P("pipe", DP, None, TENSOR),
        P("pipe", TENSOR, DP),
        P("pipe", DP, TENSOR),
        P("pipe", TENSOR, DP),
        P("pipe", None),
        P("pipe", None, None),
        P("pipe", None, None),
        P("pipe", None, None),
    )
    return jax.shard_map(on_device, mesh=fine, in_specs=in_specs, out_specs=out_specs, check_vma=False)
```

```python
from functools import partial

import jax
import jax.numpy as jnp
from jax import lax
from jax.experimental import pallas as pl
from jax.experimental.pallas import tpu as pltpu
from jax.sharding import Mesh
from jax.sharding import PartitionSpec as P

BF = jnp.bfloat16
F32 = jnp.float32
D = 768
BLOCKS = 96
TEXT = 72
ROWS = 288
PAGES = 3
SCALE = 0.125
FACTOR = 3.0
COSTS = {'fold_z_kernel': 3, 'pass_on_kernel': 1, 'fold_kernel': 0.7, 'turn_kernel': 0.7, 'pack_kernel': 0.7, 'last_kernel': 0.7, 'join_kernel': 0.7, 'join_ffn_kernel': 3, 'level_kernel': 0.7, 'ffn_first_kernel': 2.3, 'attn_second_kernel': 2.4, 'ffn_second_kernel': 3.8, 'ffn_grads_kernel': 3.5, 'attn_back_kernel': 3.7, 'attn_grads_kernel': 2.4, 'ffn_back_kernel': 3.0}

MESH_AXES = ("y", "x", "pipe", "zhi", "core")
DP = ("y", "x")
TENSOR = ("zhi", "core")


def swap_cores(value):
    return lax.ppermute(value, "core", [(0, 1), (1, 0)])


def swap_z(value, k):
    pairs = []
    for p in range(2):
        for h in range(2):
            other = (2 * h + p) ^ k
            pairs.append((p * 2 + h, (other & 1) * 2 + (other >> 1)))
    return lax.ppermute(value, ("pipe", "zhi"), pairs)


def exchange_z(value):
    return lax.all_to_all(value, ("pipe", "zhi"), 0, 0, tiled=True)


def ring_shift(value, axis_of_core, shift):
    pairs = []
    for y in range(4):
        for x in range(4):
            for c in range(2):
                if axis_of_core[c] == "x":
                    to = (y, (x + shift) % 4)
                else:
                    to = ((y + shift) % 4, x)
                pairs.append(((y * 4 + x) * 2 + c, (to[0] * 4 + to[1]) * 2 + c))
    return lax.ppermute(value, ("y", "x", "core"), pairs)


FIRST = ("x", "y")
SECOND = ("y", "x")


def mm(a, b):
    return lax.dot_general(a, b, (((1,), (0,)), ((), ())), preferred_element_type=F32)


def mt(a, b):
    return lax.dot_general(a, b, (((1,), (1,)), ((), ())), preferred_element_type=F32)


def tm(a, b):
    return lax.dot_general(a, b, (((0,), (0,)), ((), ())), preferred_element_type=F32)


def normed(values):
    centre = values - jnp.mean(values, axis=-1, keepdims=True)
    spread = jnp.mean(centre * centre, axis=-1, keepdims=True)
    inverse = lax.rsqrt(spread + 1e-05)
    return centre * inverse, inverse


def norm_back(grad, unit, inverse, gain):
    scaled = grad * gain
    mean_one = jnp.mean(scaled, axis=-1, keepdims=True)
    mean_two = jnp.mean(scaled * unit, axis=-1, keepdims=True)
    return inverse * (scaled - mean_one - unit * mean_two)


def column_sum(values):
    return jnp.sum(values, axis=0, keepdims=True)


def half_masks():
    lane = lax.broadcasted_iota(jnp.int32, (1, 128), 1)
    low = (lane < 64).astype(F32)
    return low.astype(BF), (1.0 - low).astype(BF)


def ring_slot(d1, j2):
    if d1 == 0:
        return 3
    if d1 == 2:
        return 0 if j2 < 2 else 1
    if d1 == 1:
        return 2 if j2 < 2 else 0
    return 1 if j2 < 2 else 2


def row_of(place, d1, j2):
    step1 = jnp.where(place[3] == 0, 48, 192)
    step2 = jnp.where(place[3] == 0, 192, 48)
    return pl.multiple_of(((place[1] + d1) & 3) * step1 + j2 * step2, 16)


def send_blocks(place, total, outs):
    for d1 in range(4):
        for j2 in range(4):
            outs[ring_slot(d1, j2)][j2] = total[pl.ds(row_of(place, d1, j2), 48), :]


def send_z(place, total, near, far, later, home):
    for k in range(4):
        cols = pl.ds(pl.multiple_of((place[5] ^ k) * 384, 128), 384)
        top, low = total[pl.ds(0, 384), cols], total[pl.ds(384, 384), cols]
        if k == 0:
            home[0:384], home[384:768] = top, low
        elif k == 1:
            near[384:768], later[384:768] = top, low
        elif k == 2:
            near[0:384], far[384:768] = top, low
        else:
            later[0:384], far[0:384] = top, low


def level_kernel(place, own, one, two, three, first, last):
    for d, source in enumerate((own, one, two, three)):
        rows = pl.ds(pl.multiple_of(((place[1] + d) & 3) * 96, 16), 96)
        first[0, rows] = source[0]
        first[1, rows] = source[1]
        last[rows] = source[2]


def half_kernel(first, source, out):
    out[...] = source[first : first + 384]


def join_attn_kernel(layer, place, own, near, across, over, far, held):
    pipe, zhi = place[0], place[4]

    def put(group, half, value):
        held[pl.ds(pl.multiple_of(group * 384 + half * 192, 16), 192)] = value

    @pl.when(pipe == layer)
    def _():
        for group in range(4):
            put(group, zhi, own[group * 192 : group * 192 + 192])
            from_two = across if group < 2 else over
            put(group, 1 - zhi, from_two[group % 2 * 192 : group % 2 * 192 + 192])

    @pl.when(pipe != layer)
    def _():
        for group in range(4):
            put(group, zhi, near[group * 192 : group * 192 + 192])
            put(group, 1 - zhi, far[group * 192 : group * 192 + 192])


def join_ffn_kernel(layer, place, own_up, own_down, *refs):
    parts, held = refs[:-1], refs[-1]
    pipe, i2, zhi = place[0], place[2], place[4]

    def gathered(half, slot):
        def put(value, d2, first=0, count=384):
            held[half, pl.ds(pl.multiple_of(((i2 + d2) & 3) * 384 + first, 16), count)] = value

        for n, d2 in enumerate((0, 1, 3)):
            put(parts[n][slot] if slot < 2 else parts[5 + n][...], d2)
        if slot < 2:
            put(parts[3 + slot][...], 2)
        else:
            put(parts[8][...], 2, 0, 192)
            put(parts[9][...], 2, 192, 192)

    @pl.when(pipe == layer)
    def _():
        held[zhi, 0:768] = own_up[...]
        held[zhi, 768:1536] = own_down[...]
        gathered(1 - zhi, 2 * layer)

    @pl.when(pipe != layer)
    def _():
        gathered(zhi, layer)
        gathered(1 - zhi, layer + 1)


def attn_forward_body(x, small, mask_ref, held, a_ref, p_ref, o_ref, scores_ref, probs_ref, part_ref):
    unit, _ = normed(x)
    a_ref[...] = (unit * small[0:1] + small[1:2]).astype(BF)
    p_ref[...] = mt(a_ref[...], held[pl.ds(0, 1152), :]).astype(BF)
    halves = half_masks()
    for page in range(PAGES):
        rows = pl.ds(page * BLOCKS, BLOCKS)
        for pair in range(3):
            q = p_ref[rows, pl.ds(pair * 128, 128)]
            k = p_ref[rows, pl.ds(384 + pair * 128, 128)]
            for n, half in enumerate(halves):
                scores_ref[page, pair * 2 + n] = mt(q, k * half)
    for page in range(PAGES):
        allowed = mask_ref[page] > 0.5
        for head in range(6):
            scores = jnp.where(allowed, scores_ref[page, head] * SCALE, -1e30)
            expo = jnp.exp(scores - jnp.max(scores, axis=-1, keepdims=True))
            probs_ref[page, head] = (expo * (1.0 / jnp.sum(expo, axis=-1, keepdims=True))).astype(BF)
    for page in range(PAGES):
        rows = pl.ds(page * BLOCKS, BLOCKS)
        for pair in range(3):
            v = p_ref[rows, pl.ds(768 + pair * 128, 128)]
            total = mm(probs_ref[page, pair * 2], v * halves[0]) + mm(probs_ref[page, pair * 2 + 1], v * halves[1])
            o_ref[rows, pl.ds(pair * 128, 128)] = total.astype(BF)
    part_ref[...] = mm(o_ref[...], held[pl.ds(1152, 384), :]).astype(BF)


def attn_first_kernel(
    x_ref, small, mask_ref, held, p_ref, part_ref, a_ref, o_ref, scores_ref, probs_ref
):
    attn_forward_body(
        x_ref[...].astype(F32), small, mask_ref, held, a_ref, p_ref, o_ref, scores_ref, probs_ref, part_ref,
    )


def attn_second_kernel(
    mid_ref, mine, other, before, small, mask_ref, held,
    y_ref, p_ref, part_ref, a_ref, o_ref, scores_ref, probs_ref,
):
    total = mine[...].astype(F32) + other[...].astype(F32)
    y_ref[...] = (mid_ref[...] + total + before[5:6]).astype(BF)
    attn_forward_body(
        y_ref[...].astype(F32), small, mask_ref, held, a_ref, p_ref, o_ref, scores_ref, probs_ref, part_ref,
    )


def middle(x_ref, mine, other, small, mid_ref, c_ref):
    mid = x_ref[...].astype(F32) + (mine[...].astype(F32) + other[...].astype(F32)) + small[4:5]
    mid_ref[...] = mid
    unit, _ = normed(mid)
    c_ref[...] = (unit * small[2:3] + small[3:4]).astype(BF)


def gelu_parts(pre):
    cdf = 0.5 * (1.0 + lax.erf(pre * 0.7071067811865476))
    return pre * cdf, cdf + pre * (jnp.exp(-0.5 * pre * pre) * 0.3989422804014327)


def down_product(e_ref, held, part_ref):
    part_ref[...] = (
        mm(e_ref[:, pl.ds(0, 768)], held[0, pl.ds(768, 768), :])
        + mm(e_ref[:, pl.ds(768, 768)], held[1, pl.ds(768, 768), :])
    ).astype(BF)


def up_tile(n, c_ref, held, hidden):
    return mm(c_ref[...], held[n // 3, pl.ds(0, 768), pl.ds(n % 3 * 256, 256)]) + hidden[:, pl.ds(n * 256, 256)]


def ffn_first_kernel(
    x_ref, mine, other, small, hidden, held, mid_ref, pre_ref, part_ref, c_ref, e_ref
):
    middle(x_ref, mine, other, small, mid_ref, c_ref)
    for n in range(6):
        wide = pl.ds(n * 256, 256)
        pre = up_tile(n, c_ref, held, hidden)
        pre_ref[:, wide] = pre
        e_ref[:, wide] = (0.5 * pre * (1.0 + lax.erf(pre * 0.7071067811865476))).astype(BF)
    down_product(e_ref, held, part_ref)


def ffn_back_tile(n, grad, slope, held, du_ref, hidden_ref):
    wide = pl.ds(n * 256, 256)
    grad_e = mt(grad, held[n // 3, pl.ds(768 + n % 3 * 256, 256), :])
    grad_u = (grad_e * slope).astype(BF)
    du_ref[:, wide] = grad_u
    hidden_ref[:, wide] = column_sum(grad_u.astype(F32))


def ffn_back_product(du_ref, held, back_ref):
    back_ref[...] = (
        mt(du_ref[:, pl.ds(0, 768)], held[0, pl.ds(0, 768), :])
        + mt(du_ref[:, pl.ds(768, 768)], held[1, pl.ds(0, 768), :])
    ).astype(BF)


def ffn_grads_kernel(place, c_ref, du_ref, grad_ref, e_ref, g0, g1, g2, g3, total):
    turned = c_ref[...].T
    for n in range(6):
        wide = pl.ds(n * 256, 256)
        total[:, wide] = mm(turned, du_ref[:, wide]).astype(BF)
    turned = grad_ref[...].T
    for n in range(6):
        total[:, pl.ds(1536 + n * 256, 256)] = mm(turned, e_ref[:, pl.ds(n * 256, 256)]).astype(BF)
    send_blocks(place, total, (g0, g1, g2, g3))


def ffn_second_kernel(
    x_ref, mine, other, small, hidden, grad_ref, held,
    mid_ref, part_ref, back_ref, hidden_ref, c_ref, e_ref, du_ref, slope_ref,
):
    middle(x_ref, mine, other, small, mid_ref, c_ref)
    for n in range(6):
        wide = pl.ds(n * 256, 256)
        value, slope_ref[:, wide] = gelu_parts(up_tile(n, c_ref, held, hidden))
        e_ref[:, wide] = value.astype(BF)
    down_product(e_ref, held, part_ref)
    for n in range(6):
        ffn_back_tile(n, grad_ref[...], slope_ref[:, pl.ds(n * 256, 256)], held, du_ref, hidden_ref)
    ffn_back_product(du_ref, held, back_ref)


def layer_input_back(mine, other, up_grad, x_ref, small, dx_ref, sums_ref):
    grad = mine[...].astype(F32) + other[...].astype(F32)
    unit, inverse = normed(x_ref[...].astype(F32))
    sums_ref[0:1] = column_sum(grad * unit)
    sums_ref[1:2] = column_sum(grad)
    dx_ref[...] = (up_grad[...] + norm_back(grad, unit, inverse, small[0:1])).astype(BF)


def ffn_back_kernel(
    mine, other, up_grad, x_ref, small, below, mid_ref, pre_ref, held,
    dx_ref, back_ref, hidden_ref, sums_ref, c_ref, e_ref, du_ref,
):
    layer_input_back(mine, other, up_grad, x_ref, small, dx_ref, sums_ref)
    unit, _ = normed(mid_ref[...])
    c_ref[...] = (unit * below[2:3] + below[3:4]).astype(BF)
    for n in range(6):
        wide = pl.ds(n * 256, 256)
        value, slope = gelu_parts(pre_ref[:, wide])
        e_ref[:, wide] = value.astype(BF)
        ffn_back_tile(n, dx_ref[...], slope, held, du_ref, hidden_ref)
    ffn_back_product(du_ref, held, back_ref)


def last_kernel(mine, other, up_grad, x_ref, small, sums0, hidden0, first1, sums1, hidden1, dx_ref, vec):
    layer_input_back(mine, other, up_grad, x_ref, small, dx_ref, vec)
    vec[2:6] = sums0[...]
    vec[8:10] = first1[...]
    vec[10:14] = sums1[...]
    for n, part in enumerate((hidden0, hidden1)):
        vec[8 * n + 6 : 8 * n + 7] = part[:, 0:768]
        vec[8 * n + 7 : 8 * n + 8] = part[:, 768:1536]


def attn_back_kernel(layer, *refs):
    if layer == 1:
        end_mine, end_other, y_ref = refs[0], refs[1], refs[11]
        refs = refs[2:11] + refs[12:]
    (mine, other, dy_ref, mid_ref, small, mask_ref, p_ref, x_ref, held,
     dmid_ref, part_ref, sums_ref, a_ref, dr_ref, dp_ref, o_ref,
     do_ref, scores, dprobs, probs, dscores) = refs
    if layer == 1:
        y_ref[...] = (
            mid_ref[...] + (end_mine[...].astype(F32) + end_other[...].astype(F32)) + small[5:6]
        ).astype(BF)
    grad = mine[...].astype(F32) + other[...].astype(F32)
    dy = dy_ref[...].astype(F32)
    unit, inverse = normed(mid_ref[...])
    sums_ref[0:1] = column_sum(grad * unit)
    sums_ref[1:2] = column_sum(grad)
    dmid = dy + norm_back(grad, unit, inverse, small[2:3])
    dmid_ref[...] = dmid
    sums_ref[2:3] = column_sum(dmid)
    sums_ref[3:4] = column_sum(dy)
    dr_ref[...] = dmid.astype(BF)
    unit, _ = normed(x_ref[...].astype(F32))
    a_ref[...] = (unit * small[0:1] + small[1:2]).astype(BF)
    do_ref[...] = mt(dr_ref[...], held[pl.ds(1152, 384), :]).astype(BF)
    halves = half_masks()
    for page in range(PAGES):
        rows = pl.ds(page * BLOCKS, BLOCKS)
        for pair in range(3):
            q = p_ref[rows, pl.ds(pair * 128, 128)]
            k = p_ref[rows, pl.ds(384 + pair * 128, 128)]
            v = p_ref[rows, pl.ds(768 + pair * 128, 128)]
            do = do_ref[rows, pl.ds(pair * 128, 128)]
            for n, half in enumerate(halves):
                scores[page, pair * 2 + n] = mt(k * half, q)
                dprobs[page, pair * 2 + n] = mt(v * half, do)
    for page in range(PAGES):
        allowed = mask_ref[page] > 0.5
        for head in range(6):
            masked = jnp.where(allowed, scores[page, head] * SCALE, -1e30)
            expo = jnp.exp(masked - jnp.max(masked, axis=0, keepdims=True))
            share = expo * (1.0 / jnp.sum(expo, axis=0, keepdims=True))
            slope = dprobs[page, head]
            inner = jnp.sum(share * slope, axis=0, keepdims=True)
            probs[page, head] = share.astype(BF)
            dscores[page, head] = (share * (slope - inner)).astype(BF)
    for page in range(PAGES):
        rows = pl.ds(page * BLOCKS, BLOCKS)
        for pair in range(3):
            q = p_ref[rows, pl.ds(pair * 128, 128)]
            k = p_ref[rows, pl.ds(384 + pair * 128, 128)]
            v = p_ref[rows, pl.ds(768 + pair * 128, 128)]
            do = do_ref[rows, pl.ds(pair * 128, 128)]

            def both(product, left, right):
                one = product(left[page, pair * 2], right * halves[0])
                return one + product(left[page, pair * 2 + 1], right * halves[1])

            dp_ref[rows, pl.ds(pair * 128, 128)] = (both(tm, dscores, k) * SCALE).astype(BF)
            dp_ref[rows, pl.ds(384 + pair * 128, 128)] = (both(mm, dscores, q) * SCALE).astype(BF)
            dp_ref[rows, pl.ds(768 + pair * 128, 128)] = both(mm, probs, do).astype(BF)
            o_ref[rows, pl.ds(pair * 128, 128)] = both(tm, probs, v).astype(BF)
    part_ref[...] = mm(dp_ref[...], held[pl.ds(0, 1152), :]).astype(BF)


def attn_grads_kernel(place, a_ref, dp_ref, dr_ref, o_ref, near, far, later, home, total):
    turned = a_ref[...].T
    for n in range(3):
        cols = pl.ds(n * 384, 384)
        total[:, cols] = mm(turned, dp_ref[:, cols]).astype(BF)
    total[:, pl.ds(1152, 384)] = mm(dr_ref[...].T, o_ref[...]).astype(BF)
    send_z(place, total, near, far, later, home)


def added(left, right):
    return (left.astype(F32) + right.astype(F32)).astype(BF)


def added(left, right):
    return (left.astype(F32) + right.astype(F32)).astype(BF)


def arrived(home, plus, minus, total):
    half = home.shape[0] // 2
    total[0:half] = added(home[0:half], minus[0:half])
    total[half : 2 * half] = added(home[half : 2 * half], plus[half : 2 * half])


def pass_on_kernel(later, home, plus, minus, on_plus, on_minus, total):
    half = later.shape[0] // 2
    on_plus[...] = added(later[0:half], plus[0:half])
    on_minus[...] = added(later[half:], minus[half : 2 * half])
    arrived(home, plus, minus, total)


def join_kernel(plus, minus, later, home, got_plus, got_minus, out_plus, out_minus, total):
    size, half = plus.shape[0], plus.shape[0] // 2
    out_plus[0:size] = plus[...]
    out_minus[0:size] = minus[...]
    out_plus[size : size + half] = added(later[0:half], got_plus[0:half])
    out_minus[size : size + half] = added(later[half:], got_minus[half:size])
    arrived(home, got_plus, got_minus, total)


def join_z_kernel(near, far, later, home, got_near, got_far, out_near, out_far, total):
    out_near[0:768] = near[...]
    out_far[0:768] = far[...]
    out_far[768:1152] = added(later[0:384], got_near[0:384])
    out_near[768:1152] = added(later[384:768], got_far[384:768])
    total[0:384] = added(home[0:384], got_near[384:768])
    total[384:768] = added(home[384:768], got_far[0:384])


def pass_on_z_kernel(later, home, near, far, on_far, on_near, total):
    on_far[...] = added(later[0:384], near[0:384])
    on_near[...] = added(later[384:768], far[384:768])
    total[0:384] = added(home[0:384], near[384:768])
    total[384:768] = added(home[384:768], far[0:384])


def fold_kernel(place, some1, some0, plus0, minus0, last_plus, last_minus, plus, minus, later, home, total):
    total[1, 0:2] = added(some1[0:2], plus0[4:6])
    total[1, 2:4] = added(some1[2:4], minus0[4:6])
    total[0, 0:2] = added(some0[0:2], last_plus[...])
    total[0, 2:4] = added(some0[2:4], last_minus[...])

    def block(layer, d):
        return total[layer, (place[2] + d) & 3]

    plus[0], plus[1] = block(0, 2), block(1, 1)
    minus[0], minus[1] = block(0, 3), block(1, 2)
    later[0], later[1] = block(0, 1), block(1, 3)
    home[0], home[1] = block(0, 0), block(1, 0)


def put_split(out, first, value):
    count = value.shape[0]
    high = value.astype(BF)
    out[first : first + count] = high
    out[first + count : first + 2 * count] = (value - high.astype(F32)).astype(BF)


def get_split(ref, first, count):
    return ref[first : first + count].astype(F32) + ref[first + count : first + 2 * count].astype(F32)


def fold_z_kernel(place, *refs):
    some1, some0, near0, far0, last_far, last_near = refs[0:6]
    vec, outs, total = refs[6], refs[7:11], refs[11]
    total[0:384, 384:768] = added(some1[0:384], far0[768:1152])
    total[384:768, 384:768] = added(some1[384:768], near0[768:1152])
    total[0:384, 0:384] = added(some0[0:384], last_far[...])
    total[384:768, 0:384] = added(some0[384:768], last_near[...])
    for d1 in range(4):
        for j2 in range(4):
            outs[d1][j2 * 48 : j2 * 48 + 48] = total[pl.ds(row_of(place, d1, j2), 48)]
        put_split(outs[d1], 192, vec[...])


def turn_kernel(place, own, one, two, three, m0, m1, m2, m3, total, vecs):
    got = (own, one, two, three)
    total[...] = sum(r[0:192].astype(F32) for r in got).astype(BF)
    for s, r in enumerate(got):
        vecs[(place[1] - s) & 3] = get_split(r, 192, 16)
    vec = (vecs[0] + vecs[1]) + (vecs[2] + vecs[3])
    for s, out in enumerate((m0, m1, m2, m3)):
        row = pl.multiple_of(((place[2] + s) & 3) * 48, 16)
        out[0:48] = total[pl.ds(row, 48)]
        put_split(out, 48, vec)


def pack_kernel(place, *refs):
    some, last_plus, last_minus = refs[0:3]
    got, outs, staged, vecs = refs[3:7], refs[7:11], refs[11], refs[12]
    ffn0 = some[0].astype(F32) + last_plus[0].astype(F32)
    ffn1 = some[1].astype(F32) + last_minus[0].astype(F32)
    attn = sum(r[0:48].astype(F32) for r in got)
    for s, r in enumerate(got):
        vecs[(place[2] - s) & 3] = get_split(r, 48, 16)
    vec = (vecs[0] + vecs[1]) + (vecs[2] + vecs[3])
    zz = place[5]
    for half in range(2):
        for layer, ffn in ((0, ffn0), (1, ffn1)):
            to = staged.at[2 * half + layer]
            at = layer * 384 + half * 192
            for group in range(4):
                to[0:48, pl.ds(group * 192, 192)] = jnp.where(zz == group, attn[:, at : at + 192], 0.0).astype(BF)
            to[48:96] = ffn[:, half * 768 : half * 768 + 768].astype(BF)
            to[96:144] = ffn[:, 1536 + half * 768 : 1536 + half * 768 + 768].astype(BF)
            put_split(to, 144, vec[8 * layer : 8 * layer + 8])
    for k in range(4):
        outs[k][...] = staged[zz ^ k]


def finish_kernel(place, a, b, c, d, qkv_ref, out_ref, up_ref, down_ref, vec_ref, vecs):
    got = (a, b, c, d)
    total = sum(r[0:144].astype(F32) for r in got)
    for group in range(3):
        qkv_ref[group] = total[0:48, group * 192 : group * 192 + 192]
    out_ref[...] = total[0:48, 576:768]
    up_ref[...] = total[48:96]
    down_ref[...] = total[96:144]
    for k, r in enumerate(got):
        vecs[place[5] ^ k] = get_split(r, 144, 8)
    vec_ref[...] = (vecs[0] + vecs[1]) + (vecs[2] + vecs[3])


def rows_kernel(place, y0, dx0, y1, dx1, out):
    for layer, pair in enumerate(((y0, dx0), (y1, dx1))):
        for half in range(2):
            for n in range(2):
                out[2 * layer + half, n] = pair[n][2 * half + place[3]]


def by_batch_kernel(got, first, second):
    for batch, q in enumerate((0, 2, 1, 3)):
        first[batch] = got[q, 0]
        second[batch] = got[q, 1]


def small_kernel(place, mine, other, hidden_ref, gains_ref, shifts_ref, biases_ref):
    first = place[3] == 0
    low = jnp.where(first, mine[...], other[...])
    high = jnp.where(first, other[...], mine[...])
    for n, row in enumerate((low[6:7], high[6:7], low[7:8], high[7:8])):
        hidden_ref[:, n * 768 : n * 768 + 768] = row
    for n in range(2):
        gains_ref[0, n : n + 1] = low[2 * n : 2 * n + 1]
        shifts_ref[0, n : n + 1] = low[2 * n + 1 : 2 * n + 2]
    biases_ref[0] = low[4:6]


VM = pl.BlockSpec(memory_space=pltpu.VMEM)
SM = pl.BlockSpec(memory_space=pltpu.SMEM)
ANY = pl.BlockSpec(memory_space=pl.ANY)


def shape(dims, dtype):
    return jax.ShapeDtypeStruct(dims, dtype)


def call(body, ins, outs, scratch, args, limit=16, after=()):
    count, extra = len(args), len(after)
    name = getattr(body, 'func', body).__name__
    if extra:
        inner = body

        def body(*refs):
            return inner(*refs[:count], *refs[count + extra :])

        ins, args = ins + [ANY] * extra, [*args, *after]
    return pl.pallas_call(
        body,
        in_specs=ins,
        out_specs=tuple(spec for spec, _ in outs),
        out_shape=tuple(form for _, form in outs),
        scratch_shapes=scratch,
        compiler_params=pltpu.CompilerParams(vmem_limit_bytes=limit * 1024 * 1024),
        cost_estimate=pl.CostEstimate(flops=int(COSTS.get(name, 0.0) * FACTOR * 1e9) + 1024, bytes_accessed=1024, transcendentals=0),
    )(*args)


ROW_BF = (VM, shape((ROWS, D), BF))
ROW_F32 = (VM, shape((ROWS, D), F32))


def pairs_allowed(flags, valid):
    place = lax.broadcasted_iota(jnp.int32, (BLOCKS,), 0)
    visual = place >= TEXT
    dropped = (flags[:, None] == 1) & visual[None] | (flags[:, None] == 2) & ~visual[None]
    key_ok = (valid == 1) & ~dropped
    same = place[:, None] == place[None, :]
    other = visual[:, None] != visual[None, :]
    cross = same[None] | other[None] & key_ok[:, None, :]
    plain = same[None] | key_ok[:, None, :]
    masks = []
    for allowed in (cross, plain):
        allowed = allowed.astype(F32)
        masks.append((allowed, jnp.swapaxes(allowed, 1, 2)))
    return masks


def on_device(
    block_input, out_cotangent, drop_flags, key_valid, qkv_weight, out_weight, up_weight, down_weight,
    hidden_bias, norm_gains, norm_shifts, out_biases,
):
    y, x = lax.axis_index("y"), lax.axis_index("x")
    pipe, zhi, core = lax.axis_index("pipe"), lax.axis_index("zhi"), lax.axis_index("core")
    zz = 2 * zhi + pipe
    i1 = jnp.where(core == 0, x, y)
    i2 = jnp.where(core == 0, y, x)
    place = jnp.stack([pipe, i1, i2, core, zhi, zz]).astype(jnp.int32)

    packed = jnp.concatenate([
        norm_gains[0, 0:1], norm_shifts[0, 0:1], norm_gains[0, 1:2], norm_shifts[0, 1:2], out_biases[0],
        hidden_bias, jnp.zeros((1, D), F32),
    ])
    terms, rest = [], packed
    for _ in range(3):
        term = lax.reduce_precision(rest, 8, 7)
        terms.append(term.astype(BF))
        rest = rest - term
    packed_low = jnp.concatenate(terms)

    own_up, own_down = up_weight[0], down_weight[0]
    number = i2 * 4 + i1
    ffn_slice = jnp.where(
        number < 8,
        lax.dynamic_slice_in_dim(own_up, (number & 7) * 96, 96),
        lax.dynamic_slice_in_dim(own_down, (number & 7) * 96, 96),
    )
    piece = jnp.concatenate([ffn_slice, packed_low])
    from_z = [piece] + [swap_z(piece, k) for k in (1, 2, 3)]
    order = jnp.where(
        pipe == 0,
        jnp.stack([from_z[k][:96] for k in (2, 1, 3)]),
        jnp.stack([from_z[k][:96] for k in (1, 3, 2)]),
    )
    level = [order] + [ring_shift(order, FIRST, 4 - d) for d in (1, 2, 3)]
    first_level, last_level = call(
        level_kernel, [SM] + [VM] * 4, [(VM, shape((2, 384, D), BF)), (VM, shape((384, D), BF))], [],
        [place, *level],
    )
    after, before = ring_shift(first_level, SECOND, 3), ring_shift(first_level, SECOND, 1)
    parts = [first_level, after, before, ring_shift(before[0], SECOND, 1), ring_shift(after[1], SECOND, 3)]
    last_level, *_ = lax.optimization_barrier((last_level, after, before))
    after, before = ring_shift(last_level, SECOND, 3), ring_shift(last_level, SECOND, 1)
    more_parts = parts + [
        last_level, after, before, ring_shift(before[:192], SECOND, 1), ring_shift(after[192:], SECOND, 3)
    ]

    given = lax.dynamic_index_in_dim(block_input, zz ^ 3, 0, keepdims=False)
    qkv_weight, out_weight, _ = lax.optimization_barrier((qkv_weight, out_weight, piece))
    own_attn = jnp.concatenate([jnp.transpose(qkv_weight[0], (1, 2, 0)).reshape(576, D), out_weight[0]])
    near = swap_z(own_attn, 1)
    far = swap_z(jnp.concatenate([own_attn, given]), 3)
    (top,) = call(partial(half_kernel, 0), [VM], [(VM, shape((384, D), BF))], [], [near])
    (low,) = call(partial(half_kernel, 384), [VM], [(VM, shape((384, D), BF))], [], [far])
    diagonal = [swap_z(top, 3), swap_z(low, 1)]

    def whole(k):
        return sum(from_z[k][96 + 8 * n : 104 + 8 * n].astype(F32) for n in range(3))

    full = [whole(k) for k in range(4)]
    small, hidden = [], []
    for layer in range(2):
        same = jnp.where(pipe == layer, full[0], full[1])
        other = jnp.where(pipe == layer, full[2], full[3])
        small.append(same[:6])
        hidden.append(
            jnp.where(
                zhi == 0,
                jnp.concatenate([same[6:7], other[6:7]], axis=1),
                jnp.concatenate([other[6:7], same[6:7]], axis=1),
            )
        )

    drop_flags, key_valid, _ = lax.optimization_barrier((drop_flags, key_valid, level[1]))

    def all_rows(kept, came):
        halves = jnp.where(zhi == 0, jnp.stack([kept, came]), jnp.stack([came, kept]))
        across = swap_cores(halves)
        rows = jnp.where(core == 0, jnp.stack([halves, across], 1), jnp.stack([across, halves], 1))
        return rows.reshape(ROWS, D)

    x0 = all_rows(lax.dynamic_index_in_dim(block_input, zz, 0, keepdims=False), far[768:])
    out_cotangent, *_ = lax.optimization_barrier((out_cotangent, *parts[1:3]))
    cotangent = all_rows(
        lax.dynamic_index_in_dim(out_cotangent, zz, 0, keepdims=False),
        swap_z(lax.dynamic_index_in_dim(out_cotangent, zz ^ 3, 0, keepdims=False), 3),
    )
    flags = lax.dynamic_index_in_dim(drop_flags, zz, 0, keepdims=False)
    valid = lax.dynamic_index_in_dim(key_valid, zz, 0, keepdims=False)
    masks = pairs_allowed(flags, valid)

    attn_whole, ffn_whole = (VM, shape((1536, D), BF)), (VM, shape((2, 1536, D), BF))

    def join_attn(layer):
        (held,) = call(
            partial(join_attn_kernel, layer), [SM] + [VM] * 5, [attn_whole], [],
            [place, own_attn, near, *diagonal, far],
        )
        return held

    def join_ffn(layer, sources, after=()):
        (held,) = call(
            partial(join_ffn_kernel, layer), [SM] + [VM] * (2 + len(sources)), [ffn_whole], [],
            [place, own_up, own_down, *sources], after=after,
        )
        return held

    projected = (VM, shape((ROWS, 1152), BF))
    row_scratch = pltpu.VMEM((ROWS, D), BF)
    head_scratch = pltpu.VMEM((ROWS, 384), BF)
    wide_scratch = pltpu.VMEM((ROWS, 1536), BF)
    scores, probs = pltpu.VMEM((PAGES, 6, BLOCKS, BLOCKS), F32), pltpu.VMEM((PAGES, 6, BLOCKS, BLOCKS), BF)
    attn_scratch = [row_scratch, head_scratch, scores, probs]
    attn_held0, attn_held1 = join_attn(0), join_attn(1)
    p0, part = call(
        attn_first_kernel, [VM] * 4, [projected, ROW_BF], attn_scratch, [x0, small[0], masks[0][0], attn_held0]
    )
    ffn_held0 = join_ffn(0, parts)
    mid0, pre0, part = call(
        ffn_first_kernel, [VM] * 6, [ROW_F32, (VM, shape((ROWS, 1536), F32)), ROW_BF], [row_scratch, wide_scratch],
        [x0, part, swap_cores(part), small[0], hidden[0], ffn_held0],
    )
    y0, p1, part = call(
        attn_second_kernel, [VM] * 7, [ROW_BF, projected, ROW_BF], attn_scratch,
        [mid0, part, swap_cores(part), small[0], small[1], masks[1][0], attn_held1],
    )
    ffn_held1 = join_ffn(1, more_parts, [part])

    hidden_sum = (VM, shape((1, 1536), F32))
    two_sums = (VM, shape((2, D), F32))
    ring_blocks = [(VM, shape((4, 48, 3072), BF))] * 4
    z_blocks = [(VM, shape((D, 384), BF))] * 4
    ffn_total = pltpu.VMEM((D, 3072), BF)
    wide = (VM, shape((ROWS, 1536), BF))
    mid1, part, back, dhidden1, c1, e1, du1 = call(
        ffn_second_kernel, [VM] * 7, [ROW_F32, ROW_BF, ROW_BF, hidden_sum, ROW_BF, wide, wide],
        [pltpu.VMEM((ROWS, 1536), F32)],
        [y0, part, swap_cores(part), small[1], hidden[1], cotangent, ffn_held1],
    )
    plus1, minus1, later1, home1 = call(
        ffn_grads_kernel, [SM] + [VM] * 4, ring_blocks, [ffn_total], [place, c1, du1, cotangent, e1]
    )
    token = later1
    plus1, minus1 = ring_shift(plus1, FIRST, 1), ring_shift(minus1, FIRST, 3)

    back_scratch = [head_scratch, scores, scores, probs, probs]
    back_outs = [ROW_F32, ROW_BF, (VM, shape((4, D), F32)), ROW_BF, ROW_BF, projected, (VM, shape((ROWS, 384), BF))]
    y1, dmid1, back, sums1, a1, dr1, dp1, o1 = call(
        partial(attn_back_kernel, 1), [VM] * 11, [ROW_BF] + back_outs, back_scratch,
        [part, swap_cores(part), back, swap_cores(back), cotangent, mid1, small[1], masks[1][1], p1, y0,
         attn_held1], after=[token],
    )
    attn_total = [pltpu.VMEM((D, 1536), BF)]
    near1, far1, later_z1, home_z1 = call(
        attn_grads_kernel, [SM] + [VM] * 4, z_blocks, attn_total, [place, a1, dp1, dr1, o1]
    )
    token = later_z1
    near1, far1 = swap_z(near1, 1), swap_z(far1, 3)
    dx1, back, dhidden0, first1, c0, e0, du0 = call(
        ffn_back_kernel, [VM] * 9, [ROW_BF, ROW_BF, hidden_sum, two_sums, ROW_BF, wide, wide], [],
        [back, swap_cores(back), dmid1, y0, small[1], small[0], mid0, pre0, ffn_held0], after=[token],
    )
    plus0, minus0, later0, home0 = call(
        ffn_grads_kernel, [SM] + [VM] * 4, ring_blocks, [ffn_total], [place, c0, du0, dx1, e0]
    )
    six, four = [(VM, shape((6, 48, 3072), BF))] * 2, [(VM, shape((4, 48, 3072), BF))]
    plus0, minus0, some1 = call(
        join_kernel, [VM] * 6, six + four, [], [plus0, minus0, later1, home1, plus1, minus1], 20
    )
    token = some1
    plus0, minus0 = ring_shift(plus0, FIRST, 1), ring_shift(minus0, FIRST, 3)
    dmid0, back, sums0, a0, dr0, dp0, o0 = call(
        partial(attn_back_kernel, 0), [VM] * 9, back_outs, back_scratch,
        [back, swap_cores(back), dx1, mid0, small[0], masks[0][1], p0, x0, attn_held0],
        after=[token],
    )
    near0, far0, later_z0, home_z0 = call(
        attn_grads_kernel, [SM] + [VM] * 4, z_blocks, attn_total, [place, a0, dp0, dr0, o0]
    )
    tall = [(VM, shape((1152, 384), BF))] * 2
    near0, far0, some_z1 = call(
        join_z_kernel, [VM] * 6, tall + z_blocks[:1], [], [near0, far0, later_z1, home_z1, near1, far1]
    )
    token = some_z1
    near0, far0 = swap_z(near0, 1), swap_z(far0, 3)
    dx0, vec = call(
        last_kernel, [VM] * 10, [ROW_BF, (VM, shape((16, D), F32))], [],
        [back, swap_cores(back), dmid0, x0, small[0], sums0, dhidden0, first1, sums1, dhidden1], after=[token],
    )

    pair, one = [(VM, shape((2, 48, 3072), BF))], [(VM, shape((1, 48, 3072), BF))]
    on_plus, on_minus, some0 = call(
        pass_on_kernel, [VM] * 4, pair * 2 + four, [], [later0, home0, plus0, minus0], after=[vec]
    )
    last_plus, last_minus = ring_shift(on_plus, FIRST, 1), ring_shift(on_minus, FIRST, 3)
    half = [(VM, shape((384, 384), BF))]
    on_far, on_near, some_z0 = call(
        pass_on_z_kernel, [VM] * 4, half * 2 + z_blocks[:1], [], [later_z0, home_z0, near0, far0], after=[some0]
    )
    last_far, last_near = swap_z(on_far, 3), swap_z(on_near, 1)
    plus, minus, later, home = call(
        fold_kernel, [SM] + [VM] * 6, pair * 4, [pltpu.VMEM((2, 4, 48, 3072), BF)],
        [place, some1, some0, plus0, minus0, last_plus, last_minus], after=[some_z0],
    )
    plus, minus = ring_shift(plus, SECOND, 1), ring_shift(minus, SECOND, 3)
    turned = call(
        fold_z_kernel, [SM] + [VM] * 7, [(VM, shape((224, D), BF))] * 4, [pltpu.VMEM((D, D), BF)],
        [place, some_z1, some_z0, near0, far0, last_far, last_near, vec], after=[home],
    )
    token = turned[0]
    on_plus, on_minus, some = call(
        pass_on_kernel, [VM] * 4, one * 2 + pair, [], [later, home, plus, minus], after=[turned[0]]
    )
    last_plus, last_minus = ring_shift(on_plus, SECOND, 1), ring_shift(on_minus, SECOND, 3)
    turned = call(
        turn_kernel, [SM] + [VM] * 4, [(VM, shape((80, D), BF))] * 4,
        [pltpu.VMEM((192, D), BF), pltpu.VMEM((4, 16, D), F32)],
        [place, turned[0]] + [ring_shift(turned[s], FIRST, s) for s in (1, 2, 3)],
        after=[some],
    )
    turned = [turned[0]] + [ring_shift(turned[s], SECOND, s) for s in (1, 2, 3)]
    packs = call(
        pack_kernel, [SM] + [VM] * 7, [(VM, shape((160, D), BF))] * 4,
        [pltpu.VMEM((4, 160, D), BF), pltpu.VMEM((4, 16, D), F32)], [place, some, last_plus, last_minus, *turned],
    )
    grad_qkv, grad_out, grad_up, grad_down, vec = call(
        finish_kernel, [SM] + [VM] * 4,
        [(VM, shape((3, 48, 192), F32)), (VM, shape((48, 192), F32))] + [(VM, shape((48, D), F32))] * 2
        + [(VM, shape((8, D), F32))], [pltpu.VMEM((4, 8, D), F32)],
        [place, packs[0]] + [swap_z(packs[k], k) for k in (1, 2, 3)],
    )
    grad_qkv = jnp.transpose(grad_qkv, (1, 0, 2))
    grad_out, grad_down = grad_out.T, grad_down.T
    grad_hidden, grad_gains, grad_shifts, grad_biases = call(
        small_kernel, [SM] + [VM] * 2, [(VM, shape((1, 4 * D), F32))] + [(VM, shape((1, 2, D), F32))] * 3, [],
        [place, vec, swap_cores(vec)],
    )

    quarters = [value.reshape(4, 72, D) for value in (y0, dx0, y1, dx1)]
    (rows,) = call(
        rows_kernel, [SM] + [VM] * 4, [(VM, shape((4, 2, 72, D), BF))], [], [place, *quarters], after=[token]
    )
    activations, input_grads = call(
        by_batch_kernel, [VM], [(VM, shape((4, 72, D), BF))] * 2, [], [exchange_z(rows)]
    )
    return (
        activations[None],
        input_grads[None],
        grad_qkv[None],
        grad_out[None],
        grad_up[None],
        grad_down[None],
        grad_hidden,
        grad_gains,
        grad_shifts,
        grad_biases,
    )


def solution(mesh):
    fine = Mesh(mesh.devices.reshape(4, 4, 2, 2, 2), MESH_AXES)
    rows = DP + TENSOR
    in_specs = (
        P(None, rows, None),
        P(None, rows, None),
        P(None, DP),
        P(None, DP, None),
        P("pipe", None, None, TENSOR),
        P("pipe", TENSOR, None),
        P("pipe", None, TENSOR),
        P("pipe", TENSOR, None),
        P("pipe", TENSOR),
        P("pipe", None, None),
        P("pipe", None, None),
        P("pipe", None, None),
    )
    out_specs = (
        P("pipe", None, rows, None),
        P("pipe", None, rows, None),
        P("pipe", DP, None, TENSOR),
        P("pipe", TENSOR, DP),
        P("pipe", DP, TENSOR),
        P("pipe", TENSOR, DP),
        P("pipe", None),
        P("pipe", None, None),
        P("pipe", None, None),
        P("pipe", None, None),
    )
    return jax.shard_map(on_device, mesh=fine, in_specs=in_specs, out_specs=out_specs, check_vma=False)
```
